32 devices in a mesh: row: 8 (over z, y), col: 4 (over x, core).
Axes of the slice: x: 2, y: 2, z: 4, core: 2. Of those that a mesh axis runs over, the one named last changes fastest.
Arguments:
- factor: bfloat16 [8192, 8192], P('row', 'col')
- panels: float32 [8192, 1024], P(('row', 'col')), may hold values from -100 to 100, as said below
Outputs:
- new_columns: float32 [8192, 1024], P(('row', 'col'))
The draws below stay inside these ranges and needn't reach their ends.
Inputs may be any that keep to these rules, and one draw needn't show every extreme that they name: The block of rows and columns 0 to 1023 of panels minus factor's first 1024 rows times their transpose is symmetric positive definite.
All inputs are finite; a program needn't handle non-finite values.
Results may differ from the reference program's by a relative error of at most 0.0003.
Values may be sent and summed in bfloat16 or wider, within the bound.
No kernel may reach another device: no remote copies, remote signals or barrier semaphores. Data moves between devices by JAX's collectives and lax.ppermute only.
A program may use at most 64 MiB of HBM per device.

```python
import jax
import jax.numpy as jnp
from jax import lax

PANEL = 512
FACTOR_COLS = 8192
SLAB_ROWS = 8192


def shared_draw(key):
    folded = jax.random.fold_in(key, 7)
    key_factor, key_base, key_rest = jax.random.split(folded, 3)
    width = 2 * PANEL
    values = jax.random.normal(key_factor, (SLAB_ROWS, FACTOR_COLS), jnp.float32)
    row_ids = jnp.arange(SLAB_ROWS)[:, None]
    pivot_scale = 1.0 / jnp.sqrt(jnp.float32(FACTOR_COLS))
    row_scale = jnp.where(row_ids < width, pivot_scale, jnp.float32(1.0))
    factor = (values * row_scale).astype(jnp.bfloat16)
    base = jax.random.normal(key_base, (width, width), jnp.float32)
    top_block = jnp.dot(base, base.T, precision=lax.Precision.HIGHEST) / width + 0.5 * jnp.eye(width, dtype=jnp.float32)
    rest = jax.random.normal(key_rest, (SLAB_ROWS - width, width), jnp.float32)
    extra = jnp.concatenate([top_block, rest], 0)
    wide = factor.astype(jnp.float32)
    panels = extra + jnp.dot(wide, wide[:width].T, precision=lax.Precision.HIGHEST)
    return (factor, panels)


def draw_factor(key, part):
    return shared_draw(key)[0]


def draw_panels(key, part):
    return shared_draw(key)[1]


def setup_inputs(seed: int = 0) -> dict:
    key_of = jax.random.split(jax.random.key(seed), 3)
    factor = draw_factor(jax.random.fold_in(key_of[2], 71), 0)
    panels = draw_panels(jax.random.fold_in(key_of[2], 71), 0)
    return {"factor": factor, "panels": panels}


def solve_right(lower_factor, values):
    return jax.scipy.linalg.solve_triangular(lower_factor, values.T, lower=True).T

def reference(factor, panels):
    width = 2 * PANEL
    pivots = factor[:width]
    update = lax.dot_general(factor.astype(jnp.float32), pivots.astype(jnp.float32), (((1,), (1,)), ((), ())), preferred_element_type=jnp.float32)
    schur = panels - update
    first_diag = jnp.linalg.cholesky(schur[:PANEL, :PANEL])
    middle = solve_right(first_diag, schur[PANEL:width, :PANEL])
    second_in = schur[PANEL:width, PANEL:width] - jnp.dot(middle, middle.T, precision=lax.Precision.HIGHEST)
    second_diag = jnp.linalg.cholesky(second_in)
    lower_one = solve_right(first_diag, schur[width:, :PANEL])
    rest_two = schur[width:, PANEL:] - jnp.dot(lower_one, middle.T, precision=lax.Precision.HIGHEST)
    lower_two = solve_right(second_diag, rest_two)
    zero_block = jnp.zeros((PANEL, PANEL), jnp.float32)
    top_out = jnp.concatenate([jnp.concatenate([first_diag, zero_block], 1), jnp.concatenate([middle, second_diag], 1)], 0)
    return jnp.concatenate([top_out, jnp.concatenate([lower_one, lower_two], 1)], 0)
```

```python
import functools
import jax
import jax.numpy as jnp
from jax import lax
from jax.experimental import pallas as pl
from jax.experimental.pallas import tpu as pltpu
from jax.sharding import PartitionSpec as P

SUB = 8
BLOCK = 128
STEP = 32
HEIGHT = 256
PARTS = 2
BOTH = ("row", "col")
HIGH = lax.Precision.HIGHEST


def tn_dot(a, b):
    return lax.dot_general(a, b, (((0,), (0,)), ((), ())), precision=HIGH, preferred_element_type=jnp.float32)


def nn_dot(a, b):
    return lax.dot_general(a, b, (((1,), (0,)), ((), ())), precision=HIGH, preferred_element_type=jnp.float32)


def row_of(x, k):
    return jnp.broadcast_to(x[k : k + 1, :], x.shape)


def lane_of(x, k):
    return jnp.broadcast_to(x[:, k : k + 1], x.shape)


def inverse_factor(block):
    lane = lax.broadcasted_iota(jnp.int32, (SUB, BLOCK), 1)
    sub = lax.broadcasted_iota(jnp.int32, (SUB, BLOCK), 0)
    groups = [block[SUB * q : SUB * (q + 1), :] for q in range(BLOCK // SUB)]
    per_step = STEP // SUB
    done = []
    for step in range(BLOCK // STEP):
        end = (step + 1) * per_step
        here = []
        for p in range(step * per_step, end):
            first = SUB * p
            inside = (lane >= first) & (lane < first + SUB)
            cols = [lane_of(groups[p], first + k) for k in range(SUB)]
            rows = jnp.where(inside, jnp.where(lane - first == sub, 1.0, 0.0), groups[p])
            scale = jnp.zeros((SUB, BLOCK), jnp.float32)
            col_rows, own_rows = [], []
            for k in range(SUB):
                pivot = row_of(cols[k], k)
                inv = pl.reciprocal(pivot, approx=True)
                scale = jnp.where(sub == k, lax.rsqrt(pivot), scale)
                below = jnp.where(sub > k, cols[k], 0.0)
                raw = [row_of(cols[m], k) for m in range(k + 1, SUB)]
                own = row_of(rows, k) * inv
                for i, m in enumerate(range(k + 1, SUB)):
                    cols[m] = cols[m] - (below * raw[i]) * inv
                rows = rows - below * own
                col_rows.append([r * inv for r in raw])
                own_rows.append(own)
            here.append(rows * scale)
            for q in range(p + 1, end):
                mult = [lane_of(groups[q], first + k) for k in range(SUB)]
                acc = jnp.where(inside, 0.0, groups[q])
                for k in range(SUB):
                    for i, m in enumerate(range(k + 1, SUB)):
                        mult[m] = mult[m] - mult[k] * col_rows[k][i]
                    acc = acc - mult[k] * own_rows[k]
                groups[q] = acc
        span = jnp.concatenate(here, 0)
        base = step * STEP
        span_lane = lax.broadcasted_iota(jnp.int32, (STEP, BLOCK), 1)
        span_row = lax.broadcasted_iota(jnp.int32, (STEP, BLOCK), 0) + base
        span = jnp.where((span_lane <= span_row) | (span_lane >= base + STEP), span, 0.0)
        done.append(jnp.where(span_lane <= span_row, span, 0.0))
        if base + STEP < BLOCK:
            delta = tn_dot(span, span)
            in_step = (lane >= base) & (lane < base + STEP)
            for q in range(end, BLOCK // SUB):
                groups[q] = jnp.where(in_step, 0.0, groups[q]) - delta[SUB * q : SUB * (q + 1), :]
    return jnp.concatenate(done, 0)


def panel_kernel(height, before, *refs):
    own_ref, earlier, out_ref = refs[0], refs[1:-1], refs[-1]
    acc = own_ref[...]
    for ref, skip in zip(earlier, before):
        span = ref[:, skip:]
        acc = acc - tn_dot(span[:, :height], span)
    out_ref[...] = jnp.zeros_like(out_ref)
    rest = acc
    uppers, inverses = [], []
    nblk = height // BLOCK
    for i in range(nblk):
        at = i * BLOCK
        inverse = inverse_factor(rest[:, :BLOCK][:BLOCK])
        out_ref[at : at + BLOCK, at : at + BLOCK] = inverse
        if rest.shape[1] > BLOCK:
            upper = nn_dot(inverse, rest[:BLOCK, BLOCK:])
        for j in range(i):
            tot = 0.0
            for k in range(j, i):
                blk = uppers[k][:, (i - k - 1) * BLOCK : (i - k) * BLOCK]
                tot = tot + tn_dot(blk, inverses[k][j])
            inverses.append([]) if len(inverses) == i else None
            inverses[i].append(-nn_dot(inverse, tot))
        if len(inverses) == i:
            inverses.append([])
        inverses[i].append(inverse)
        for j in range(i):
            out_ref[at : at + BLOCK, j * BLOCK : (j + 1) * BLOCK] = inverses[i][j]
        if rest.shape[1] > BLOCK:
            uppers.append(upper)
            left = height - at - BLOCK
            if upper.shape[1] > left:
                out_ref[at : at + BLOCK, height:] = upper[:, left:]
            if left:
                rest = rest[BLOCK:, BLOCK:] - tn_dot(upper[:, :left], upper)


def panel_factor(own, earlier, skips):
    height, wide = own.shape
    return pl.pallas_call(
        functools.partial(panel_kernel, height, skips),
        out_shape=jax.ShapeDtypeStruct((height, wide), jnp.float32),
        in_specs=[pl.BlockSpec(memory_space=pltpu.VMEM)] * (1 + len(earlier)),
        out_specs=pl.BlockSpec(memory_space=pltpu.VMEM),
        compiler_params=pltpu.CompilerParams(vmem_limit_bytes=40 << 20),
        cost_estimate=pl.CostEstimate(flops=12 * height * height * wide, bytes_accessed=8 * height * wide, transcendentals=0),
    )(own, *earlier)


def nt_dot(a, b, precision=None):
    return lax.dot_general(
        a, b, (((1,), (1,)), ((), ())), precision=precision, preferred_element_type=jnp.float32
    )


def core_halves(block):
    half = block.shape[0] // 2
    low = lax.axis_index("col") % 2
    mine = lax.dynamic_slice_in_dim(block, low * half, half, 0)
    other = lax.dynamic_slice_in_dim(block, (1 - low) * half, half, 0)
    return mine, other


def join_halves(mine, pairs):
    other = lax.ppermute(mine, BOTH, pairs)
    low = lax.axis_index("col") % 2
    return jnp.where(low == 0, jnp.concatenate([mine, other], 0), jnp.concatenate([other, mine], 0))


def sum_in_first_row(block, ncol):
    swap = [(c, c ^ 1) for c in range(ncol)]
    mine, other = core_halves(block)
    mine = mine + lax.ppermute(other, BOTH, swap)
    bit = 2
    while bit < ncol:
        mine = mine + lax.ppermute(mine, BOTH, [(c, c ^ bit) for c in range(ncol)])
        bit *= 2
    return join_halves(mine, swap)


def to_every_row(block, nrow, ncol):
    row = lax.axis_index("row")
    mine, _ = core_halves(block)
    step = nrow // 2
    while step:
        pairs = [
            (r * ncol + c, (r + step) * ncol + c) for r in range(0, nrow, 2 * step) for c in range(ncol)
        ]
        got = lax.ppermute(mine, BOTH, pairs)
        mine = jnp.where(row % (2 * step) == step, got, mine)
        step //= 2
    return join_halves(mine, [(r * ncol + c, r * ncol + (c ^ 1)) for r in range(nrow) for c in range(ncol)])


def spread_pivots(rows, nrow, ncol):
    row = lax.axis_index("row")
    piece = rows.shape[0] // nrow
    mine = rows[:piece]
    for r in range(1, nrow):
        got = lax.ppermute(
            rows[r * piece : (r + 1) * piece], BOTH, [(c, r * ncol + c) for c in range(ncol)]
        )
        mine = jnp.where(row == r, got, mine)
    return lax.all_gather(mine, "row", axis=0, tiled=True)


def own_part(panels, at, end):
    own = panels.shape[0]
    col = lax.axis_index("col")
    blocks = []
    for c in range(at // own, -(-end // own)):
        first, last = max(at, c * own), min(end, (c + 1) * own)
        blocks.append(jnp.where(col == c, panels[first - c * own : last - c * own, at:], 0.0))
    return jnp.concatenate(blocks, 0)


def on_device(nrow, ncol, factor, panels):
    own, width = panels.shape
    row, col = lax.axis_index("row"), lax.axis_index("col")

    pivots = []
    share = width // PARTS
    for part in range(PARTS):
        pivots.append(spread_pivots(factor[part * share : (part + 1) * share], nrow, ncol))

    tops, packs = [], []
    for at in range(0, width, HEIGHT):
        piece = own_part(panels, at, at + HEIGHT) - nt_dot(factor[at : at + HEIGHT], factor[at:width])
        tops.append(sum_in_first_row(piece, ncol))
    for j, top in enumerate(tops):
        packs.append(panel_factor(top, packs, [(j - p) * HEIGHT for p in range(j)]))
    packs = [to_every_row(pack, nrow, ncol) for pack in packs]

    rest = []
    for part in range(PARTS):
        update = lax.psum_scatter(nt_dot(factor, pivots[part]), "col", scatter_dimension=0, tiled=True)
        rest.append(panels[:, part * share : (part + 1) * share] - update)
    rest = jnp.concatenate(rest, 1)
    out = []
    for pack in packs:
        solved = nt_dot(rest[:, :HEIGHT], pack[:, :HEIGHT], HIGH)
        rest = rest[:, HEIGHT:] - jnp.dot(solved, pack[:, HEIGHT:], precision=HIGH)
        out.append(solved)
    out = jnp.concatenate(out, 1)
    at_row = lax.broadcasted_iota(jnp.int32, out.shape, 0) + (row * ncol + col) * own
    at_col = lax.broadcasted_iota(jnp.int32, out.shape, 1)
    return jnp.where(at_col <= at_row, out, 0.0)


def solution(mesh):
    return jax.shard_map(
        functools.partial(on_device, mesh.shape["row"], mesh.shape["col"]),
        mesh=mesh,
        in_specs=(P("row", "col"), P(BOTH, None)),
        out_specs=P(BOTH, None),
        check_vma=False,
    )
```

```python
import functools
import jax
import jax.numpy as jnp
from jax import lax
from jax.experimental import pallas as pl
from jax.experimental.pallas import tpu as pltpu
from jax.sharding import PartitionSpec as P

SUB = 8
BLOCK = 128
STEP = 32
HEIGHT = 256
BOTH = ("row", "col")
HIGH = lax.Precision.HIGHEST


def tn_dot(a, b):
    return lax.dot_general(a, b, (((0,), (0,)), ((), ())), precision=HIGH, preferred_element_type=jnp.float32)


def nn_dot(a, b):
    return lax.dot_general(a, b, (((1,), (0,)), ((), ())), precision=HIGH, preferred_element_type=jnp.float32)


def row_of(x, k):
    return jnp.broadcast_to(x[k : k + 1, :], x.shape)


def lane_of(x, k):
    return jnp.broadcast_to(x[:, k : k + 1], x.shape)


def inverse_factor(block):
    lane = lax.broadcasted_iota(jnp.int32, (SUB, BLOCK), 1)
    sub = lax.broadcasted_iota(jnp.int32, (SUB, BLOCK), 0)
    groups = [block[SUB * q : SUB * (q + 1), :] for q in range(BLOCK // SUB)]
    per_step = STEP // SUB
    done = []
    for step in range(BLOCK // STEP):
        end = (step + 1) * per_step
        here = []
        for p in range(step * per_step, end):
            first = SUB * p
            inside = (lane >= first) & (lane < first + SUB)
            cols = [lane_of(groups[p], first + k) for k in range(SUB)]
            rows = jnp.where(inside, jnp.where(lane - first == sub, 1.0, 0.0), groups[p])
            scale = jnp.zeros((SUB, BLOCK), jnp.float32)
            col_rows, own_rows = [], []
            for k in range(SUB):
                pivot = row_of(cols[k], k)
                inv = pl.reciprocal(pivot, approx=True)
                scale = jnp.where(sub == k, lax.rsqrt(pivot), scale)
                below = jnp.where(sub > k, cols[k], 0.0)
                raw = [row_of(cols[m], k) for m in range(k + 1, SUB)]
                own = row_of(rows, k) * inv
                for i, m in enumerate(range(k + 1, SUB)):
                    cols[m] = cols[m] - (below * raw[i]) * inv
                rows = rows - below * own
                col_rows.append([r * inv for r in raw])
                own_rows.append(own)
            here.append(rows * scale)
            for q in range(p + 1, end):
                mult = [lane_of(groups[q], first + k) for k in range(SUB)]
                acc = jnp.where(inside, 0.0, groups[q])
                for k in range(SUB):
                    for i, m in enumerate(range(k + 1, SUB)):
                        mult[m] = mult[m] - mult[k] * col_rows[k][i]
                    acc = acc - mult[k] * own_rows[k]
                groups[q] = acc
        span = jnp.concatenate(here, 0)
        base = step * STEP
        span_lane = lax.broadcasted_iota(jnp.int32, (STEP, BLOCK), 1)
        span_row = lax.broadcasted_iota(jnp.int32, (STEP, BLOCK), 0) + base
        span = jnp.where((span_lane <= span_row) | (span_lane >= base + STEP), span, 0.0)
        done.append(jnp.where(span_lane <= span_row, span, 0.0))
        if base + STEP < BLOCK:
            delta = tn_dot(span, span)
            in_step = (lane >= base) & (lane < base + STEP)
            for q in range(end, BLOCK // SUB):
                groups[q] = jnp.where(in_step, 0.0, groups[q]) - delta[SUB * q : SUB * (q + 1), :]
    return jnp.concatenate(done, 0)


def factor_panel(height, skips, own_ref, earlier, out_ref):
    rest = own_ref[...]
    for ref, skip in zip(earlier, skips):
        span = ref[:, skip:]
        rest = rest - tn_dot(span[:, :height], span)
    out_ref[...] = jnp.zeros_like(out_ref)
    uppers, inverses = [], []
    for i in range(height // BLOCK):
        at = i * BLOCK
        inverse = inverse_factor(rest[:BLOCK, :BLOCK])
        if rest.shape[1] > BLOCK:
            upper = nn_dot(inverse, rest[:BLOCK, BLOCK:])
        line = []
        for j in range(i):
            total = 0.0
            for k in range(j, i):
                block = uppers[k][:, (i - k - 1) * BLOCK : (i - k) * BLOCK]
                total = total + tn_dot(block, inverses[k][j])
            line.append(-nn_dot(inverse, total))
        line.append(inverse)
        inverses.append(line)
        for j, block in enumerate(line):
            out_ref[at : at + BLOCK, j * BLOCK : (j + 1) * BLOCK] = block
        if rest.shape[1] > BLOCK:
            uppers.append(upper)
            left = height - at - BLOCK
            if upper.shape[1] > left:
                out_ref[at : at + BLOCK, height:] = upper[:, left:]
            if left:
                rest = rest[BLOCK:, BLOCK:] - tn_dot(upper[:, :left], upper)


def panel_kernel(height, skips, row_ref, own_ref, *refs):
    earlier, out_ref = refs[: len(skips)], refs[-1]

    @pl.when(row_ref[0] == 0)
    def _():
        factor_panel(height, skips, own_ref, earlier, out_ref)


def panel_stage(row, own, earlier, passing):
    height, wide = own.shape
    skips = [(len(earlier) - p) * height for p in range(len(earlier))]
    vmem, hbm = pl.BlockSpec(memory_space=pltpu.VMEM), pl.BlockSpec(memory_space=pltpu.HBM)
    count = len(passing)

    def body(row_ref, *refs):
        panel_kernel(height, skips, row_ref, *refs[count : -count - 1], refs[-1])

    results = pl.pallas_call(
        body,
        out_shape=[jax.ShapeDtypeStruct(x.shape, x.dtype) for x in passing]
        + [jax.ShapeDtypeStruct((height, wide), jnp.float32)],
        in_specs=[pl.BlockSpec(memory_space=pltpu.SMEM)] + [hbm] * count + [vmem] * (1 + len(earlier)),
        out_specs=[hbm] * count + [vmem],
        input_output_aliases={i + 1: i for i in range(count)},
        compiler_params=pltpu.CompilerParams(vmem_limit_bytes=40 << 20),
        cost_estimate=pl.CostEstimate(flops=10**10, bytes_accessed=8 * height * wide, transcendentals=0),
    )(row[None], *passing, own, *earlier)
    return results[-1], results[:-1]


def pick_kernel(which_ref, *refs):
    choices, out_ref, sem = refs[:-2], refs[-2], refs[-1]
    for i, choice in enumerate(choices):

        @pl.when(which_ref[0] == i)
        def _():
            copy = pltpu.make_async_copy(choice, out_ref, sem)
            copy.start()
            copy.wait()


def pick(which, choices):
    hbm = pl.BlockSpec(memory_space=pltpu.HBM)
    return pl.pallas_call(
        pick_kernel,
        out_shape=jax.ShapeDtypeStruct(choices[0].shape, choices[0].dtype),
        in_specs=[pl.BlockSpec(memory_space=pltpu.SMEM)] + [hbm] * len(choices),
        out_specs=hbm,
        scratch_shapes=[pltpu.SemaphoreType.DMA],
    )(which[None], *choices)


def nt_dot(a, b, precision=None):
    return lax.dot_general(
        a, b, (((1,), (1,)), ((), ())), precision=precision, preferred_element_type=jnp.float32
    )


def update_kernel(slots, order_ref, factor_ref, *refs):
    choices, (keep_ref, send_ref, pivots, sem) = refs[:-4], refs[-4:]
    slot = pl.program_id(0)
    for i, choice in enumerate(choices):

        @pl.when((slot == 0) & (order_ref[slots] == i))
        def _():
            copy = pltpu.make_async_copy(choice, pivots, sem)
            copy.start()
            copy.wait()

    product = nt_dot(factor_ref[...], pivots[...])

    @pl.when(slot < slots // 2)
    def _():
        keep_ref[...] = product

    @pl.when(slot >= slots // 2)
    def _():
        send_ref[...] = product


def update_product(factor, choices, which, col, ncol):
    rows, depth = factor.shape
    own, count = rows // ncol, choices[0].shape[0]
    half = ncol // 2
    flips = list(range(0, ncol, 2)) + list(range(1, ncol, 2))
    order = jnp.concatenate([col ^ jnp.asarray(flips, jnp.int32), which[None]])
    out = jax.ShapeDtypeStruct((half * own, count), jnp.float32)
    return pl.pallas_call(
        functools.partial(update_kernel, ncol),
        out_shape=(out, out),
        grid_spec=pltpu.PrefetchScalarGridSpec(
            num_scalar_prefetch=1,
            grid=(ncol,),
            in_specs=[pl.BlockSpec((own, depth), lambda s, order: (order[s], 0))]
            + [pl.BlockSpec(memory_space=pltpu.HBM)] * len(choices),
            out_specs=(
                pl.BlockSpec((own, count), lambda s, order: (jnp.minimum(s, half - 1), 0)),
                pl.BlockSpec((own, count), lambda s, order: (jnp.maximum(s - half, 0), 0)),
            ),
            scratch_shapes=[pltpu.VMEM((count, depth), factor.dtype), pltpu.SemaphoreType.DMA],
        ),
        compiler_params=pltpu.CompilerParams(vmem_limit_bytes=40 << 20),
        cost_estimate=pl.CostEstimate(
            flops=2 * rows * depth * count, bytes_accessed=2 * rows * depth + 4 * rows * count, transcendentals=0
        ),
    )(order, factor, *choices)


def everywhere(pairs_of_col, nrow, ncol):
    pairs = []
    for c in range(ncol):
        moves = dict(pairs_of_col[c % 2])
        pairs += [(r * ncol + c, moves.get(r, r) * ncol + c) for r in range(nrow)]
    return pairs


def ring(rows):
    return {a: b for a, b in zip(rows, rows[1:] + rows[:1])}


def along_col(block, bit, nrow, ncol):
    return lax.ppermute(block, BOTH, [(r * ncol + c, r * ncol + (c ^ bit)) for r in range(nrow) for c in range(ncol)])


def core_halves(block):
    half = block.shape[0] // 2
    low = lax.axis_index("col") % 2
    mine = lax.dynamic_slice_in_dim(block, low * half, half, 0)
    other = lax.dynamic_slice_in_dim(block, (1 - low) * half, half, 0)
    return mine, other


def join_halves(mine, nrow, ncol):
    other = along_col(mine, 1, nrow, ncol)
    low = lax.axis_index("col") % 2
    return jnp.where(low == 0, jnp.concatenate([mine, other], 0), jnp.concatenate([other, mine], 0))


def sum_over_col(block, nrow, ncol):
    mine, other = core_halves(block)
    mine = mine + along_col(other, 1, nrow, ncol)
    bit = 2
    while bit < ncol:
        mine = mine + along_col(mine, bit, nrow, ncol)
        bit *= 2
    return join_halves(mine, nrow, ncol)


def scatter_sum(keep, send, nrow, ncol):
    keep = keep + along_col(send, 1, nrow, ncol)
    bit = ncol // 2
    while bit > 1:
        half = keep.shape[0] // 2
        keep = keep[:half] + along_col(keep[half:], bit, nrow, ncol)
        bit //= 2
    return keep


def to_rows(mine, step, row, nrow, ncol):
    moves = {}
    for r in range(0, nrow, 2 * step):
        moves[r], moves[r + step] = r + step, r
    got = lax.ppermute(mine, BOTH, everywhere((moves, moves), nrow, ncol))
    return jnp.where(row % (2 * step) == step, got, mine)


def own_part(panels, at, end):
    own = panels.shape[0]
    col = lax.axis_index("col")
    blocks = []
    for c in range(at // own, -(-end // own)):
        first, last = max(at, c * own), min(end, (c + 1) * own)
        blocks.append(jnp.where(col == c, panels[first - c * own : last - c * own, at:], 0.0))
    return jnp.concatenate(blocks, 0)


def on_device(nrow, ncol, factor, panels):
    own, width = panels.shape
    row, col = lax.axis_index("row"), lax.axis_index("col")
    odd = col % 2
    depth = nrow // 2
    count = width // HEIGHT
    even_line, odd_line = list(range(0, nrow, 2)), list(range(1, nrow, 2))
    first_hop = everywhere((ring(even_line), {0: 1, 1: 0}), nrow, ncol)
    next_hop = everywhere((ring(even_line), ring(odd_line)), nrow, ncol)
    last_hop = everywhere(({}, ring(odd_line)), nrow, ncol)
    across = [
        (r * ncol + c, (r ^ 1) * ncol + c) for r in range(nrow) for c in range(ncol) if r % 2 == c % 2
    ]
    arrives = jnp.where(odd == 0, row // 2, jnp.where(row == 0, 0, row // 2 + 1))
    on_line = row % 2 == odd
    steps = []
    while nrow >> (len(steps) + 1):
        steps.append(nrow >> (len(steps) + 1))

    hops = [[factor[j * HEIGHT : (j + 1) * HEIGHT]] for j in range(count)]
    lines, swapped = [None] * count, [None] * count
    packs, mine, rounds = [], [], [0] * count

    def advance(j):
        done = len(hops[j])
        if done <= depth:
            pairs = first_hop if done == 1 else (last_hop if done == depth else next_hop)
            hops[j].append(lax.ppermute(hops[j][-1], BOTH, pairs))
            return hops[j], done
        lines[j] = pick(arrives, hops[j])
        swapped[j] = lax.ppermute(lines[j], BOTH, across)
        return swapped, j

    def send_on(j):
        mine[j] = to_rows(mine[j], steps[rounds[j]], row, nrow, ncol)
        rounds[j] += 1
        return mine, j

    def stage(number):
        return [advance(j) for j in range(count) if 0 <= number - j <= depth]

    tops = []
    for j in range(count):
        at = j * HEIGHT
        piece = own_part(panels, at, at + HEIGHT) - nt_dot(factor[at : at + HEIGHT], factor[at:width])
        tops.append(sum_over_col(piece, nrow, ncol))

    stage(0)
    for j in range(count):
        kept = stage(j + 1)
        for i in range(j - 1):
            if rounds[i] < len(steps):
                kept.append(send_on(i))
        pack, passed = panel_stage(row, tops[j], packs, [where[at] for where, at in kept])
        for (where, at), value in zip(kept, passed):
            where[at] = value
        packs.append(pack)
        mine.append(core_halves(pack)[0])

    rest = []
    for number in range(count + 1, count + depth):
        stage(number)
    which = jnp.where((row == 0) | on_line, 0, 1)
    for j in range(count):
        keep, send = update_product(factor, [lines[j], swapped[j]], which, col, ncol)
        rest.append(panels[:, j * HEIGHT : (j + 1) * HEIGHT] - scatter_sum(keep, send, nrow, ncol))
    rest = jnp.concatenate(rest, 1)
    out = []
    for j in range(count):
        while rounds[j] < len(steps):
            send_on(j)
        pack = join_halves(mine[j], nrow, ncol)
        solved = nt_dot(rest[:, :HEIGHT], pack[:, :HEIGHT], HIGH)
        rest = rest[:, HEIGHT:] - jnp.dot(solved, pack[:, HEIGHT:], precision=HIGH)
        out.append(solved)
    out = jnp.concatenate(out, 1)
    at_row = lax.broadcasted_iota(jnp.int32, out.shape, 0) + (row * ncol + col) * own
    at_col = lax.broadcasted_iota(jnp.int32, out.shape, 1)
    return jnp.where(at_col <= at_row, out, 0.0)


def solution(mesh):
    return jax.shard_map(
        functools.partial(on_device, mesh.shape["row"], mesh.shape["col"]),
        mesh=mesh,
        in_specs=(P("row", "col"), P(BOTH, None)),
        out_specs=P(BOTH, None),
        check_vma=False,
    )
```

```python
import functools
import jax
import jax.numpy as jnp
from jax import lax
from jax.experimental import pallas as pl
from jax.experimental.pallas import tpu as pltpu
from jax.sharding import PartitionSpec as P

SUB = 8
BLOCK = 128
STEP = 32
HEIGHT = 256
BOTH = ("row", "col")
HIGH = lax.Precision.HIGHEST


def tn_dot(a, b):
    return lax.dot_general(a, b, (((0,), (0,)), ((), ())), precision=HIGH, preferred_element_type=jnp.float32)


def nn_dot(a, b):
    return lax.dot_general(a, b, (((1,), (0,)), ((), ())), precision=HIGH, preferred_element_type=jnp.float32)


def row_of(x, k):
    return jnp.broadcast_to(x[k : k + 1, :], x.shape)


def lane_of(x, k):
    return jnp.broadcast_to(x[:, k : k + 1], x.shape)


def inverse_factor(block):
    lane = lax.broadcasted_iota(jnp.int32, (SUB, BLOCK), 1)
    sub = lax.broadcasted_iota(jnp.int32, (SUB, BLOCK), 0)
    groups = [block[SUB * q : SUB * (q + 1), :] for q in range(BLOCK // SUB)]
    per_step = STEP // SUB
    done = []
    for step in range(BLOCK // STEP):
        end = (step + 1) * per_step
        here = []
        for p in range(step * per_step, end):
            first = SUB * p
            inside = (lane >= first) & (lane < first + SUB)
            cols = [lane_of(groups[p], first + k) for k in range(SUB)]
            rows = jnp.where(inside, jnp.where(lane - first == sub, 1.0, 0.0), groups[p])
            scale = jnp.zeros((SUB, BLOCK), jnp.float32)
            col_rows, own_rows = [], []
            for k in range(SUB):
                pivot = row_of(cols[k], k)
                inv = pl.reciprocal(pivot, approx=True)
                scale = jnp.where(sub == k, lax.rsqrt(pivot), scale)
                below = jnp.where(sub > k, cols[k], 0.0)
                raw = [row_of(cols[m], k) for m in range(k + 1, SUB)]
                own = row_of(rows, k) * inv
                for i, m in enumerate(range(k + 1, SUB)):
                    cols[m] = cols[m] - (below * raw[i]) * inv
                rows = rows - below * own
                col_rows.append([r * inv for r in raw])
                own_rows.append(own)
            here.append(rows * scale)
            for q in range(p + 1, end):
                mult = [lane_of(groups[q], first + k) for k in range(SUB)]
                acc = jnp.where(inside, 0.0, groups[q])
                for k in range(SUB):
                    for i, m in enumerate(range(k + 1, SUB)):
                        mult[m] = mult[m] - mult[k] * col_rows[k][i]
                    acc = acc - mult[k] * own_rows[k]
                groups[q] = acc
        span = jnp.concatenate(here, 0)
        base = step * STEP
        span_lane = lax.broadcasted_iota(jnp.int32, (STEP, BLOCK), 1)
        span_row = lax.broadcasted_iota(jnp.int32, (STEP, BLOCK), 0) + base
        span = jnp.where((span_lane <= span_row) | (span_lane >= base + STEP), span, 0.0)
        done.append(jnp.where(span_lane <= span_row, span, 0.0))
        if base + STEP < BLOCK:
            delta = tn_dot(span, span)
            in_step = (lane >= base) & (lane < base + STEP)
            for q in range(end, BLOCK // SUB):
                groups[q] = jnp.where(in_step, 0.0, groups[q]) - delta[SUB * q : SUB * (q + 1), :]
    return jnp.concatenate(done, 0)


def factor_panel(height, skips, own_ref, earlier, out_ref):
    rest = own_ref[...]
    for ref, skip in zip(earlier, skips):
        span = ref[:, skip:]
        rest = rest - tn_dot(span[:, :height], span)
    out_ref[...] = jnp.zeros_like(out_ref)
    uppers, inverses = [], []
    for i in range(height // BLOCK):
        at = i * BLOCK
        inverse = inverse_factor(rest[:BLOCK, :BLOCK])
        if rest.shape[1] > BLOCK:
            upper = nn_dot(inverse, rest[:BLOCK, BLOCK:])
        line = []
        for j in range(i):
            total = 0.0
            for k in range(j, i):
                block = uppers[k][:, (i - k - 1) * BLOCK : (i - k) * BLOCK]
                total = total + tn_dot(block, inverses[k][j])
            line.append(-nn_dot(inverse, total))
        line.append(inverse)
        inverses.append(line)
        for j, block in enumerate(line):
            out_ref[at : at + BLOCK, j * BLOCK : (j + 1) * BLOCK] = block
        if rest.shape[1] > BLOCK:
            uppers.append(upper)
            left = height - at - BLOCK
            if upper.shape[1] > left:
                out_ref[at : at + BLOCK, height:] = upper[:, left:]
            if left:
                rest = rest[BLOCK:, BLOCK:] - tn_dot(upper[:, :left], upper)


def panel_kernel(height, skips, place_ref, own_ref, *refs):
    earlier, out_ref, half_ref = refs[: len(skips)], refs[-2], refs[-1]

    @pl.when(place_ref[0] == 0)
    def _():
        factor_panel(height, skips, own_ref, earlier, out_ref)
        half = height // 2
        half_ref[...] = out_ref[pl.ds(pl.multiple_of(place_ref[1] * half, half), half), :]


def panel_factor(place, own, earlier):
    height, wide = own.shape
    skips = [(len(earlier) - p) * height for p in range(len(earlier))]
    vmem = pl.BlockSpec(memory_space=pltpu.VMEM)
    return pl.pallas_call(
        functools.partial(panel_kernel, height, skips),
        out_shape=[jax.ShapeDtypeStruct((h, wide), jnp.float32) for h in (height, height // 2)],
        in_specs=[pl.BlockSpec(memory_space=pltpu.SMEM)] + [vmem] * (1 + len(earlier)),
        out_specs=[vmem, vmem],
        compiler_params=pltpu.CompilerParams(vmem_limit_bytes=40 << 20),
        cost_estimate=pl.CostEstimate(flops=10**10, bytes_accessed=8 * height * wide, transcendentals=0),
    )(place, own, *earlier)


def nt_dot(a, b, precision=None):
    return lax.dot_general(
        a, b, (((1,), (1,)), ((), ())), precision=precision, preferred_element_type=jnp.float32
    )


def update_kernel(slots, order_ref, factor_ref, *refs):
    choices, (keep_ref, send_ref, pivots, sem) = refs[:-4], refs[-4:]
    slot = pl.program_id(0)
    for i, choice in enumerate(choices):

        @pl.when((slot == 0) & (order_ref[slots] == i))
        def _():
            copy = pltpu.make_async_copy(choice, pivots, sem)
            copy.start()
            copy.wait()

    product = nt_dot(factor_ref[...], pivots[...])

    @pl.when(slot < slots // 2)
    def _():
        keep_ref[...] = product

    @pl.when(slot >= slots // 2)
    def _():
        send_ref[...] = product


def update_product(factor, choices, which, col, ncol):
    rows, depth = factor.shape
    own, count = rows // ncol, choices[0].shape[0]
    half = ncol // 2
    flips = list(range(0, ncol, 2)) + list(range(1, ncol, 2))
    order = jnp.concatenate([col ^ jnp.asarray(flips, jnp.int32), which[None]])
    out = jax.ShapeDtypeStruct((half * own, count), jnp.float32)
    return pl.pallas_call(
        functools.partial(update_kernel, ncol),
        out_shape=(out, out),
        grid_spec=pltpu.PrefetchScalarGridSpec(
            num_scalar_prefetch=1,
            grid=(ncol,),
            in_specs=[pl.BlockSpec((own, depth), lambda s, order: (order[s], 0))]
            + [pl.BlockSpec(memory_space=pltpu.HBM)] * len(choices),
            out_specs=(
                pl.BlockSpec((own, count), lambda s, order: (jnp.minimum(s, half - 1), 0)),
                pl.BlockSpec((own, count), lambda s, order: (jnp.maximum(s - half, 0), 0)),
            ),
            scratch_shapes=[pltpu.VMEM((count, depth), factor.dtype), pltpu.SemaphoreType.DMA],
        ),
        compiler_params=pltpu.CompilerParams(vmem_limit_bytes=40 << 20),
        cost_estimate=pl.CostEstimate(
            flops=2 * rows * depth * count, bytes_accessed=2 * rows * depth + 4 * rows * count, transcendentals=0
        ),
    )(order, factor, *choices)


def along_row(block, moves, ncol):
    return lax.ppermute(block, BOTH, [(a * ncol + c, b * ncol + c) for c in range(ncol) for a, b in moves[c % 2]])


def spread_block(block, row, odd, nrow, ncol):
    depth = nrow // 2
    line, cross, choices = [block], [None], [block]
    for h in range(1, depth + 1):
        even = [(2 * h - 2, 2 * h)] if h < depth else []
        line.append(along_row(line[-1], (even, [(max(2 * h - 3, 0), 2 * h - 1)]), ncol))
        even = [(2 * h, 2 * h + 1)] if h < depth else []
        odds = [(2 * h - 1, 2 * h - 2)] if h > 1 else []
        cross.append(along_row(line[-1], (even, odds), ncol))
    last = along_row(cross[1], ([(3, 1)], []), ncol)
    choices = line + cross[1:] + [last]
    half = row // 2
    even_which = jnp.where(row % 2 == 0, half, jnp.where(row == 1, 2 * depth + 1, depth + half))
    odd_which = jnp.where(row % 2 == 1, half + 1, jnp.where(row == 0, 0, depth + half + 1))
    which = jnp.where(odd == 1, odd_which, even_which)
    if depth > 4:
        kept = choices[0]
        for i, choice in enumerate(choices[1:]):
            kept = jnp.where(which == i + 1, choice, kept)
        choices, which = [kept], jnp.zeros_like(which)
    return choices, which


def along_col(block, bit, nrow, ncol):
    return lax.ppermute(block, BOTH, [(r * ncol + c, r * ncol + (c ^ bit)) for r in range(nrow) for c in range(ncol)])


def core_halves(block):
    half = block.shape[0] // 2
    low = lax.axis_index("col") % 2
    mine = lax.dynamic_slice_in_dim(block, low * half, half, 0)
    other = lax.dynamic_slice_in_dim(block, (1 - low) * half, half, 0)
    return mine, other


def join_halves(mine, nrow, ncol):
    other = along_col(mine, 1, nrow, ncol)
    low = lax.axis_index("col") % 2
    return jnp.where(low == 0, jnp.concatenate([mine, other], 0), jnp.concatenate([other, mine], 0))


def sum_over_col(block, nrow, ncol):
    mine, other = core_halves(block)
    mine = mine + along_col(other, 1, nrow, ncol)
    bit = 2
    while bit < ncol:
        mine = mine + along_col(mine, bit, nrow, ncol)
        bit *= 2
    return join_halves(mine, nrow, ncol)


def scatter_sum(keep, send, nrow, ncol):
    keep = keep + along_col(send, 1, nrow, ncol)
    bit = ncol // 2
    while bit > 1:
        half = keep.shape[0] // 2
        keep = keep[:half] + along_col(keep[half:], bit, nrow, ncol)
        bit //= 2
    return keep


def to_rows(mine, row, nrow, ncol):
    step = nrow // 2
    while step:
        moves = [(r, r + step) for r in range(0, nrow, 2 * step)]
        got = along_row(mine, (moves, moves), ncol)
        mine = jnp.where(row % (2 * step) == step, got, mine)
        step //= 2
    return mine


def own_part(panels, at, end):
    own = panels.shape[0]
    col = lax.axis_index("col")
    blocks = []
    for c in range(at // own, -(-end // own)):
        first, last = max(at, c * own), min(end, (c + 1) * own)
        blocks.append(jnp.where(col == c, panels[first - c * own : last - c * own, at:], 0.0))
    return jnp.concatenate(blocks, 0)


def on_device(nrow, ncol, factor, panels):
    own, width = panels.shape
    row, col = lax.axis_index("row"), lax.axis_index("col")
    odd = col % 2
    count = width // HEIGHT
    place = jnp.stack([row, odd]).astype(jnp.int32)

    pivots = [spread_block(factor[j * HEIGHT : (j + 1) * HEIGHT], row, odd, nrow, ncol) for j in range(count)]

    packs, spread = [], []
    for j in range(count):
        at = j * HEIGHT
        piece = own_part(panels, at, at + HEIGHT) - nt_dot(factor[at : at + HEIGHT], factor[at:width])
        pack, half = panel_factor(place, sum_over_col(piece, nrow, ncol), packs)
        packs.append(pack)
        spread.append(join_halves(to_rows(half, row, nrow, ncol), nrow, ncol))

    rest = []
    for j, (choices, which) in enumerate(pivots):
        keep, send = update_product(factor, choices, which, col, ncol)
        rest.append(panels[:, j * HEIGHT : (j + 1) * HEIGHT] - scatter_sum(keep, send, nrow, ncol))
    rest = jnp.concatenate(rest, 1)
    out = []
    for pack in spread:
        solved = nt_dot(rest[:, :HEIGHT], pack[:, :HEIGHT], HIGH)
        rest = rest[:, HEIGHT:] - jnp.dot(solved, pack[:, HEIGHT:], precision=HIGH)
        out.append(solved)
    out = jnp.concatenate(out, 1)
    at_row = lax.broadcasted_iota(jnp.int32, out.shape, 0) + (row * ncol + col) * own
    at_col = lax.broadcasted_iota(jnp.int32, out.shape, 1)
    return jnp.where(at_col <= at_row, out, 0.0)


def solution(mesh):
    return jax.shard_map(
        functools.partial(on_device, mesh.shape["row"], mesh.shape["col"]),
        mesh=mesh,
        in_specs=(P("row", "col"), P(BOTH, None)),
        out_specs=P(BOTH, None),
        check_vma=False,
    )
```

```python
import functools
import jax
import jax.numpy as jnp
from jax import lax
from jax.experimental import pallas as pl
from jax.experimental.pallas import tpu as pltpu
from jax.sharding import PartitionSpec as P

SUB = 8
BLOCK = 128
STEP = 32
COLUMNS = 256
PARTS = 2
BOTH = ("row", "col")
HIGH = lax.Precision.HIGHEST


def tn_dot(a, b):
    return lax.dot_general(a, b, (((0,), (0,)), ((), ())), precision=HIGH, preferred_element_type=jnp.float32)


def nn_dot(a, b):
    return lax.dot_general(a, b, (((1,), (0,)), ((), ())), precision=HIGH, preferred_element_type=jnp.float32)


def row_of(x, k):
    return jnp.broadcast_to(x[k : k + 1, :], x.shape)


def lane_of(x, k):
    return jnp.broadcast_to(x[:, k : k + 1], x.shape)


def inverse_factor(block):
    lane = lax.broadcasted_iota(jnp.int32, (SUB, BLOCK), 1)
    sub = lax.broadcasted_iota(jnp.int32, (SUB, BLOCK), 0)
    groups = [block[SUB * q : SUB * (q + 1), :] for q in range(BLOCK // SUB)]
    per_step = STEP // SUB
    done = []
    for step in range(BLOCK // STEP):
        end = (step + 1) * per_step
        here = []
        for p in range(step * per_step, end):
            first = SUB * p
            inside = (lane >= first) & (lane < first + SUB)
            cols = [lane_of(groups[p], first + k) for k in range(SUB)]
            rows = jnp.where(inside, jnp.where(lane - first == sub, 1.0, 0.0), groups[p])
            scale = jnp.zeros((SUB, BLOCK), jnp.float32)
            col_rows, own_rows = [], []
            for k in range(SUB):
                pivot = row_of(cols[k], k)
                inv = pl.reciprocal(pivot, approx=True)
                scale = jnp.where(sub == k, lax.rsqrt(pivot), scale)
                below = jnp.where(sub > k, cols[k], 0.0)
                raw = [row_of(cols[m], k) for m in range(k + 1, SUB)]
                own = row_of(rows, k) * inv
                for i, m in enumerate(range(k + 1, SUB)):
                    cols[m] = cols[m] - (below * raw[i]) * inv
                rows = rows - below * own
                col_rows.append([r * inv for r in raw])
                own_rows.append(own)
            here.append(rows * scale)
            for q in range(p + 1, end):
                mult = [lane_of(groups[q], first + k) for k in range(SUB)]
                acc = jnp.where(inside, 0.0, groups[q])
                for k in range(SUB):
                    for i, m in enumerate(range(k + 1, SUB)):
                        mult[m] = mult[m] - mult[k] * col_rows[k][i]
                    acc = acc - mult[k] * own_rows[k]
                groups[q] = acc
        span = jnp.concatenate(here, 0)
        base = step * STEP
        span_lane = lax.broadcasted_iota(jnp.int32, (STEP, BLOCK), 1)
        span_row = lax.broadcasted_iota(jnp.int32, (STEP, BLOCK), 0) + base
        span = jnp.where((span_lane <= span_row) | (span_lane >= base + STEP), span, 0.0)
        done.append(jnp.where(span_lane <= span_row, span, 0.0))
        if base + STEP < BLOCK:
            delta = tn_dot(span, span)
            in_step = (lane >= base) & (lane < base + STEP)
            for q in range(end, BLOCK // SUB):
                groups[q] = jnp.where(in_step, 0.0, groups[q]) - delta[SUB * q : SUB * (q + 1), :]
    return jnp.concatenate(done, 0)


def factor_panel(height, skips, own_ref, earlier, out_ref):
    rest = own_ref[...]
    for ref, skip in zip(earlier, skips):
        span = ref[:, skip:]
        rest = rest - tn_dot(span[:, :height], span)
    out_ref[...] = jnp.zeros_like(out_ref)
    uppers, inverses = [], []
    for i in range(height // BLOCK):
        at = i * BLOCK
        inverse = inverse_factor(rest[:BLOCK, :BLOCK])
        if rest.shape[1] > BLOCK:
            upper = nn_dot(inverse, rest[:BLOCK, BLOCK:])
        line = []
        for j in range(i):
            total = 0.0
            for k in range(j, i):
                block = uppers[k][:, (i - k - 1) * BLOCK : (i - k) * BLOCK]
                total = total + tn_dot(block, inverses[k][j])
            line.append(-nn_dot(inverse, total))
        line.append(inverse)
        inverses.append(line)
        for j, block in enumerate(line):
            out_ref[at : at + BLOCK, j * BLOCK : (j + 1) * BLOCK] = block
        if rest.shape[1] > BLOCK:
            uppers.append(upper)
            left = height - at - BLOCK
            if upper.shape[1] > left:
                out_ref[at : at + BLOCK, height:] = upper[:, left:]
            if left:
                rest = rest[BLOCK:, BLOCK:] - tn_dot(upper[:, :left], upper)


def panel_kernel(height, skips, place_ref, own_ref, *refs):
    earlier, out_ref, share_ref = refs[: len(skips)], refs[-2], refs[-1]
    share = share_ref.shape[0]

    @pl.when(place_ref[0] == 0)
    def _():
        factor_panel(height, skips, own_ref, earlier, out_ref)
        share_ref[...] = out_ref[pl.ds(pl.multiple_of(place_ref[1] * share, share), share), :]


def panel_factor(place, ncol, own, earlier):
    height, wide = own.shape
    skips = [(len(earlier) - p) * height for p in range(len(earlier))]
    vmem = pl.BlockSpec(memory_space=pltpu.VMEM)
    return pl.pallas_call(
        functools.partial(panel_kernel, height, skips),
        out_shape=[jax.ShapeDtypeStruct((h, wide), jnp.float32) for h in (height, height // ncol)],
        in_specs=[pl.BlockSpec(memory_space=pltpu.SMEM)] + [vmem] * (1 + len(earlier)),
        out_specs=[vmem, vmem],
        compiler_params=pltpu.CompilerParams(vmem_limit_bytes=40 << 20),
        cost_estimate=pl.CostEstimate(flops=2 * 10**10, bytes_accessed=8 * height * wide, transcendentals=0),
    )(place, own, *earlier)


def nt_dot(a, b, precision=None):
    return lax.dot_general(
        a, b, (((1,), (1,)), ((), ())), precision=precision, preferred_element_type=jnp.float32
    )


def update_kernel(slots, order_ref, factor_ref, pivots_ref, keep_ref, send_ref):
    slot = pl.program_id(0)
    product = nt_dot(factor_ref[...], pivots_ref[...])

    @pl.when(slot < slots // 2)
    def _():
        keep_ref[...] = product

    @pl.when(slot >= slots // 2)
    def _():
        send_ref[...] = product


def update_product(factor, pivots, at, col, ncol):
    rows, depth = factor.shape
    own = rows // ncol
    half = ncol // 2
    flips = list(range(0, ncol, 2)) + list(range(1, ncol, 2))
    order = col ^ jnp.asarray(flips, jnp.int32)
    out = jax.ShapeDtypeStruct((half * own, COLUMNS), jnp.float32)
    return pl.pallas_call(
        functools.partial(update_kernel, ncol),
        out_shape=(out, out),
        grid_spec=pltpu.PrefetchScalarGridSpec(
            num_scalar_prefetch=1,
            grid=(ncol,),
            in_specs=[
                pl.BlockSpec((own, depth), lambda s, order: (order[s], 0)),
                pl.BlockSpec((COLUMNS, depth), lambda s, order: (at, 0)),
            ],
            out_specs=(
                pl.BlockSpec((own, COLUMNS), lambda s, order: (jnp.minimum(s, half - 1), 0)),
                pl.BlockSpec((own, COLUMNS), lambda s, order: (jnp.maximum(s - half, 0), 0)),
            ),
        ),
        compiler_params=pltpu.CompilerParams(vmem_limit_bytes=40 << 20),
        cost_estimate=pl.CostEstimate(
            flops=2 * rows * depth * COLUMNS, bytes_accessed=2 * rows * depth + 4 * rows * COLUMNS, transcendentals=0
        ),
    )(order, factor, pivots)


def along_row(block, moves, ncol):
    return lax.ppermute(block, BOTH, [(a * ncol + c, b * ncol + c) for c in range(ncol) for a, b in moves[c % 2]])


def spread_pivots(rows, row, odd, nrow, ncol):
    piece = rows.shape[0] // nrow
    even_order = list(range(2, nrow, 2)) + list(range(1, nrow, 2))
    odd_order = list(range(1, nrow, 2)) + list(range(2, nrow, 2))
    mine = rows[:piece]
    for a, b in zip(even_order, odd_order):
        start = jnp.where(odd == 1, b, a) * piece
        part = lax.dynamic_slice_in_dim(rows, start, piece, 0)
        got = along_row(part, ([(0, a)], [(0, b)]), ncol)
        mine = jnp.where(row == jnp.where(odd == 1, b, a), got, mine)
    return lax.all_gather(mine, "row", axis=0, tiled=True)


def along_col(block, bit, nrow, ncol):
    return lax.ppermute(block, BOTH, [(r * ncol + c, r * ncol + (c ^ bit)) for r in range(nrow) for c in range(ncol)])


def core_halves(block):
    half = block.shape[0] // 2
    low = lax.axis_index("col") % 2
    mine = lax.dynamic_slice_in_dim(block, low * half, half, 0)
    other = lax.dynamic_slice_in_dim(block, (1 - low) * half, half, 0)
    return mine, other


def join(mine, bit, nrow, ncol):
    other = along_col(mine, bit, nrow, ncol)
    low = lax.axis_index("col") & bit
    return jnp.where(low == 0, jnp.concatenate([mine, other], 0), jnp.concatenate([other, mine], 0))


def sum_over_col(block, nrow, ncol):
    mine, other = core_halves(block)
    mine = mine + along_col(other, 1, nrow, ncol)
    bit = 2
    while bit < ncol:
        mine = mine + along_col(mine, bit, nrow, ncol)
        bit *= 2
    return join(mine, 1, nrow, ncol)


def scatter_sum(keep, send, nrow, ncol):
    keep = keep + along_col(send, 1, nrow, ncol)
    bit = ncol // 2
    while bit > 1:
        half = keep.shape[0] // 2
        keep = keep[:half] + along_col(keep[half:], bit, nrow, ncol)
        bit //= 2
    return keep


def to_rows(mine, row, nrow, ncol):
    step = nrow // 2
    while step:
        moves = [(r, r + step) for r in range(0, nrow, 2 * step)]
        got = along_row(mine, (moves, moves), ncol)
        mine = jnp.where(row % (2 * step) == step, got, mine)
        step //= 2
    return mine


def own_part(panels, at, end):
    own = panels.shape[0]
    col = lax.axis_index("col")
    blocks = []
    for c in range(at // own, -(-end // own)):
        first, last = max(at, c * own), min(end, (c + 1) * own)
        blocks.append(jnp.where(col == c, panels[first - c * own : last - c * own, at:], 0.0))
    return jnp.concatenate(blocks, 0)


def on_device(nrow, ncol, factor, panels):
    own, width = panels.shape
    row, col = lax.axis_index("row"), lax.axis_index("col")
    odd = col % 2
    share = width // PARTS
    place = jnp.stack([row, col]).astype(jnp.int32)

    packs, spread = [], []
    for at in range(0, width, share):
        piece = own_part(panels, at, at + share) - nt_dot(factor[at : at + share], factor[at:width])
        pack, mine = panel_factor(place, ncol, sum_over_col(piece, nrow, ncol), packs)
        packs.append(pack)
        mine = to_rows(mine, row, nrow, ncol)
        bit = 1
        while bit < ncol:
            mine = join(mine, bit, nrow, ncol)
            bit *= 2
        spread.append(mine)

    rest = []
    for at in range(0, width, share):
        pivots = spread_pivots(factor[at : at + share], row, odd, nrow, ncol)
        for j in range(share // COLUMNS):
            keep, send = update_product(factor, pivots, j, col, ncol)
            first = at + j * COLUMNS
            rest.append(panels[:, first : first + COLUMNS] - scatter_sum(keep, send, nrow, ncol))
    rest = jnp.concatenate(rest, 1)
    out = []
    for pack in spread:
        solved = nt_dot(rest[:, :share], pack[:, :share], HIGH)
        rest = rest[:, share:] - jnp.dot(solved, pack[:, share:], precision=HIGH)
        out.append(solved)
    out = jnp.concatenate(out, 1)
    at_row = lax.broadcasted_iota(jnp.int32, out.shape, 0) + (row * ncol + col) * own
    at_col = lax.broadcasted_iota(jnp.int32, out.shape, 1)
    return jnp.where(at_col <= at_row, out, 0.0)


def solution(mesh):
    return jax.shard_map(
        functools.partial(on_device, mesh.shape["row"], mesh.shape["col"]),
        mesh=mesh,
        in_specs=(P("row", "col"), P(BOTH, None)),
        out_specs=P(BOTH, None),
        check_vma=False,
    )
```

```python
import functools
import jax
import jax.numpy as jnp
from jax import lax
from jax.experimental import pallas as pl
from jax.experimental.pallas import tpu as pltpu
from jax.sharding import PartitionSpec as P

SUB = 8
BLOCK = 128
STEP = 32
COLUMNS = 256
PARTS = 2
BOTH = ("row", "col")
HIGH = lax.Precision.HIGHEST


def tn_dot(a, b):
    return lax.dot_general(a, b, (((0,), (0,)), ((), ())), precision=HIGH, preferred_element_type=jnp.float32)


def nn_dot(a, b):
    return lax.dot_general(a, b, (((1,), (0,)), ((), ())), precision=HIGH, preferred_element_type=jnp.float32)


def row_of(x, k):
    return jnp.broadcast_to(x[k : k + 1, :], x.shape)


def lane_of(x, k):
    return jnp.broadcast_to(x[:, k : k + 1], x.shape)


def inverse_factor(block):
    lane = lax.broadcasted_iota(jnp.int32, (SUB, BLOCK), 1)
    sub = lax.broadcasted_iota(jnp.int32, (SUB, BLOCK), 0)
    groups = [block[SUB * q : SUB * (q + 1), :] for q in range(BLOCK // SUB)]
    per_step = STEP // SUB
    done = []
    for step in range(BLOCK // STEP):
        end = (step + 1) * per_step
        here = []
        for p in range(step * per_step, end):
            first = SUB * p
            inside = (lane >= first) & (lane < first + SUB)
            cols = [lane_of(groups[p], first + k) for k in range(SUB)]
            rows = jnp.where(inside, jnp.where(lane - first == sub, 1.0, 0.0), groups[p])
            scale = jnp.zeros((SUB, BLOCK), jnp.float32)
            col_rows, own_rows = [], []
            for k in range(SUB):
                pivot = row_of(cols[k], k)
                inv = pl.reciprocal(pivot, approx=True)
                scale = jnp.where(sub == k, lax.rsqrt(pivot), scale)
                below = jnp.where(sub > k, cols[k], 0.0)
                raw = [row_of(cols[m], k) for m in range(k + 1, SUB)]
                own = row_of(rows, k) * inv
                for i, m in enumerate(range(k + 1, SUB)):
                    cols[m] = cols[m] - (below * raw[i]) * inv
                rows = rows - below * own
                col_rows.append([r * inv for r in raw])
                own_rows.append(own)
            here.append(rows * scale)
            for q in range(p + 1, end):
                mult = [lane_of(groups[q], first + k) for k in range(SUB)]
                acc = jnp.where(inside, 0.0, groups[q])
                for k in range(SUB):
                    for i, m in enumerate(range(k + 1, SUB)):
                        mult[m] = mult[m] - mult[k] * col_rows[k][i]
                    acc = acc - mult[k] * own_rows[k]
                groups[q] = acc
        span = jnp.concatenate(here, 0)
        base = step * STEP
        span_lane = lax.broadcasted_iota(jnp.int32, (STEP, BLOCK), 1)
        span_row = lax.broadcasted_iota(jnp.int32, (STEP, BLOCK), 0) + base
        span = jnp.where((span_lane <= span_row) | (span_lane >= base + STEP), span, 0.0)
        done.append(jnp.where(span_lane <= span_row, span, 0.0))
        if base + STEP < BLOCK:
            delta = tn_dot(span, span)
            in_step = (lane >= base) & (lane < base + STEP)
            for q in range(end, BLOCK // SUB):
                groups[q] = jnp.where(in_step, 0.0, groups[q]) - delta[SUB * q : SUB * (q + 1), :]
    return jnp.concatenate(done, 0)


def factor_panel(height, skips, own_ref, earlier, out_ref):
    rest = own_ref[...]
    for ref, skip in zip(earlier, skips):
        span = ref[:, skip:]
        rest = rest - tn_dot(span[:, :height], span)
    out_ref[...] = jnp.zeros_like(out_ref)
    uppers, inverses = [], []
    for i in range(height // BLOCK):
        at = i * BLOCK
        inverse = inverse_factor(rest[:BLOCK, :BLOCK])
        if rest.shape[1] > BLOCK:
            upper = nn_dot(inverse, rest[:BLOCK, BLOCK:])
        line = []
        for j in range(i):
            total = 0.0
            for k in range(j, i):
                block = uppers[k][:, (i - k - 1) * BLOCK : (i - k) * BLOCK]
                total = total + tn_dot(block, inverses[k][j])
            line.append(-nn_dot(inverse, total))
        line.append(inverse)
        inverses.append(line)
        for j, block in enumerate(line):
            out_ref[at : at + BLOCK, j * BLOCK : (j + 1) * BLOCK] = block
        if rest.shape[1] > BLOCK:
            uppers.append(upper)
            left = height - at - BLOCK
            if upper.shape[1] > left:
                out_ref[at : at + BLOCK, height:] = upper[:, left:]
            if left:
                rest = rest[BLOCK:, BLOCK:] - tn_dot(upper[:, :left], upper)


def panel_kernel(height, skips, place_ref, own_ref, *refs):
    earlier, out_ref, share_ref = refs[: len(skips)], refs[-2], refs[-1]
    share = share_ref.shape[0]

    @pl.when(place_ref[0] == 0)
    def _():
        factor_panel(height, skips, own_ref, earlier, out_ref)
        share_ref[...] = out_ref[pl.ds(pl.multiple_of(place_ref[1] * share, share), share), :]


def panel_factor(place, ncol, own, earlier):
    height, wide = own.shape
    skips = [(len(earlier) - p) * height for p in range(len(earlier))]
    vmem = pl.BlockSpec(memory_space=pltpu.VMEM)
    return pl.pallas_call(
        functools.partial(panel_kernel, height, skips),
        out_shape=[jax.ShapeDtypeStruct((h, wide), jnp.float32) for h in (height, height // ncol)],
        in_specs=[pl.BlockSpec(memory_space=pltpu.SMEM)] + [vmem] * (1 + len(earlier)),
        out_specs=[vmem, vmem],
        compiler_params=pltpu.CompilerParams(vmem_limit_bytes=40 << 20),
        cost_estimate=pl.CostEstimate(flops=2 * 10**10, bytes_accessed=8 * height * wide, transcendentals=0),
    )(place, own, *earlier)


def nt_dot(a, b, precision=None):
    return lax.dot_general(
        a, b, (((1,), (1,)), ((), ())), precision=precision, preferred_element_type=jnp.float32
    )


def update_kernel(slots, order_ref, factor_ref, pivots_ref, keep_ref, send_ref):
    slot = pl.program_id(0)
    product = nt_dot(factor_ref[...], pivots_ref[...])

    @pl.when(slot < slots // 2)
    def _():
        keep_ref[...] = product

    @pl.when(slot >= slots // 2)
    def _():
        send_ref[...] = product


def update_product(factor, pivots, at, col, ncol):
    rows, depth = factor.shape
    own = rows // ncol
    half = ncol // 2
    flips = list(range(0, ncol, 2)) + list(range(1, ncol, 2))
    order = col ^ jnp.asarray(flips, jnp.int32)
    out = jax.ShapeDtypeStruct((half * own, COLUMNS), jnp.float32)
    return pl.pallas_call(
        functools.partial(update_kernel, ncol),
        out_shape=(out, out),
        grid_spec=pltpu.PrefetchScalarGridSpec(
            num_scalar_prefetch=1,
            grid=(ncol,),
            in_specs=[
                pl.BlockSpec((own, depth), lambda s, order: (order[s], 0)),
                pl.BlockSpec((COLUMNS, depth), lambda s, order: (at, 0)),
            ],
            out_specs=(
                pl.BlockSpec((own, COLUMNS), lambda s, order: (jnp.minimum(s, half - 1), 0)),
                pl.BlockSpec((own, COLUMNS), lambda s, order: (jnp.maximum(s - half, 0), 0)),
            ),
        ),
        compiler_params=pltpu.CompilerParams(vmem_limit_bytes=40 << 20),
        cost_estimate=pl.CostEstimate(
            flops=2 * rows * depth * COLUMNS, bytes_accessed=2 * rows * depth + 4 * rows * COLUMNS, transcendentals=0
        ),
    )(order, factor, pivots)


def along_row(block, moves, ncol):
    return lax.ppermute(block, BOTH, [(a * ncol + c, b * ncol + c) for c in range(ncol) for a, b in moves[c % 2]])


def along_col(block, bit, nrow, ncol):
    return lax.ppermute(block, BOTH, [(r * ncol + c, r * ncol + (c ^ bit)) for r in range(nrow) for c in range(ncol)])


def core_halves(block):
    half = block.shape[0] // 2
    low = lax.axis_index("col") % 2
    mine = lax.dynamic_slice_in_dim(block, low * half, half, 0)
    other = lax.dynamic_slice_in_dim(block, (1 - low) * half, half, 0)
    return mine, other


def join(mine, bit, nrow, ncol):
    other = along_col(mine, bit, nrow, ncol)
    low = lax.axis_index("col") & bit
    return jnp.where(low == 0, jnp.concatenate([mine, other], 0), jnp.concatenate([other, mine], 0))


def sum_over_col(block, nrow, ncol):
    mine, other = core_halves(block)
    mine = mine + along_col(other, 1, nrow, ncol)
    bit = 2
    while bit < ncol:
        mine = mine + along_col(mine, bit, nrow, ncol)
        bit *= 2
    return join(mine, 1, nrow, ncol)


def scatter_sum(keep, send, nrow, ncol):
    keep = keep + along_col(send, 1, nrow, ncol)
    bit = ncol // 2
    while bit > 1:
        half = keep.shape[0] // 2
        keep = keep[:half] + along_col(keep[half:], bit, nrow, ncol)
        bit //= 2
    return keep


def to_rows(mine, row, nrow, ncol):
    step = nrow // 2
    while step:
        moves = [(r, r + step) for r in range(0, nrow, 2 * step)]
        got = along_row(mine, (moves, moves), ncol)
        mine = jnp.where(row % (2 * step) == step, got, mine)
        step //= 2
    return mine


def own_part(panels, at, end):
    own = panels.shape[0]
    col = lax.axis_index("col")
    blocks = []
    for c in range(at // own, -(-end // own)):
        first, last = max(at, c * own), min(end, (c + 1) * own)
        blocks.append(jnp.where(col == c, panels[first - c * own : last - c * own, at:], 0.0))
    return jnp.concatenate(blocks, 0)


def on_device(nrow, ncol, factor, panels):
    own, width = panels.shape
    row, col = lax.axis_index("row"), lax.axis_index("col")
    share = width // PARTS
    place = jnp.stack([row, col]).astype(jnp.int32)

    packs, spread = [], []
    for at in range(0, width, share):
        piece = own_part(panels, at, at + share) - nt_dot(factor[at : at + share], factor[at:width])
        pack, mine = panel_factor(place, ncol, sum_over_col(piece, nrow, ncol), packs)
        packs.append(pack)
        mine = to_rows(mine, row, nrow, ncol)
        bit = 1
        while bit < ncol:
            mine = join(mine, bit, nrow, ncol)
            bit *= 2
        spread.append(mine)

    pivots = lax.psum(jnp.where(row == 0, factor, jnp.zeros_like(factor)), "row")
    rest = []
    for j in range(width // COLUMNS):
        keep, send = update_product(factor, pivots, j, col, ncol)
        first = j * COLUMNS
        rest.append(panels[:, first : first + COLUMNS] - scatter_sum(keep, send, nrow, ncol))
    rest = jnp.concatenate(rest, 1)
    out = []
    for pack in spread:
        solved = nt_dot(rest[:, :share], pack[:, :share], HIGH)
        rest = rest[:, share:] - jnp.dot(solved, pack[:, share:], precision=HIGH)
        out.append(solved)
    out = jnp.concatenate(out, 1)
    at_row = lax.broadcasted_iota(jnp.int32, out.shape, 0) + (row * ncol + col) * own
    at_col = lax.broadcasted_iota(jnp.int32, out.shape, 1)
    return jnp.where(at_col <= at_row, out, 0.0)


def solution(mesh):
    return jax.shard_map(
        functools.partial(on_device, mesh.shape["row"], mesh.shape["col"]),
        mesh=mesh,
        in_specs=(P("row", "col"), P(BOTH, None)),
        out_specs=P(BOTH, None),
        check_vma=False,
    )
```

```python
import functools
import jax
import jax.numpy as jnp
from jax import lax
from jax.experimental import pallas as pl
from jax.experimental.pallas import tpu as pltpu
from jax.sharding import PartitionSpec as P

SUB = 8
BLOCK = 128
STEP = 32
PARTS = 2
BOTH = ("row", "col")
HIGH = lax.Precision.HIGHEST


def tn_dot(a, b):
    return lax.dot_general(a, b, (((0,), (0,)), ((), ())), precision=HIGH, preferred_element_type=jnp.float32)


def nn_dot(a, b):
    return lax.dot_general(a, b, (((1,), (0,)), ((), ())), precision=HIGH, preferred_element_type=jnp.float32)


def row_of(x, k):
    return jnp.broadcast_to(x[k : k + 1, :], x.shape)


def lane_of(x, k):
    return jnp.broadcast_to(x[:, k : k + 1], x.shape)


def inverse_factor(block):
    lane = lax.broadcasted_iota(jnp.int32, (SUB, BLOCK), 1)
    sub = lax.broadcasted_iota(jnp.int32, (SUB, BLOCK), 0)
    groups = [block[SUB * q : SUB * (q + 1), :] for q in range(BLOCK // SUB)]
    per_step = STEP // SUB
    done = []
    for step in range(BLOCK // STEP):
        end = (step + 1) * per_step
        here = []
        for p in range(step * per_step, end):
            first = SUB * p
            inside = (lane >= first) & (lane < first + SUB)
            cols = [lane_of(groups[p], first + k) for k in range(SUB)]
            rows = jnp.where(inside, jnp.where(lane - first == sub, 1.0, 0.0), groups[p])
            scale = jnp.zeros((SUB, BLOCK), jnp.float32)
            col_rows, own_rows = [], []
            for k in range(SUB):
                pivot = row_of(cols[k], k)
                inv = pl.reciprocal(pivot, approx=True)
                scale = jnp.where(sub == k, lax.rsqrt(pivot), scale)
                below = jnp.where(sub > k, cols[k], 0.0)
                raw = [row_of(cols[m], k) for m in range(k + 1, SUB)]
                own = row_of(rows, k) * inv
                for i, m in enumerate(range(k + 1, SUB)):
                    cols[m] = cols[m] - (below * raw[i]) * inv
                rows = rows - below * own
                col_rows.append([r * inv for r in raw])
                own_rows.append(own)
            here.append(rows * scale)
            for q in range(p + 1, end):
                mult = [lane_of(groups[q], first + k) for k in range(SUB)]
                acc = jnp.where(inside, 0.0, groups[q])
                for k in range(SUB):
                    for i, m in enumerate(range(k + 1, SUB)):
                        mult[m] = mult[m] - mult[k] * col_rows[k][i]
                    acc = acc - mult[k] * own_rows[k]
                groups[q] = acc
        span = jnp.concatenate(here, 0)
        base = step * STEP
        span_lane = lax.broadcasted_iota(jnp.int32, (STEP, BLOCK), 1)
        span_row = lax.broadcasted_iota(jnp.int32, (STEP, BLOCK), 0) + base
        span = jnp.where((span_lane <= span_row) | (span_lane >= base + STEP), span, 0.0)
        done.append(jnp.where(span_lane <= span_row, span, 0.0))
        if base + STEP < BLOCK:
            delta = tn_dot(span, span)
            in_step = (lane >= base) & (lane < base + STEP)
            for q in range(end, BLOCK // SUB):
                groups[q] = jnp.where(in_step, 0.0, groups[q]) - delta[SUB * q : SUB * (q + 1), :]
    return jnp.concatenate(done, 0)


def factor_panel(height, skips, own_ref, earlier, out_ref):
    rest = own_ref[...]
    for ref, skip in zip(earlier, skips):
        span = ref[:, skip:]
        rest = rest - tn_dot(span[:, :height], span)
    out_ref[...] = jnp.zeros_like(out_ref)
    uppers, inverses = [], []
    for i in range(height // BLOCK):
        at = i * BLOCK
        inverse = inverse_factor(rest[:BLOCK, :BLOCK])
        if rest.shape[1] > BLOCK:
            upper = nn_dot(inverse, rest[:BLOCK, BLOCK:])
        line = []
        for j in range(i):
            total = 0.0
            for k in range(j, i):
                block = uppers[k][:, (i - k - 1) * BLOCK : (i - k) * BLOCK]
                total = total + tn_dot(block, inverses[k][j])
            line.append(-nn_dot(inverse, total))
        line.append(inverse)
        inverses.append(line)
        for j, block in enumerate(line):
            out_ref[at : at + BLOCK, j * BLOCK : (j + 1) * BLOCK] = block
        if rest.shape[1] > BLOCK:
            uppers.append(upper)
            left = height - at - BLOCK
            if upper.shape[1] > left:
                out_ref[at : at + BLOCK, height:] = upper[:, left:]
            if left:
                rest = rest[BLOCK:, BLOCK:] - tn_dot(upper[:, :left], upper)


def panel_kernel(height, skips, place_ref, own_ref, *refs):
    earlier, out_ref, share_ref = refs[: len(skips)], refs[-2], refs[-1]
    share = share_ref.shape[0]

    @pl.when(place_ref[0] == 0)
    def _():
        factor_panel(height, skips, own_ref, earlier, out_ref)
        share_ref[...] = out_ref[pl.ds(pl.multiple_of(place_ref[1] * share, share), share), :]


def panel_factor(place, ncol, own, earlier):
    height, wide = own.shape
    skips = [(len(earlier) - p) * height for p in range(len(earlier))]
    vmem = pl.BlockSpec(memory_space=pltpu.VMEM)
    return pl.pallas_call(
        functools.partial(panel_kernel, height, skips),
        out_shape=[jax.ShapeDtypeStruct((h, wide), jnp.float32) for h in (height, height // ncol)],
        in_specs=[pl.BlockSpec(memory_space=pltpu.SMEM)] + [vmem] * (1 + len(earlier)),
        out_specs=[vmem, vmem],
        compiler_params=pltpu.CompilerParams(vmem_limit_bytes=40 << 20),
        cost_estimate=pl.CostEstimate(flops=2 * 10**10, bytes_accessed=8 * height * wide, transcendentals=0),
    )(place, own, *earlier)


def nt_dot(a, b, precision=None):
    return lax.dot_general(
        a, b, (((1,), (1,)), ((), ())), precision=precision, preferred_element_type=jnp.float32
    )


def update_kernel(slots, order_ref, factor_ref, *refs):
    choices, (keep_ref, send_ref, pivots, sem) = refs[:-4], refs[-4:]
    slot = pl.program_id(0)
    for i, choice in enumerate(choices):

        @pl.when((slot == 0) & (order_ref[slots] == i))
        def _():
            copy = pltpu.make_async_copy(choice, pivots, sem)
            copy.start()
            copy.wait()

    product = nt_dot(factor_ref[...], pivots[...])

    @pl.when(slot < slots // 2)
    def _():
        keep_ref[...] = product

    @pl.when(slot >= slots // 2)
    def _():
        send_ref[...] = product


def update_product(factor, choices, which, col, ncol):
    rows, depth = factor.shape
    own, count = rows // ncol, choices[0].shape[0]
    half = ncol // 2
    flips = list(range(0, ncol, 2)) + list(range(1, ncol, 2))
    order = jnp.concatenate([col ^ jnp.asarray(flips, jnp.int32), which[None].astype(jnp.int32)])
    out = jax.ShapeDtypeStruct((half * own, count), jnp.float32)
    return pl.pallas_call(
        functools.partial(update_kernel, ncol),
        out_shape=(out, out),
        grid_spec=pltpu.PrefetchScalarGridSpec(
            num_scalar_prefetch=1,
            grid=(ncol,),
            in_specs=[pl.BlockSpec((own, depth), lambda s, order: (order[s], 0))]
            + [pl.BlockSpec(memory_space=pltpu.HBM)] * len(choices),
            out_specs=(
                pl.BlockSpec((own, count), lambda s, order: (jnp.minimum(s, half - 1), 0)),
                pl.BlockSpec((own, count), lambda s, order: (jnp.maximum(s - half, 0), 0)),
            ),
            scratch_shapes=[pltpu.VMEM((count, depth), factor.dtype), pltpu.SemaphoreType.DMA],
        ),
        compiler_params=pltpu.CompilerParams(vmem_limit_bytes=40 << 20),
        cost_estimate=pl.CostEstimate(
            flops=2 * rows * depth * count, bytes_accessed=2 * rows * depth + 4 * rows * count, transcendentals=0
        ),
    )(order, factor, *choices)


def stage_end(arrays):
    hbm = pl.BlockSpec(memory_space=pltpu.HBM)
    names = sorted(arrays)
    results = pl.pallas_call(
        lambda *refs: None,
        out_shape=[jax.ShapeDtypeStruct(arrays[n].shape, arrays[n].dtype) for n in names],
        in_specs=[hbm] * len(names),
        out_specs=[hbm] * len(names),
        input_output_aliases={i: i for i in range(len(names))},
    )(*[arrays[n] for n in names])
    return dict(zip(names, results))


def along_row(block, moves, ncol):
    return lax.ppermute(block, BOTH, [(a * ncol + c, b * ncol + c) for c in range(ncol) for a, b in moves[c % 2]])


def tree_step(step, block, buffers, row, odd, nrow, ncol):
    line = nrow // 2
    new = {}
    if step == 0:
        new["first"] = along_row(block, ([], [(0, 1)]), ncol)
    elif step == 1:
        held = jnp.where(odd == 1, buffers["first"], block)
        new["half"] = along_row(held, both_lines([(0, line // 2)]), ncol)
    elif step == 2:
        held, reach = buffers["half"], line // 4
        while reach:
            ahead = [(p, p + reach) for p in range(2 * reach, line, 2 * reach)]
            new["on%d" % reach] = along_row(held, both_lines(ahead), ncol)
            new["back%d" % reach] = along_row(held, both_lines([(2 * reach, reach)]), ncol)
            if reach > 1:
                place = row // 2
                held = jnp.where(place % (2 * reach) == reach, new["on%d" % reach], held)
                held = jnp.where(place == reach, new["back%d" % reach], held)
            reach //= 2
        if line > 4:
            names = ["own", "first", "half"] + sorted(new)
            arrived = dict(buffers, own=block, **new)
            which = which_buffer(names, row, odd, nrow)
            held = block
            for i, name in enumerate(names[1:]):
                held = jnp.where(which == i + 1, arrived[name], held)
            buffers.clear()
            new = {"line": held}
        new["near"] = along_row(block, ([(0, 1)], []), ncol)
    else:
        for name in sorted(buffers):
            if name not in ("first", "near"):
                moves = arrivals(name, line)
                even = [(2 * p, 2 * p + 1) for p in moves]
                odds = [(2 * p + 1, 2 * p) for p in moves]
                new["x" + name] = along_row(buffers[name], (even, odds), ncol)
    return new


def both_lines(moves):
    return [(2 * a, 2 * b) for a, b in moves], [(2 * a + 1, 2 * b + 1) for a, b in moves]


def arrivals(name, line):
    if name == "half":
        return [line // 2]
    if name == "line":
        return list(range(1, line))
    reach = int(name.strip("onback"))
    if name.startswith("on"):
        return [p + reach for p in range(2 * reach, line, 2 * reach)]
    return [reach]


def which_buffer(names, row, odd, nrow):
    line = nrow // 2
    place, on_odd = row // 2, row % 2
    which = jnp.zeros_like(row)
    for i, name in enumerate(names):
        if name == "own":
            hit = row == 0
        elif name in ("first", "line") and line > 4:
            hit = (on_odd == odd) & ((place > 0) if name == "line" else (place == 0) & (odd == 1))
            hit = hit | ((row == 1) & (odd == 1))
        elif name == "first":
            hit = (row == 1) & (odd == 1)
        elif name == "near":
            hit = (row == 1) & (odd == 0)
        else:
            crossed = name.startswith("x")
            hit = (on_odd != odd) if crossed else (on_odd == odd)
            at = jnp.zeros_like(hit)
            for p in arrivals(name[1:] if crossed else name, line):
                at = at | (place == p)
            hit = hit & at
        which = jnp.where(hit, i, which)
    return which


def along_col(block, bit, nrow, ncol):
    return lax.ppermute(block, BOTH, [(r * ncol + c, r * ncol + (c ^ bit)) for r in range(nrow) for c in range(ncol)])


def core_halves(block):
    half = block.shape[0] // 2
    low = lax.axis_index("col") % 2
    mine = lax.dynamic_slice_in_dim(block, low * half, half, 0)
    other = lax.dynamic_slice_in_dim(block, (1 - low) * half, half, 0)
    return mine, other


def join_cores(mine, nrow, ncol):
    other = along_col(mine, 1, nrow, ncol)
    low = lax.axis_index("col") % 2
    return jnp.where(low == 0, jnp.concatenate([mine, other], 0), jnp.concatenate([other, mine], 0))


def sum_between_chips(mine, nrow, ncol):
    bit = 2
    while bit < ncol:
        mine = mine + along_col(mine, bit, nrow, ncol)
        bit *= 2
    return mine


def scatter_sum(keep, send, nrow, ncol):
    keep = keep + along_col(send, 1, nrow, ncol)
    bit = ncol // 2
    while bit > 1:
        half = keep.shape[0] // 2
        keep = keep[:half] + along_col(keep[half:], bit, nrow, ncol)
        bit //= 2
    return keep


def to_rows(mine, step, row, nrow, ncol):
    moves = [(r, r + step) for r in range(0, nrow, 2 * step)]
    got = along_row(mine, (moves, moves), ncol)
    return jnp.where(row % (2 * step) == step, got, mine)


def join_all(mine, nrow, ncol):
    share, wide = mine.shape
    mine = mine[None]
    bit = ncol // 2
    while bit:
        other = along_col(mine, bit, nrow, ncol)
        low = (lax.axis_index("col") & bit) == 0
        pair = [jnp.where(low, mine, other), jnp.where(low, other, mine)]
        mine = jnp.stack(pair, 1).reshape(-1, share, wide)
        bit //= 2
    return mine.reshape(ncol * share, wide)


def own_part(panels, at, end):
    own = panels.shape[0]
    col = lax.axis_index("col")
    blocks = []
    for c in range(at // own, -(-end // own)):
        first, last = max(at, c * own), min(end, (c + 1) * own)
        blocks.append(jnp.where(col == c, panels[first - c * own : last - c * own, at:], 0.0))
    return jnp.concatenate(blocks, 0)


def on_device(nrow, ncol, factor, panels):
    own, width = panels.shape
    row, col = lax.axis_index("row"), lax.axis_index("col")
    odd = col % 2
    share = width // PARTS
    place = jnp.stack([row, col]).astype(jnp.int32)
    steps = []
    while nrow >> (len(steps) + 1):
        steps.append(nrow >> (len(steps) + 1))
    live = {"own%d" % i: factor[i * share : (i + 1) * share] for i in range(PARTS)}
    pivots = [{} for _ in range(PARTS)]
    fresh = [[] for _ in range(PARTS)]
    rest = [None] * PARTS

    def hops(number):
        for i in range(PARTS):
            if 0 <= number - i <= 3:
                new = tree_step(number - i, live["own%d" % i], pivots[i], row, odd, nrow, ncol)
                pivots[i].update(new)
                fresh[i] = list(new)
            else:
                fresh[i] = []

    def update(i):
        names = ["own"] + sorted(pivots[i])
        choices = [live["own%d" % i]] + [pivots[i][n] for n in names[1:]]
        which = which_buffer(names, row, odd, nrow)
        keep, send = update_product(factor, choices, which, col, ncol)
        rest[i] = panels[:, i * share : (i + 1) * share] - scatter_sum(keep, send, nrow, ncol)

    def end(extra, number):
        named = dict(extra)
        for i in range(PARTS):
            if i == number + 1:
                named["own%d" % i] = live["own%d" % i]
            for n in fresh[i]:
                named["%s of %d" % (n, i)] = pivots[i][n]
        named = stage_end(named)
        for i in range(PARTS):
            if i == number + 1:
                live["own%d" % i] = named["own%d" % i]
            for n in fresh[i]:
                pivots[i][n] = named["%s of %d" % (n, i)]
        return {n: named[n] for n in extra}

    hops(0)
    tops = []
    for i in range(PARTS):
        at = i * share
        piece = own_part(panels, at, at + share) - nt_dot(factor[at : at + share], factor[at:width])
        mine, other = core_halves(piece)
        tops.append(mine + along_col(other, 1, nrow, ncol))
    tops[0] = sum_between_chips(tops[0], nrow, ncol)
    tops = end({"top0": tops[0], "top1": tops[1]}, 0)
    hops(1)
    pack0, mine0 = panel_factor(place, ncol, join_cores(tops["top0"], nrow, ncol), [])
    top1 = sum_between_chips(tops["top1"], nrow, ncol)
    kept = end({"pack0": pack0, "mine0": mine0, "top1": top1}, 1)
    hops(2)
    mine0 = to_rows(kept["mine0"], steps[0], row, nrow, ncol)
    pack1, mine1 = panel_factor(place, ncol, join_cores(kept["top1"], nrow, ncol), [kept["pack0"]])
    kept = end({"mine0": mine0, "mine1": mine1}, 2)
    hops(3)
    mine0, mine1 = kept["mine0"], to_rows(kept["mine1"], steps[0], row, nrow, ncol)
    for step in steps[1:]:
        mine0 = to_rows(mine0, step, row, nrow, ncol)
    kept = end({"mine0": mine0, "mine1": mine1}, 3)
    hops(4)
    update(0)
    pack0, mine1 = join_all(kept["mine0"], nrow, ncol), kept["mine1"]
    for step in steps[1:]:
        mine1 = to_rows(mine1, step, row, nrow, ncol)
    kept = end({"pack0": pack0, "mine1": mine1, "rest0": rest[0]}, 4)
    rest[0] = kept["rest0"]
    update(1)
    spread = [kept["pack0"], join_all(kept["mine1"], nrow, ncol)]
    rest = jnp.concatenate(rest, 1)
    out = []
    for pack in spread:
        solved = nt_dot(rest[:, :share], pack[:, :share], HIGH)
        rest = rest[:, share:] - jnp.dot(solved, pack[:, share:], precision=HIGH)
        out.append(solved)
    out = jnp.concatenate(out, 1)
    at_row = lax.broadcasted_iota(jnp.int32, out.shape, 0) + (row * ncol + col) * own
    at_col = lax.broadcasted_iota(jnp.int32, out.shape, 1)
    return jnp.where(at_col <= at_row, out, 0.0)


def solution(mesh):
    return jax.shard_map(
        functools.partial(on_device, mesh.shape["row"], mesh.shape["col"]),
        mesh=mesh,
        in_specs=(P("row", "col"), P(BOTH, None)),
        out_specs=P(BOTH, None),
        check_vma=False,
    )
```

```python
import functools
import jax
import jax.numpy as jnp
from jax import lax
from jax.experimental import pallas as pl
from jax.experimental.pallas import tpu as pltpu
from jax.sharding import PartitionSpec as P

SUB = 8
BLOCK = 128
STEP = 32
PARTS = 2
BOTH = ("row", "col")
HIGH = lax.Precision.HIGHEST


def tn_dot(a, b):
    return lax.dot_general(a, b, (((0,), (0,)), ((), ())), precision=HIGH, preferred_element_type=jnp.float32)


def nn_dot(a, b):
    return lax.dot_general(a, b, (((1,), (0,)), ((), ())), precision=HIGH, preferred_element_type=jnp.float32)


def row_of(x, k):
    return jnp.broadcast_to(x[k : k + 1, :], x.shape)


def lane_of(x, k):
    return jnp.broadcast_to(x[:, k : k + 1], x.shape)


def inverse_factor(block):
    lane = lax.broadcasted_iota(jnp.int32, (SUB, BLOCK), 1)
    sub = lax.broadcasted_iota(jnp.int32, (SUB, BLOCK), 0)
    groups = [block[SUB * q : SUB * (q + 1), :] for q in range(BLOCK // SUB)]
    per_step = STEP // SUB
    done = []
    for step in range(BLOCK // STEP):
        end = (step + 1) * per_step
        here = []
        for p in range(step * per_step, end):
            first = SUB * p
            inside = (lane >= first) & (lane < first + SUB)
            cols = [lane_of(groups[p], first + k) for k in range(SUB)]
            rows = jnp.where(inside, jnp.where(lane - first == sub, 1.0, 0.0), groups[p])
            scale = jnp.zeros((SUB, BLOCK), jnp.float32)
            col_rows, own_rows = [], []
            for k in range(SUB):
                pivot = row_of(cols[k], k)
                inv = pl.reciprocal(pivot, approx=True)
                scale = jnp.where(sub == k, lax.rsqrt(pivot), scale)
                below = jnp.where(sub > k, cols[k], 0.0)
                raw = [row_of(cols[m], k) for m in range(k + 1, SUB)]
                own = row_of(rows, k) * inv
                for i, m in enumerate(range(k + 1, SUB)):
                    cols[m] = cols[m] - (below * raw[i]) * inv
                rows = rows - below * own
                col_rows.append([r * inv for r in raw])
                own_rows.append(own)
            here.append(rows * scale)
            for q in range(p + 1, end):
                mult = [lane_of(groups[q], first + k) for k in range(SUB)]
                acc = jnp.where(inside, 0.0, groups[q])
                for k in range(SUB):
                    for i, m in enumerate(range(k + 1, SUB)):
                        mult[m] = mult[m] - mult[k] * col_rows[k][i]
                    acc = acc - mult[k] * own_rows[k]
                groups[q] = acc
        span = jnp.concatenate(here, 0)
        base = step * STEP
        span_lane = lax.broadcasted_iota(jnp.int32, (STEP, BLOCK), 1)
        span_row = lax.broadcasted_iota(jnp.int32, (STEP, BLOCK), 0) + base
        span = jnp.where((span_lane <= span_row) | (span_lane >= base + STEP), span, 0.0)
        done.append(jnp.where(span_lane <= span_row, span, 0.0))
        if base + STEP < BLOCK:
            delta = tn_dot(span, span)
            in_step = (lane >= base) & (lane < base + STEP)
            for q in range(end, BLOCK // SUB):
                groups[q] = jnp.where(in_step, 0.0, groups[q]) - delta[SUB * q : SUB * (q + 1), :]
    return jnp.concatenate(done, 0)


def factor_panel(height, skips, own_ref, earlier, out_ref):
    rest = own_ref[...]
    for ref, skip in zip(earlier, skips):
        span = ref[:, skip:]
        rest = rest - tn_dot(span[:, :height], span)
    out_ref[...] = jnp.zeros_like(out_ref)
    uppers, inverses = [], []
    for i in range(height // BLOCK):
        at = i * BLOCK
        inverse = inverse_factor(rest[:BLOCK, :BLOCK])
        if rest.shape[1] > BLOCK:
            upper = nn_dot(inverse, rest[:BLOCK, BLOCK:])
        line = []
        for j in range(i):
            total = 0.0
            for k in range(j, i):
                block = uppers[k][:, (i - k - 1) * BLOCK : (i - k) * BLOCK]
                total = total + tn_dot(block, inverses[k][j])
            line.append(-nn_dot(inverse, total))
        line.append(inverse)
        inverses.append(line)
        for j, block in enumerate(line):
            out_ref[at : at + BLOCK, j * BLOCK : (j + 1) * BLOCK] = block
        if rest.shape[1] > BLOCK:
            uppers.append(upper)
            left = height - at - BLOCK
            if upper.shape[1] > left:
                out_ref[at : at + BLOCK, height:] = upper[:, left:]
            if left:
                rest = rest[BLOCK:, BLOCK:] - tn_dot(upper[:, :left], upper)


def panel_kernel(height, skips, place_ref, own_ref, *refs):
    earlier, out_ref, share_ref = refs[: len(skips)], refs[-2], refs[-1]
    share = share_ref.shape[0]

    @pl.when(place_ref[0] == 0)
    def _():
        factor_panel(height, skips, own_ref, earlier, out_ref)
        share_ref[...] = out_ref[pl.ds(pl.multiple_of(place_ref[1] * share, share), share), :]


def panel_factor(place, ncol, own, earlier):
    height, wide = own.shape
    skips = [(len(earlier) - p) * height for p in range(len(earlier))]
    vmem = pl.BlockSpec(memory_space=pltpu.VMEM)
    return pl.pallas_call(
        functools.partial(panel_kernel, height, skips),
        out_shape=[jax.ShapeDtypeStruct((h, wide), jnp.float32) for h in (height, height // ncol)],
        in_specs=[pl.BlockSpec(memory_space=pltpu.SMEM)] + [vmem] * (1 + len(earlier)),
        out_specs=[vmem, vmem],
        compiler_params=pltpu.CompilerParams(vmem_limit_bytes=40 << 20),
        cost_estimate=pl.CostEstimate(flops=2 * 10**10, bytes_accessed=8 * height * wide, transcendentals=0),
    )(place, own, *earlier)


def nt_dot(a, b, precision=None):
    return lax.dot_general(
        a, b, (((1,), (1,)), ((), ())), precision=precision, preferred_element_type=jnp.float32
    )


def update_kernel(slots, count, order_ref, factor_ref, *refs):
    choices, (keep_ref, send_ref, pivots, sem) = refs[:count], refs[-4:]
    slot = pl.program_id(0)
    for i, choice in enumerate(choices):

        @pl.when((slot == 0) & (order_ref[slots] == i))
        def _():
            copy = pltpu.make_async_copy(choice, pivots, sem)
            copy.start()
            copy.wait()

    product = nt_dot(factor_ref[...], pivots[...])

    @pl.when(slot < slots // 2)
    def _():
        keep_ref[...] = product

    @pl.when(slot >= slots // 2)
    def _():
        send_ref[...] = product


def update_product(factor, choices, which, col, ncol, after):
    rows, depth = factor.shape
    own, count = rows // ncol, choices[0].shape[0]
    half = ncol // 2
    flips = list(range(0, ncol, 2)) + list(range(1, ncol, 2))
    order = jnp.concatenate([col ^ jnp.asarray(flips, jnp.int32), which[None].astype(jnp.int32)])
    out = jax.ShapeDtypeStruct((half * own, count), jnp.float32)
    return pl.pallas_call(
        functools.partial(update_kernel, ncol, len(choices)),
        out_shape=(out, out),
        grid_spec=pltpu.PrefetchScalarGridSpec(
            num_scalar_prefetch=1,
            grid=(ncol,),
            in_specs=[pl.BlockSpec((own, depth), lambda s, order: (order[s], 0))]
            + [pl.BlockSpec(memory_space=pltpu.HBM)] * (len(choices) + len(after)),
            out_specs=(
                pl.BlockSpec((own, count), lambda s, order: (jnp.minimum(s, half - 1), 0)),
                pl.BlockSpec((own, count), lambda s, order: (jnp.maximum(s - half, 0), 0)),
            ),
            scratch_shapes=[pltpu.VMEM((count, depth), factor.dtype), pltpu.SemaphoreType.DMA],
        ),
        compiler_params=pltpu.CompilerParams(vmem_limit_bytes=40 << 20),
        cost_estimate=pl.CostEstimate(
            flops=2 * rows * depth * count, bytes_accessed=2 * rows * depth + 4 * rows * count, transcendentals=0
        ),
    )(order, factor, *choices, *after)


def stage_end(arrays):
    hbm = pl.BlockSpec(memory_space=pltpu.HBM)
    names = sorted(arrays)
    results = pl.pallas_call(
        lambda *refs: None,
        out_shape=[jax.ShapeDtypeStruct(arrays[n].shape, arrays[n].dtype) for n in names],
        in_specs=[hbm] * len(names),
        out_specs=[hbm] * len(names),
        input_output_aliases={i: i for i in range(len(names))},
    )(*[arrays[n] for n in names])
    return dict(zip(names, results))


def along_row(block, moves, ncol):
    return lax.ppermute(block, BOTH, [(a * ncol + c, b * ncol + c) for c in range(ncol) for a, b in moves[c % 2]])


def tree_step(step, block, buffers, row, odd, nrow, ncol):
    line = nrow // 2
    new = {}
    if step == 0:
        new["first"] = along_row(block, ([], [(0, 1)]), ncol)
    elif step == 1:
        held = jnp.where(odd == 1, buffers["first"], block)
        new["half"] = along_row(held, both_lines([(0, line // 2)]), ncol)
    elif step == 2:
        held, reach = buffers["half"], line // 4
        while reach:
            ahead = [(p, p + reach) for p in range(2 * reach, line, 2 * reach)]
            new["on%d" % reach] = along_row(held, both_lines(ahead), ncol)
            new["back%d" % reach] = along_row(held, both_lines([(2 * reach, reach)]), ncol)
            if reach > 1:
                place = row // 2
                held = jnp.where(place % (2 * reach) == reach, new["on%d" % reach], held)
                held = jnp.where(place == reach, new["back%d" % reach], held)
            reach //= 2
    else:
        held, place = block, row // 2
        for name in sorted(buffers):
            for p in arrivals(name, line):
                held = jnp.where((row == 1) if name == "first" else (place == p), buffers[name], held)
        buffers.clear()
        new["line"] = held
        even = [(2 * p, 2 * p + 1) for p in range(line)]
        odds = [(2 * p + 1, 2 * p) for p in range(1, line)]
        new["across"] = along_row(held, (even, odds), ncol)
    return new


def both_lines(moves):
    return [(2 * a, 2 * b) for a, b in moves], [(2 * a + 1, 2 * b + 1) for a, b in moves]


def arrivals(name, line):
    if name == "first":
        return [0]
    if name == "half":
        return [line // 2]
    reach = int(name.strip("onback"))
    if name.startswith("on"):
        return [p + reach for p in range(2 * reach, line, 2 * reach)]
    return [reach]


def along_col(block, bit, nrow, ncol):
    return lax.ppermute(block, BOTH, [(r * ncol + c, r * ncol + (c ^ bit)) for r in range(nrow) for c in range(ncol)])


def core_halves(block):
    half = block.shape[0] // 2
    low = lax.axis_index("col") % 2
    mine = lax.dynamic_slice_in_dim(block, low * half, half, 0)
    other = lax.dynamic_slice_in_dim(block, (1 - low) * half, half, 0)
    return mine, other


def join_cores(mine, nrow, ncol):
    other = along_col(mine, 1, nrow, ncol)
    low = lax.axis_index("col") % 2
    return jnp.where(low == 0, jnp.concatenate([mine, other], 0), jnp.concatenate([other, mine], 0))


def sum_between_chips(mine, nrow, ncol):
    bit = 2
    while bit < ncol:
        mine = mine + along_col(mine, bit, nrow, ncol)
        bit *= 2
    return mine


def scatter_sum(keep, send, nrow, ncol):
    keep = keep + along_col(send, 1, nrow, ncol)
    bit = ncol // 2
    while bit > 1:
        half = keep.shape[0] // 2
        keep = keep[:half] + along_col(keep[half:], bit, nrow, ncol)
        bit //= 2
    return keep


def to_rows(mine, step, nrow, ncol):
    moves = [(r, r + step) for r in range(0, nrow, 2 * step)]
    return along_row(mine, (moves, moves), ncol)


def received(mine, got, step, row):
    return jnp.where(row % (2 * step) == step, got, mine)


def join_all(mine, nrow, ncol):
    share, wide = mine.shape
    mine = mine[None]
    bit = ncol // 2
    while bit:
        other = along_col(mine, bit, nrow, ncol)
        low = (lax.axis_index("col") & bit) == 0
        pair = [jnp.where(low, mine, other), jnp.where(low, other, mine)]
        mine = jnp.stack(pair, 1).reshape(-1, share, wide)
        bit //= 2
    return mine.reshape(ncol * share, wide)


def own_part(panels, at, end):
    own = panels.shape[0]
    col = lax.axis_index("col")
    blocks = []
    for c in range(at // own, -(-end // own)):
        first, last = max(at, c * own), min(end, (c + 1) * own)
        blocks.append(jnp.where(col == c, panels[first - c * own : last - c * own, at:], 0.0))
    return jnp.concatenate(blocks, 0)


def on_device(nrow, ncol, factor, panels):
    own, width = panels.shape
    row, col = lax.axis_index("row"), lax.axis_index("col")
    odd = col % 2
    share = width // PARTS
    place = jnp.stack([row, col]).astype(jnp.int32)
    steps = []
    while nrow >> (len(steps) + 1):
        steps.append(nrow >> (len(steps) + 1))
    live = {"own%d" % i: factor[i * share : (i + 1) * share] for i in range(PARTS)}
    pivots = [{} for _ in range(PARTS)]
    fresh = [[] for _ in range(PARTS)]
    rest = [None] * PARTS

    def hops(number):
        for i in range(PARTS):
            if 0 <= number - i <= 3:
                new = tree_step(number - i, live["own%d" % i], pivots[i], row, odd, nrow, ncol)
                pivots[i].update(new)
                fresh[i] = list(new)
            else:
                fresh[i] = []

    def update(i, after):
        across = (row > 0) & (row % 2 != odd)
        choices = [pivots[i]["line"], pivots[i]["across"]]
        keep, send = update_product(factor, choices, across, col, ncol, after)
        rest[i] = panels[:, i * share : (i + 1) * share] - scatter_sum(keep, send, nrow, ncol)

    def end(extra, number):
        named = dict(extra)
        for i in range(PARTS):
            if i == number + 1:
                named["own%d" % i] = live["own%d" % i]
            for n in fresh[i]:
                named["%s of %d" % (n, i)] = pivots[i][n]
        named = stage_end(named)
        for i in range(PARTS):
            if i == number + 1:
                live["own%d" % i] = named["own%d" % i]
            for n in fresh[i]:
                pivots[i][n] = named["%s of %d" % (n, i)]
        return {n: named[n] for n in extra}

    hops(0)
    tops = []
    for i in range(PARTS):
        at = i * share
        piece = own_part(panels, at, at + share) - nt_dot(factor[at : at + share], factor[at:width])
        mine, other = core_halves(piece)
        tops.append(mine + along_col(other, 1, nrow, ncol))
    tops = [sum_between_chips(top, nrow, ncol) for top in tops]
    tops = end({"top0": tops[0], "top1": tops[1]}, 0)
    hops(1)
    pack0, mine0 = panel_factor(place, ncol, join_cores(tops["top0"], nrow, ncol), [])
    kept = end({"pack0": pack0, "mine0": mine0, "top1": tops["top1"]}, 1)
    hops(2)
    got0 = to_rows(kept["mine0"], steps[0], nrow, ncol)
    pack1, mine1 = panel_factor(place, ncol, join_cores(kept["top1"], nrow, ncol), [kept["pack0"]])
    kept = end({"mine0": kept["mine0"], "got0": got0, "mine1": mine1}, 2)
    hops(3)
    mine0, mine1 = received(kept["mine0"], kept["got0"], steps[0], row), kept["mine1"]
    got1 = to_rows(mine1, steps[0], nrow, ncol)
    for step in steps[1:-1]:
        mine0 = received(mine0, to_rows(mine0, step, nrow, ncol), step, row)
    got0 = to_rows(mine0, steps[-1], nrow, ncol)
    kept = end({"mine0": mine0, "got0": got0, "mine1": mine1, "got1": got1}, 3)
    hops(4)
    update(0, [pivots[1]["line"]])
    pack0 = join_all(received(kept["mine0"], kept["got0"], steps[-1], row), nrow, ncol)
    mine1 = received(kept["mine1"], kept["got1"], steps[0], row)
    for step in steps[1:]:
        mine1 = received(mine1, to_rows(mine1, step, nrow, ncol), step, row)
    kept = end({"pack0": pack0, "mine1": mine1, "rest0": rest[0]}, 4)
    rest[0] = kept["rest0"]
    update(1, [])
    spread = [kept["pack0"], join_all(kept["mine1"], nrow, ncol)]
    rest = jnp.concatenate(rest, 1)
    out = []
    for pack in spread:
        solved = nt_dot(rest[:, :share], pack[:, :share], HIGH)
        rest = rest[:, share:] - jnp.dot(solved, pack[:, share:], precision=HIGH)
        out.append(solved)
    out = jnp.concatenate(out, 1)
    at_row = lax.broadcasted_iota(jnp.int32, out.shape, 0) + (row * ncol + col) * own
    at_col = lax.broadcasted_iota(jnp.int32, out.shape, 1)
    return jnp.where(at_col <= at_row, out, 0.0)


def solution(mesh):
    return jax.shard_map(
        functools.partial(on_device, mesh.shape["row"], mesh.shape["col"]),
        mesh=mesh,
        in_specs=(P("row", "col"), P(BOTH, None)),
        out_specs=P(BOTH, None),
        check_vma=False,
    )
```

```python
import functools
import jax
import jax.numpy as jnp
from jax import lax
from jax.experimental import pallas as pl
from jax.experimental.pallas import tpu as pltpu
from jax.sharding import PartitionSpec as P

SUB = 8
BLOCK = 128
STEP = 32
PARTS = 2
BOTH = ("row", "col")
HIGH = lax.Precision.HIGHEST


def tn_dot(a, b):
    return lax.dot_general(a, b, (((0,), (0,)), ((), ())), precision=HIGH, preferred_element_type=jnp.float32)


def nn_dot(a, b):
    return lax.dot_general(a, b, (((1,), (0,)), ((), ())), precision=HIGH, preferred_element_type=jnp.float32)


def row_of(x, k):
    return jnp.broadcast_to(x[k : k + 1, :], x.shape)


def lane_of(x, k):
    return jnp.broadcast_to(x[:, k : k + 1], x.shape)


def inverse_factor(block):
    lane = lax.broadcasted_iota(jnp.int32, (SUB, BLOCK), 1)
    sub = lax.broadcasted_iota(jnp.int32, (SUB, BLOCK), 0)
    groups = [block[SUB * q : SUB * (q + 1), :] for q in range(BLOCK // SUB)]
    per_step = STEP // SUB
    done = []
    for step in range(BLOCK // STEP):
        end = (step + 1) * per_step
        here = []
        for p in range(step * per_step, end):
            first = SUB * p
            inside = (lane >= first) & (lane < first + SUB)
            cols = [lane_of(groups[p], first + k) for k in range(SUB)]
            rows = jnp.where(inside, jnp.where(lane - first == sub, 1.0, 0.0), groups[p])
            scale = jnp.zeros((SUB, BLOCK), jnp.float32)
            col_rows, own_rows = [], []
            for k in range(SUB):
                pivot = row_of(cols[k], k)
                inv = pl.reciprocal(pivot, approx=True)
                scale = jnp.where(sub == k, lax.rsqrt(pivot), scale)
                below = jnp.where(sub > k, cols[k], 0.0)
                raw = [row_of(cols[m], k) for m in range(k + 1, SUB)]
                own = row_of(rows, k) * inv
                for i, m in enumerate(range(k + 1, SUB)):
                    cols[m] = cols[m] - (below * raw[i]) * inv
                rows = rows - below * own
                col_rows.append([r * inv for r in raw])
                own_rows.append(own)
            here.append(rows * scale)
            for q in range(p + 1, end):
                mult = [lane_of(groups[q], first + k) for k in range(SUB)]
                acc = jnp.where(inside, 0.0, groups[q])
                for k in range(SUB):
                    for i, m in enumerate(range(k + 1, SUB)):
                        mult[m] = mult[m] - mult[k] * col_rows[k][i]
                    acc = acc - mult[k] * own_rows[k]
                groups[q] = acc
        span = jnp.concatenate(here, 0)
        base = step * STEP
        span_lane = lax.broadcasted_iota(jnp.int32, (STEP, BLOCK), 1)
        span_row = lax.broadcasted_iota(jnp.int32, (STEP, BLOCK), 0) + base
        span = jnp.where((span_lane <= span_row) | (span_lane >= base + STEP), span, 0.0)
        done.append(jnp.where(span_lane <= span_row, span, 0.0))
        if base + STEP < BLOCK:
            delta = tn_dot(span, span)
            in_step = (lane >= base) & (lane < base + STEP)
            for q in range(end, BLOCK // SUB):
                groups[q] = jnp.where(in_step, 0.0, groups[q]) - delta[SUB * q : SUB * (q + 1), :]
    return jnp.concatenate(done, 0)


def inverse_panel(rest, out_ref, first):
    size = rest.shape[0]
    uppers, inverses = [], []
    for i in range(size // BLOCK):
        at = i * BLOCK
        inverse = inverse_factor(rest[:BLOCK, :BLOCK])
        line = []
        for j in range(i):
            total = 0.0
            for k in range(j, i):
                block = uppers[k][:, (i - k - 1) * BLOCK : (i - k) * BLOCK]
                total = total + tn_dot(block, inverses[k][j])
            line.append(-nn_dot(inverse, total))
        line.append(inverse)
        inverses.append(line)
        for j, block in enumerate(line):
            out_ref[at : at + BLOCK, first + j * BLOCK : first + (j + 1) * BLOCK] = block
        if at + BLOCK < size:
            out_ref[at : at + BLOCK, first + at + BLOCK : first + size] = jnp.zeros(
                (BLOCK, size - at - BLOCK), jnp.float32
            )
            uppers.append(nn_dot(inverse, rest[:BLOCK, BLOCK:]))
            rest = rest[BLOCK:, BLOCK:] - tn_dot(uppers[-1], uppers[-1])


def panel_kernel(place_ref, mine_ref, other_ref, *refs):
    earlier, (out_ref, share_ref, whole) = refs[:-3], refs[-3:]
    size, share, half = out_ref.shape[0], share_ref.shape[0], mine_ref.shape[0]

    @pl.when(place_ref[0] == 0)
    def _():
        low = place_ref[1] % 2
        whole[pl.ds(pl.multiple_of(low * half, half), half), :] = mine_ref[...]
        whole[pl.ds(pl.multiple_of((1 - low) * half, half), half), :] = other_ref[...]
        if earlier:
            upper = nn_dot(earlier[0][...], whole[:, :size])
            out_ref[:, :size] = upper
            inverse_panel(whole[:, size:] - tn_dot(upper, upper), out_ref, size)
        else:
            inverse_panel(whole[...], out_ref, 0)
        share_ref[...] = out_ref[pl.ds(pl.multiple_of(place_ref[1] * share, share), share), :]


def panel_factor(place, ncol, mine, other, earlier):
    half, wide = mine.shape
    size = 2 * half
    vmem = pl.BlockSpec(memory_space=pltpu.VMEM)
    return pl.pallas_call(
        panel_kernel,
        out_shape=[jax.ShapeDtypeStruct((h, wide), jnp.float32) for h in (size, size // ncol)],
        in_specs=[pl.BlockSpec(memory_space=pltpu.SMEM)] + [vmem] * (2 + len(earlier)),
        out_specs=[vmem, vmem],
        scratch_shapes=[pltpu.VMEM((size, wide), jnp.float32)],
        compiler_params=pltpu.CompilerParams(vmem_limit_bytes=40 << 20),
        cost_estimate=pl.CostEstimate(flops=2 * 10**10, bytes_accessed=8 * size * wide, transcendentals=0),
    )(place, mine, other, *earlier)


def nt_dot(a, b, precision=None):
    return lax.dot_general(
        a, b, (((1,), (1,)), ((), ())), precision=precision, preferred_element_type=jnp.float32
    )


def update_kernel(slots, count, order_ref, factor_ref, *refs):
    choices, (keep_ref, send_ref, pivots, sem) = refs[:count], refs[-4:]
    slot = pl.program_id(0)
    for i, choice in enumerate(choices):

        @pl.when((slot == 0) & (order_ref[slots] == i))
        def _():
            copy = pltpu.make_async_copy(choice, pivots, sem)
            copy.start()
            copy.wait()

    product = nt_dot(factor_ref[...], pivots[...])

    @pl.when(slot < slots // 2)
    def _():
        keep_ref[...] = product

    @pl.when(slot >= slots // 2)
    def _():
        send_ref[...] = product


def update_product(factor, choices, which, col, ncol, after):
    rows, depth = factor.shape
    own, count = rows // ncol, choices[0].shape[0]
    half = ncol // 2
    flips = list(range(0, ncol, 2)) + list(range(1, ncol, 2))
    order = jnp.concatenate([col ^ jnp.asarray(flips, jnp.int32), which[None].astype(jnp.int32)])
    out = jax.ShapeDtypeStruct((half * own, count), jnp.float32)
    return pl.pallas_call(
        functools.partial(update_kernel, ncol, len(choices)),
        out_shape=(out, out),
        grid_spec=pltpu.PrefetchScalarGridSpec(
            num_scalar_prefetch=1,
            grid=(ncol,),
            in_specs=[pl.BlockSpec((own, depth), lambda s, order: (order[s], 0))]
            + [pl.BlockSpec(memory_space=pltpu.HBM)] * (len(choices) + len(after)),
            out_specs=(
                pl.BlockSpec((own, count), lambda s, order: (jnp.minimum(s, half - 1), 0)),
                pl.BlockSpec((own, count), lambda s, order: (jnp.maximum(s - half, 0), 0)),
            ),
            scratch_shapes=[pltpu.VMEM((count, depth), factor.dtype), pltpu.SemaphoreType.DMA],
        ),
        compiler_params=pltpu.CompilerParams(vmem_limit_bytes=40 << 20),
        cost_estimate=pl.CostEstimate(
            flops=2 * rows * depth * count, bytes_accessed=2 * rows * depth + 4 * rows * count, transcendentals=0
        ),
    )(order, factor, *choices, *after)


def stage_end(arrays):
    hbm = pl.BlockSpec(memory_space=pltpu.HBM)
    names = sorted(arrays)
    results = pl.pallas_call(
        lambda *refs: None,
        out_shape=[jax.ShapeDtypeStruct(arrays[n].shape, arrays[n].dtype) for n in names],
        in_specs=[hbm] * len(names),
        out_specs=[hbm] * len(names),
        input_output_aliases={i: i for i in range(len(names))},
    )(*[arrays[n] for n in names])
    return dict(zip(names, results))


def along_row(block, moves, ncol):
    return lax.ppermute(block, BOTH, [(a * ncol + c, b * ncol + c) for c in range(ncol) for a, b in moves[c % 2]])


def tree_step(step, block, buffers, row, odd, nrow, ncol):
    line = nrow // 2
    new = {}
    if step == 0:
        new["first"] = along_row(block, ([], [(0, 1)]), ncol)
    elif step == 1:
        held = jnp.where(odd == 1, buffers["first"], block)
        new["half"] = along_row(held, both_lines([(0, line // 2)]), ncol)
    elif step == 2:
        held, reach = buffers["half"], line // 4
        while reach:
            ahead = [(p, p + reach) for p in range(2 * reach, line, 2 * reach)]
            new["on%d" % reach] = along_row(held, both_lines(ahead), ncol)
            new["back%d" % reach] = along_row(held, both_lines([(2 * reach, reach)]), ncol)
            if reach > 1:
                place = row // 2
                held = jnp.where(place % (2 * reach) == reach, new["on%d" % reach], held)
                held = jnp.where(place == reach, new["back%d" % reach], held)
            reach //= 2
    else:
        held, place = block, row // 2
        for name in sorted(buffers):
            for p in arrivals(name, line):
                held = jnp.where((row == 1) if name == "first" else (place == p), buffers[name], held)
        buffers.clear()
        new["line"] = held
        even = [(2 * p, 2 * p + 1) for p in range(line)]
        odds = [(2 * p + 1, 2 * p) for p in range(1, line)]
        new["across"] = along_row(held, (even, odds), ncol)
    return new


def both_lines(moves):
    return [(2 * a, 2 * b) for a, b in moves], [(2 * a + 1, 2 * b + 1) for a, b in moves]


def arrivals(name, line):
    if name == "first":
        return [0]
    if name == "half":
        return [line // 2]
    reach = int(name.strip("onback"))
    if name.startswith("on"):
        return [p + reach for p in range(2 * reach, line, 2 * reach)]
    return [reach]


def along_col(block, bit, nrow, ncol):
    return lax.ppermute(block, BOTH, [(r * ncol + c, r * ncol + (c ^ bit)) for r in range(nrow) for c in range(ncol)])


def core_halves(block):
    half = block.shape[0] // 2
    low = lax.axis_index("col") % 2
    mine = lax.dynamic_slice_in_dim(block, low * half, half, 0)
    other = lax.dynamic_slice_in_dim(block, (1 - low) * half, half, 0)
    return mine, other


def sum_between_chips(mine, nrow, ncol):
    bit = 2
    while bit < ncol:
        mine = mine + along_col(mine, bit, nrow, ncol)
        bit *= 2
    return mine


def scatter_between_chips(keep, nrow, ncol):
    bit = ncol // 2
    while bit > 1:
        half = keep.shape[0] // 2
        keep = keep[:half] + along_col(keep[half:], bit, nrow, ncol)
        bit //= 2
    return keep


def to_rows(mine, step, nrow, ncol):
    moves = [(r, r + step) for r in range(0, nrow, 2 * step)]
    return along_row(mine, (moves, moves), ncol)


def received(mine, got, step, row):
    return jnp.where(row % (2 * step) == step, got, mine)


def join(mine, bits, nrow, ncol):
    share, wide = mine.shape[-2:]
    mine = mine.reshape(-1, share, wide)
    for bit in bits:
        other = along_col(mine, bit, nrow, ncol)
        low = (lax.axis_index("col") & bit) == 0
        pair = [jnp.where(low, mine, other), jnp.where(low, other, mine)]
        mine = jnp.stack(pair, 1).reshape(-1, share, wide)
    return mine


def own_part(panels, at, end, first, last):
    own = panels.shape[0]
    col = lax.axis_index("col")
    blocks = []
    for c in range(at // own, -(-end // own)):
        low, high = max(at, c * own), min(end, (c + 1) * own)
        blocks.append(jnp.where(col == c, panels[low - c * own : high - c * own, first:last], 0.0))
    return jnp.concatenate(blocks, 0)


def on_device(nrow, ncol, factor, panels):
    own, width = panels.shape
    row, col = lax.axis_index("row"), lax.axis_index("col")
    odd = col % 2
    share = width // PARTS
    place = jnp.stack([row, col]).astype(jnp.int32)
    steps = []
    while nrow >> (len(steps) + 1):
        steps.append(nrow >> (len(steps) + 1))
    live = {"own%d" % i: factor[i * share : (i + 1) * share] for i in range(PARTS)}
    pivots = [{} for _ in range(PARTS)]
    fresh = [[] for _ in range(PARTS)]

    def hops(number):
        for i in range(PARTS):
            if 0 <= number - i <= 3:
                new = tree_step(number - i, live["own%d" % i], pivots[i], row, odd, nrow, ncol)
                pivots[i].update(new)
                fresh[i] = list(new)
            else:
                fresh[i] = []

    def update(i, after):
        across = (row > 0) & (row % 2 != odd)
        choices = [pivots[i]["line"], pivots[i]["across"]]
        return update_product(factor, choices, across, col, ncol, after)

    def own_rest(i, keep):
        return panels[:, i * share : (i + 1) * share] - scatter_between_chips(keep, nrow, ncol)

    def top(at, first):
        block = factor[at : at + share], factor[first : first + share]
        return own_part(panels, at, at + share, first, first + share) - nt_dot(*block)

    chip_bits = [ncol >> (k + 1) for k in range(len(bin(ncol)) - 4)]

    def end(extra, number):
        named = dict(extra)
        for i in range(PARTS):
            if i == number + 1:
                named["own%d" % i] = live["own%d" % i]
            for n in fresh[i]:
                named["%s of %d" % (n, i)] = pivots[i][n]
        named = stage_end(named)
        for i in range(PARTS):
            if i == number + 1:
                live["own%d" % i] = named["own%d" % i]
            for n in fresh[i]:
                pivots[i][n] = named["%s of %d" % (n, i)]
        return {n: named[n] for n in extra}

    hops(0)
    mine, other = core_halves(top(0, 0))
    sum_a = sum_between_chips(mine + along_col(other, 1, nrow, ncol), nrow, ncol)
    mine, other = core_halves(jnp.concatenate([top(0, share), top(share, share)], 1))
    sum_b = mine + along_col(other, 1, nrow, ncol)
    kept = end({"a": sum_a, "b": sum_b}, 0)
    hops(1)
    sum_a, sum_b = kept["a"], sum_between_chips(kept["b"], nrow, ncol)
    pack_a, share_a = panel_factor(place, ncol, sum_a, along_col(sum_a, 1, nrow, ncol), [])
    kept = end({"b": sum_b, "share": share_a}, 1)
    hops(2)
    sum_b, share_a = kept["b"], kept["share"]
    got_a = to_rows(share_a, steps[0], nrow, ncol)
    pack_b, share_b = panel_factor(place, ncol, sum_b, along_col(sum_b, 1, nrow, ncol), [pack_a])
    kept = end({"a": got_a, "share": share_b}, 2)
    hops(3)
    share_a, share_b = received(share_a, kept["a"], steps[0], row), kept["share"]
    got_a, got_b = to_rows(share_a, steps[1], nrow, ncol), to_rows(share_b, steps[0], nrow, ncol)
    kept = end({"a": got_a, "b": got_b}, 3)
    hops(4)
    share_a, share_b = received(share_a, kept["a"], steps[1], row), received(share_b, kept["b"], steps[0], row)
    for step in steps[2:]:
        share_a = received(share_a, to_rows(share_a, step, nrow, ncol), step, row)
    for step in steps[1:]:
        share_b = received(share_b, to_rows(share_b, step, nrow, ncol), step, row)
    keep, send = update(0, [pivots[1]["line"]])
    rest_a = own_rest(0, keep + along_col(send, 1, nrow, ncol))
    kept = end({"a": share_a, "b": share_b, "rest": rest_a}, 4)
    rest_a = kept["rest"]
    share_a, share_b = join(kept["a"], chip_bits, nrow, ncol), join(kept["b"], chip_bits, nrow, ncol)
    keep, send = update(1, [])
    kept = end({"a": share_a, "b": share_b, "keep": keep, "got": along_col(send, 1, nrow, ncol)}, 5)
    rest_b = own_rest(1, kept["keep"] + kept["got"])
    pack_a = join(kept["a"], [1], nrow, ncol).reshape(share, share)
    pack_b = join(kept["b"], [1], nrow, ncol).reshape(share, 2 * share)
    out_a = nt_dot(rest_a, pack_a, HIGH)
    rest_b = rest_b - jnp.dot(out_a, pack_b[:, :share], precision=HIGH)
    out = [out_a, nt_dot(rest_b, pack_b[:, share:], HIGH)]
    out = jnp.concatenate(out, 1)
    at_row = lax.broadcasted_iota(jnp.int32, out.shape, 0) + (row * ncol + col) * own
    at_col = lax.broadcasted_iota(jnp.int32, out.shape, 1)
    return jnp.where(at_col <= at_row, out, 0.0)


def solution(mesh):
    return jax.shard_map(
        functools.partial(on_device, mesh.shape["row"], mesh.shape["col"]),
        mesh=mesh,
        in_specs=(P("row", "col"), P(BOTH, None)),
        out_specs=P(BOTH, None),
        check_vma=False,
    )
```

```python
import functools
import jax
import jax.numpy as jnp
from jax import lax
from jax.experimental import pallas as pl
from jax.experimental.pallas import tpu as pltpu
from jax.sharding import PartitionSpec as P

SUB = 8
BLOCK = 128
STEP = 32
PARTS = 2
BOTH = ("row", "col")
HIGH = lax.Precision.HIGHEST


def tn_dot(a, b):
    return lax.dot_general(a, b, (((0,), (0,)), ((), ())), precision=HIGH, preferred_element_type=jnp.float32)


def nn_dot(a, b):
    return lax.dot_general(a, b, (((1,), (0,)), ((), ())), precision=HIGH, preferred_element_type=jnp.float32)


def row_of(x, k):
    return jnp.broadcast_to(x[k : k + 1, :], x.shape)


def lane_of(x, k):
    return jnp.broadcast_to(x[:, k : k + 1], x.shape)


def inverse_factor(block):
    lane = lax.broadcasted_iota(jnp.int32, (SUB, BLOCK), 1)
    sub = lax.broadcasted_iota(jnp.int32, (SUB, BLOCK), 0)
    groups = [block[SUB * q : SUB * (q + 1), :] for q in range(BLOCK // SUB)]
    per_step = STEP // SUB
    done = []
    for step in range(BLOCK // STEP):
        end = (step + 1) * per_step
        here = []
        for p in range(step * per_step, end):
            first = SUB * p
            inside = (lane >= first) & (lane < first + SUB)
            cols = [lane_of(groups[p], first + k) for k in range(SUB)]
            rows = jnp.where(inside, jnp.where(lane - first == sub, 1.0, 0.0), groups[p])
            scale = jnp.zeros((SUB, BLOCK), jnp.float32)
            col_rows, own_rows = [], []
            for k in range(SUB):
                pivot = row_of(cols[k], k)
                inv = pl.reciprocal(pivot, approx=True)
                scale = jnp.where(sub == k, lax.rsqrt(pivot), scale)
                below = jnp.where(sub > k, cols[k], 0.0)
                raw = [row_of(cols[m], k) for m in range(k + 1, SUB)]
                own = row_of(rows, k) * inv
                for i, m in enumerate(range(k + 1, SUB)):
                    cols[m] = cols[m] - (below * raw[i]) * inv
                rows = rows - below * own
                col_rows.append([r * inv for r in raw])
                own_rows.append(own)
            here.append(rows * scale)
            for q in range(p + 1, end):
                mult = [lane_of(groups[q], first + k) for k in range(SUB)]
                acc = jnp.where(inside, 0.0, groups[q])
                for k in range(SUB):
                    for i, m in enumerate(range(k + 1, SUB)):
                        mult[m] = mult[m] - mult[k] * col_rows[k][i]
                    acc = acc - mult[k] * own_rows[k]
                groups[q] = acc
        span = jnp.concatenate(here, 0)
        base = step * STEP
        span_lane = lax.broadcasted_iota(jnp.int32, (STEP, BLOCK), 1)
        span_row = lax.broadcasted_iota(jnp.int32, (STEP, BLOCK), 0) + base
        span = jnp.where((span_lane <= span_row) | (span_lane >= base + STEP), span, 0.0)
        done.append(jnp.where(span_lane <= span_row, span, 0.0))
        if base + STEP < BLOCK:
            delta = tn_dot(span, span)
            in_step = (lane >= base) & (lane < base + STEP)
            for q in range(end, BLOCK // SUB):
                groups[q] = jnp.where(in_step, 0.0, groups[q]) - delta[SUB * q : SUB * (q + 1), :]
    return jnp.concatenate(done, 0)


def inverse_panel(rest, out_ref):
    size = rest.shape[0]
    uppers, inverses = [], []
    for i in range(size // BLOCK):
        at = i * BLOCK
        inverse = inverse_factor(rest[:BLOCK, :BLOCK])
        line = []
        for j in range(i):
            total = 0.0
            for k in range(j, i):
                block = uppers[k][:, (i - k - 1) * BLOCK : (i - k) * BLOCK]
                total = total + tn_dot(block, inverses[k][j])
            line.append(-nn_dot(inverse, total))
        line.append(inverse)
        inverses.append(line)
        for j, block in enumerate(line):
            out_ref[at : at + BLOCK, j * BLOCK : (j + 1) * BLOCK] = block
        if at + BLOCK < size:
            out_ref[at : at + BLOCK, at + BLOCK :] = jnp.zeros((BLOCK, size - at - BLOCK), jnp.float32)
            uppers.append(nn_dot(inverse, rest[:BLOCK, BLOCK:]))
            rest = rest[BLOCK:, BLOCK:] - tn_dot(uppers[-1], uppers[-1])


def panel_kernel(place_ref, *refs):
    rest_ref, upper, (out_ref, share_ref) = refs[0], refs[1:-2], refs[-2:]
    size, share = out_ref.shape[0], share_ref.shape[0]

    @pl.when(place_ref[0] == 0)
    def _():
        inverse_panel(rest_ref[...], out_ref)
        rows = pl.ds(pl.multiple_of(place_ref[1] * share, share), share)
        if upper:
            share_ref[:, :size] = upper[0][rows, :]
        share_ref[:, -size:] = out_ref[rows, :]


def first_kernel(place_ref, mine_ref, other_ref, out_ref, share_ref, whole):
    half = mine_ref.shape[0]
    low = place_ref[1] % 2

    @pl.when(place_ref[0] == 0)
    def _():
        whole[pl.ds(pl.multiple_of(low * half, half), half), :] = mine_ref[...]
        whole[pl.ds(pl.multiple_of((1 - low) * half, half), half), :] = other_ref[...]

    panel_kernel(place_ref, whole, out_ref, share_ref)


def panel_factor(place, ncol, size, *args):
    vmem = pl.BlockSpec(memory_space=pltpu.VMEM)
    first = args[0].shape[0] < size
    wide = size if first else 2 * size
    return pl.pallas_call(
        first_kernel if first else panel_kernel,
        out_shape=[
            jax.ShapeDtypeStruct((size, size), jnp.float32),
            jax.ShapeDtypeStruct((size // ncol, wide), jnp.float32),
        ],
        in_specs=[pl.BlockSpec(memory_space=pltpu.SMEM)] + [vmem] * len(args),
        out_specs=[vmem, vmem],
        scratch_shapes=[pltpu.VMEM((size, size), jnp.float32)] if first else [],
        compiler_params=pltpu.CompilerParams(vmem_limit_bytes=40 << 20),
        cost_estimate=pl.CostEstimate(flops=2 * 10**10, bytes_accessed=8 * size * wide, transcendentals=0),
    )(place, *args)


def nt_dot(a, b, precision=None):
    return lax.dot_general(
        a, b, (((1,), (1,)), ((), ())), precision=precision, preferred_element_type=jnp.float32
    )


def update_kernel(slots, count, order_ref, factor_ref, *refs):
    choices, (keep_ref, send_ref, pivots, sem) = refs[:count], refs[-4:]
    slot = pl.program_id(0)
    for i, choice in enumerate(choices):

        @pl.when((slot == 0) & (order_ref[slots] == i))
        def _():
            copy = pltpu.make_async_copy(choice, pivots, sem)
            copy.start()
            copy.wait()

    product = nt_dot(factor_ref[...], pivots[...])

    @pl.when(slot < slots // 2)
    def _():
        keep_ref[...] = product

    @pl.when(slot >= slots // 2)
    def _():
        send_ref[...] = product


def update_product(factor, choices, which, col, ncol, after):
    rows, depth = factor.shape
    own, count = rows // ncol, choices[0].shape[0]
    half = ncol // 2
    flips = list(range(0, ncol, 2)) + list(range(1, ncol, 2))
    order = jnp.concatenate([col ^ jnp.asarray(flips, jnp.int32), which[None].astype(jnp.int32)])
    out = jax.ShapeDtypeStruct((half * own, count), jnp.float32)
    return pl.pallas_call(
        functools.partial(update_kernel, ncol, len(choices)),
        out_shape=(out, out),
        grid_spec=pltpu.PrefetchScalarGridSpec(
            num_scalar_prefetch=1,
            grid=(ncol,),
            in_specs=[pl.BlockSpec((own, depth), lambda s, order: (order[s], 0))]
            + [pl.BlockSpec(memory_space=pltpu.HBM)] * (len(choices) + len(after)),
            out_specs=(
                pl.BlockSpec((own, count), lambda s, order: (jnp.minimum(s, half - 1), 0)),
                pl.BlockSpec((own, count), lambda s, order: (jnp.maximum(s - half, 0), 0)),
            ),
            scratch_shapes=[pltpu.VMEM((count, depth), factor.dtype), pltpu.SemaphoreType.DMA],
        ),
        compiler_params=pltpu.CompilerParams(vmem_limit_bytes=40 << 20),
        cost_estimate=pl.CostEstimate(
            flops=2 * rows * depth * count, bytes_accessed=2 * rows * depth + 4 * rows * count, transcendentals=0
        ),
    )(order, factor, *choices, *after)


def stage_end(arrays):
    hbm = pl.BlockSpec(memory_space=pltpu.HBM)
    names = sorted(arrays)
    results = pl.pallas_call(
        lambda *refs: None,
        out_shape=[jax.ShapeDtypeStruct(arrays[n].shape, arrays[n].dtype) for n in names],
        in_specs=[hbm] * len(names),
        out_specs=[hbm] * len(names),
        input_output_aliases={i: i for i in range(len(names))},
    )(*[arrays[n] for n in names])
    return dict(zip(names, results))


def along_row(block, moves, ncol):
    return lax.ppermute(block, BOTH, [(a * ncol + c, b * ncol + c) for c in range(ncol) for a, b in moves[c % 2]])


def tree_step(step, block, buffers, row, odd, nrow, ncol):
    line = nrow // 2
    new = {}
    if step == 0:
        new["first"] = along_row(block, ([], [(0, 1)]), ncol)
    elif step == 1:
        held = jnp.where(odd == 1, buffers["first"], block)
        new["half"] = along_row(held, both_lines([(0, line // 2)]), ncol)
    elif step == 2:
        held, reach = buffers["half"], line // 4
        while reach:
            ahead = [(p, p + reach) for p in range(2 * reach, line, 2 * reach)]
            new["on%d" % reach] = along_row(held, both_lines(ahead), ncol)
            new["back%d" % reach] = along_row(held, both_lines([(2 * reach, reach)]), ncol)
            if reach > 1:
                place = row // 2
                held = jnp.where(place % (2 * reach) == reach, new["on%d" % reach], held)
                held = jnp.where(place == reach, new["back%d" % reach], held)
            reach //= 2
    else:
        held, place = block, row // 2
        for name in sorted(buffers):
            for p in arrivals(name, line):
                held = jnp.where((row == 1) if name == "first" else (place == p), buffers[name], held)
        buffers.clear()
        new["line"] = held
        even = [(2 * p, 2 * p + 1) for p in range(line)]
        odds = [(2 * p + 1, 2 * p) for p in range(1, line)]
        new["across"] = along_row(held, (even, odds), ncol)
    return new


def both_lines(moves):
    return [(2 * a, 2 * b) for a, b in moves], [(2 * a + 1, 2 * b + 1) for a, b in moves]


def arrivals(name, line):
    if name == "first":
        return [0]
    if name == "half":
        return [line // 2]
    reach = int(name.strip("onback"))
    if name.startswith("on"):
        return [p + reach for p in range(2 * reach, line, 2 * reach)]
    return [reach]


def along_col(block, bit, nrow, ncol):
    return lax.ppermute(block, BOTH, [(r * ncol + c, r * ncol + (c ^ bit)) for r in range(nrow) for c in range(ncol)])


def core_halves(block):
    half = block.shape[0] // 2
    low = lax.axis_index("col") % 2
    mine = lax.dynamic_slice_in_dim(block, low * half, half, 0)
    other = lax.dynamic_slice_in_dim(block, (1 - low) * half, half, 0)
    return mine, other


def sum_between_chips(mine, nrow, ncol):
    bit = 2
    while bit < ncol:
        mine = mine + along_col(mine, bit, nrow, ncol)
        bit *= 2
    return mine


def scatter_between_chips(keep, nrow, ncol):
    bit = ncol // 2
    while bit > 1:
        half = keep.shape[0] // 2
        keep = keep[:half] + along_col(keep[half:], bit, nrow, ncol)
        bit //= 2
    return keep


def to_rows(mine, step, nrow, ncol):
    if step == 1:
        moves = [(0, 1)]
    else:
        moves = [(r + y, r + y + step) for r in range(0, nrow, 2 * step) for y in (0, 1)]
    return along_row(mine, (moves, moves), ncol)


def received(mine, got, step, row):
    return jnp.where(row == 1 if step == 1 else (row - row % 2) % (2 * step) == step, got, mine)


def join(mine, bits, nrow, ncol):
    share, wide = mine.shape[-2:]
    mine = mine.reshape(-1, share, wide)
    for bit in bits:
        other = along_col(mine, bit, nrow, ncol)
        low = (lax.axis_index("col") & bit) == 0
        pair = [jnp.where(low, mine, other), jnp.where(low, other, mine)]
        mine = jnp.stack(pair, 1).reshape(-1, share, wide)
    return mine


def own_part(panels, at, end, first, last):
    own = panels.shape[0]
    col = lax.axis_index("col")
    blocks = []
    for c in range(at // own, -(-end // own)):
        low, high = max(at, c * own), min(end, (c + 1) * own)
        blocks.append(jnp.where(col == c, panels[low - c * own : high - c * own, first:last], 0.0))
    return jnp.concatenate(blocks, 0)


def on_device(nrow, ncol, factor, panels):
    own, width = panels.shape
    row, col = lax.axis_index("row"), lax.axis_index("col")
    odd = col % 2
    share = width // PARTS
    place = jnp.stack([row, col]).astype(jnp.int32)
    steps = [1]
    while nrow >> len(steps) > 1:
        steps.append(nrow >> len(steps))
    live = {"own%d" % i: factor[i * share : (i + 1) * share] for i in range(PARTS)}
    pivots = [{} for _ in range(PARTS)]
    fresh = [[] for _ in range(PARTS)]

    def hops(number):
        for i in range(PARTS):
            if 0 <= number - i <= 3:
                new = tree_step(number - i, live["own%d" % i], pivots[i], row, odd, nrow, ncol)
                pivots[i].update(new)
                fresh[i] = [name for name in new if name != "line"]
            else:
                fresh[i] = []

    def update(i, after):
        across = (row > 0) & (row % 2 != odd)
        choices = [pivots[i]["line"], pivots[i]["across"]]
        return update_product(factor, choices, across, col, ncol, after)

    def own_rest(i, keep):
        return panels[:, i * share : (i + 1) * share] - scatter_between_chips(keep, nrow, ncol)

    def top(at, first):
        block = factor[at : at + share], factor[first : first + share]
        return own_part(panels, at, at + share, first, first + share) - nt_dot(*block)

    chip_bits = [ncol >> (k + 1) for k in range(len(bin(ncol)) - 4)]

    def end(extra, number):
        named = dict(extra)
        for i in range(PARTS):
            if i == number + 1:
                named["own%d" % i] = live["own%d" % i]
            for n in fresh[i]:
                named["%s of %d" % (n, i)] = pivots[i][n]
        named = stage_end(named)
        for i in range(PARTS):
            if i == number + 1:
                live["own%d" % i] = named["own%d" % i]
            for n in fresh[i]:
                pivots[i][n] = named["%s of %d" % (n, i)]
        return {n: named[n] for n in extra}

    hops(0)
    mine, other = core_halves(top(0, 0))
    sum_a = sum_between_chips(mine + along_col(other, 1, nrow, ncol), nrow, ncol)
    mine, other = core_halves(jnp.concatenate([top(0, share), top(share, share)], 1))
    got_b = along_col(other, 1, nrow, ncol)
    kept = end({"a": sum_a, "mine": mine, "got": got_b}, 0)
    hops(1)
    sum_a, sum_b = kept["a"], sum_between_chips(kept["mine"] + kept["got"], nrow, ncol)
    pack_a, share_a = panel_factor(place, ncol, share, sum_a, along_col(sum_a, 1, nrow, ncol))
    kept = end({"b": sum_b, "share": share_a}, 1)
    hops(2)
    sum_b, share_a = join(kept["b"], [1], nrow, ncol).reshape(share, 2 * share), kept["share"]
    got_a = to_rows(share_a, steps[0], nrow, ncol)
    upper = jnp.dot(pack_a, sum_b[:, :share], precision=HIGH)
    block = sum_b[:, share:] - lax.dot_general(upper, upper, (((0,), (0,)), ((), ())), precision=HIGH)
    share_b = panel_factor(place, ncol, share, block, upper)[1]
    kept = end({"a": got_a, "share": share_b}, 2)
    hops(3)
    share_a, share_b = received(share_a, kept["a"], steps[0], row), kept["share"]
    got_a, got_b = to_rows(share_a, steps[1], nrow, ncol), to_rows(share_b, steps[0], nrow, ncol)
    kept = end({"a": got_a, "b": got_b}, 3)
    hops(4)
    share_a, share_b = received(share_a, kept["a"], steps[1], row), received(share_b, kept["b"], steps[0], row)
    for step in steps[2:]:
        share_a = received(share_a, to_rows(share_a, step, nrow, ncol), step, row)
    for step in steps[1:]:
        share_b = received(share_b, to_rows(share_b, step, nrow, ncol), step, row)
    share_a = join(share_a, chip_bits, nrow, ncol)
    keep, send = update(0, [pivots[1]["line"]])
    rest_a = own_rest(0, keep + along_col(send, 1, nrow, ncol))
    kept = end({"a": share_a, "b": share_b, "rest": rest_a}, 4)
    rest_a, share_a = kept["rest"], kept["a"]
    share_b = join(kept["b"], chip_bits, nrow, ncol)
    keep, send = update(1, [])
    kept = end({"b": share_b, "keep": keep, "got": along_col(send, 1, nrow, ncol)}, 5)
    rest_b = own_rest(1, kept["keep"] + kept["got"])
    pack_a = join(share_a, [1], nrow, ncol).reshape(share, share)
    pack_b = join(kept["b"], [1], nrow, ncol).reshape(share, 2 * share)
    out_a = nt_dot(rest_a, pack_a, HIGH)
    rest_b = rest_b - jnp.dot(out_a, pack_b[:, :share], precision=HIGH)
    out = [out_a, nt_dot(rest_b, pack_b[:, share:], HIGH)]
    out = jnp.concatenate(out, 1)
    at_row = lax.broadcasted_iota(jnp.int32, out.shape, 0) + (row * ncol + col) * own
    at_col = lax.broadcasted_iota(jnp.int32, out.shape, 1)
    return jnp.where(at_col <= at_row, out, 0.0)


def solution(mesh):
    return jax.shard_map(
        functools.partial(on_device, mesh.shape["row"], mesh.shape["col"]),
        mesh=mesh,
        in_specs=(P("row", "col"), P(BOTH, None)),
        out_specs=P(BOTH, None),
        check_vma=False,
    )
```

```python
import functools
import jax
import jax.numpy as jnp
from jax import lax
from jax.experimental import pallas as pl
from jax.experimental.pallas import tpu as pltpu
from jax.sharding import PartitionSpec as P

SUB = 8
BLOCK = 128
STEP = 32
PARTS = 2
BOTH = ("row", "col")
HIGH = lax.Precision.HIGHEST


def tn_dot(a, b):
    return lax.dot_general(a, b, (((0,), (0,)), ((), ())), precision=HIGH, preferred_element_type=jnp.float32)


def nn_dot(a, b):
    return lax.dot_general(a, b, (((1,), (0,)), ((), ())), precision=HIGH, preferred_element_type=jnp.float32)


def row_of(x, k):
    return jnp.broadcast_to(x[k : k + 1, :], x.shape)


def lane_of(x, k):
    return jnp.broadcast_to(x[:, k : k + 1], x.shape)


def inverse_factor(block):
    lane = lax.broadcasted_iota(jnp.int32, (SUB, BLOCK), 1)
    sub = lax.broadcasted_iota(jnp.int32, (SUB, BLOCK), 0)
    groups = [block[SUB * q : SUB * (q + 1), :] for q in range(BLOCK // SUB)]
    per_step = STEP // SUB
    done = []
    for step in range(BLOCK // STEP):
        end = (step + 1) * per_step
        here = []
        for p in range(step * per_step, end):
            first = SUB * p
            inside = (lane >= first) & (lane < first + SUB)
            cols = [lane_of(groups[p], first + k) for k in range(SUB)]
            rows = jnp.where(inside, jnp.where(lane - first == sub, 1.0, 0.0), groups[p])
            scale = jnp.zeros((SUB, BLOCK), jnp.float32)
            col_rows, own_rows = [], []
            for k in range(SUB):
                pivot = row_of(cols[k], k)
                inv = pl.reciprocal(pivot, approx=True)
                scale = jnp.where(sub == k, lax.rsqrt(pivot), scale)
                below = jnp.where(sub > k, cols[k], 0.0)
                raw = [row_of(cols[m], k) for m in range(k + 1, SUB)]
                own = row_of(rows, k) * inv
                for i, m in enumerate(range(k + 1, SUB)):
                    cols[m] = cols[m] - (below * raw[i]) * inv
                rows = rows - below * own
                col_rows.append([r * inv for r in raw])
                own_rows.append(own)
            here.append(rows * scale)
            for q in range(p + 1, end):
                mult = [lane_of(groups[q], first + k) for k in range(SUB)]
                acc = jnp.where(inside, 0.0, groups[q])
                for k in range(SUB):
                    for i, m in enumerate(range(k + 1, SUB)):
                        mult[m] = mult[m] - mult[k] * col_rows[k][i]
                    acc = acc - mult[k] * own_rows[k]
                groups[q] = acc
        span = jnp.concatenate(here, 0)
        base = step * STEP
        span_lane = lax.broadcasted_iota(jnp.int32, (STEP, BLOCK), 1)
        span_row = lax.broadcasted_iota(jnp.int32, (STEP, BLOCK), 0) + base
        span = jnp.where((span_lane <= span_row) | (span_lane >= base + STEP), span, 0.0)
        done.append(jnp.where(span_lane <= span_row, span, 0.0))
        if base + STEP < BLOCK:
            delta = tn_dot(span, span)
            in_step = (lane >= base) & (lane < base + STEP)
            for q in range(end, BLOCK // SUB):
                groups[q] = jnp.where(in_step, 0.0, groups[q]) - delta[SUB * q : SUB * (q + 1), :]
    return jnp.concatenate(done, 0)


def inverse_panel(rest, out_ref):
    size = rest.shape[0]
    uppers, inverses = [], []
    for i in range(size // BLOCK):
        at = i * BLOCK
        inverse = inverse_factor(rest[:BLOCK, :BLOCK])
        line = []
        for j in range(i):
            total = 0.0
            for k in range(j, i):
                block = uppers[k][:, (i - k - 1) * BLOCK : (i - k) * BLOCK]
                total = total + tn_dot(block, inverses[k][j])
            line.append(-nn_dot(inverse, total))
        line.append(inverse)
        inverses.append(line)
        for j, block in enumerate(line):
            out_ref[at : at + BLOCK, j * BLOCK : (j + 1) * BLOCK] = block
        if at + BLOCK < size:
            out_ref[at : at + BLOCK, at + BLOCK :] = jnp.zeros((BLOCK, size - at - BLOCK), jnp.float32)
            uppers.append(nn_dot(inverse, rest[:BLOCK, BLOCK:]))
            rest = rest[BLOCK:, BLOCK:] - tn_dot(uppers[-1], uppers[-1])


def panel_kernel(place_ref, rest_ref, out_ref, share_ref):
    share = share_ref.shape[0]

    @pl.when(place_ref[0] == 0)
    def _():
        inverse_panel(rest_ref[...], out_ref)
        share_ref[...] = out_ref[pl.ds(pl.multiple_of(place_ref[1] * share, share), share), :]


def first_kernel(place_ref, mine_ref, other_ref, out_ref, share_ref, whole):
    half = mine_ref.shape[0]
    low = place_ref[1] % 2

    @pl.when(place_ref[0] == 0)
    def _():
        whole[pl.ds(pl.multiple_of(low * half, half), half), :] = mine_ref[...]
        whole[pl.ds(pl.multiple_of((1 - low) * half, half), half), :] = other_ref[...]

    panel_kernel(place_ref, whole, out_ref, share_ref)


def panel_factor(place, ncol, size, *args):
    vmem = pl.BlockSpec(memory_space=pltpu.VMEM)
    first = args[0].shape[0] < size
    return pl.pallas_call(
        first_kernel if first else panel_kernel,
        out_shape=[
            jax.ShapeDtypeStruct((size, size), jnp.float32),
            jax.ShapeDtypeStruct((size // ncol, size), jnp.float32),
        ],
        in_specs=[pl.BlockSpec(memory_space=pltpu.SMEM)] + [vmem] * len(args),
        out_specs=[vmem, vmem],
        scratch_shapes=[pltpu.VMEM((size, size), jnp.float32)] if first else [],
        compiler_params=pltpu.CompilerParams(vmem_limit_bytes=40 << 20),
        cost_estimate=pl.CostEstimate(flops=2 * 10**10, bytes_accessed=8 * size * size, transcendentals=0),
    )(place, *args)


def nt_dot(a, b, precision=None):
    return lax.dot_general(
        a, b, (((1,), (1,)), ((), ())), precision=precision, preferred_element_type=jnp.float32
    )


def update_kernel(slots, count, order_ref, factor_ref, *refs):
    choices, (keep_ref, send_ref, pivots, sem) = refs[:count], refs[-4:]
    slot = pl.program_id(0)
    for i, choice in enumerate(choices):

        @pl.when((slot == 0) & (order_ref[slots] == i))
        def _():
            copy = pltpu.make_async_copy(choice, pivots, sem)
            copy.start()
            copy.wait()

    product = nt_dot(factor_ref[...], pivots[...])

    @pl.when(slot < slots // 2)
    def _():
        keep_ref[...] = product

    @pl.when(slot >= slots // 2)
    def _():
        send_ref[...] = product


def update_product(factor, choices, which, col, ncol, after):
    rows, depth = factor.shape
    own, count = rows // ncol, choices[0].shape[0]
    half = ncol // 2
    flips = list(range(0, ncol, 2)) + list(range(1, ncol, 2))
    order = jnp.concatenate([col ^ jnp.asarray(flips, jnp.int32), which[None].astype(jnp.int32)])
    out = jax.ShapeDtypeStruct((half * own, count), jnp.float32)
    return pl.pallas_call(
        functools.partial(update_kernel, ncol, len(choices)),
        out_shape=(out, out),
        grid_spec=pltpu.PrefetchScalarGridSpec(
            num_scalar_prefetch=1,
            grid=(ncol,),
            in_specs=[pl.BlockSpec((own, depth), lambda s, order: (order[s], 0))]
            + [pl.BlockSpec(memory_space=pl.ANY)] * (len(choices) + len(after)),
            out_specs=(
                pl.BlockSpec((own, count), lambda s, order: (jnp.minimum(s, half - 1), 0)),
                pl.BlockSpec((own, count), lambda s, order: (jnp.maximum(s - half, 0), 0)),
            ),
            scratch_shapes=[pltpu.VMEM((count, depth), factor.dtype), pltpu.SemaphoreType.DMA],
        ),
        compiler_params=pltpu.CompilerParams(vmem_limit_bytes=40 << 20),
        cost_estimate=pl.CostEstimate(
            flops=2 * rows * depth * count, bytes_accessed=2 * rows * depth + 4 * rows * count, transcendentals=0
        ),
    )(order, factor, *choices, *after)


def stage_end(arrays):
    hbm = pl.BlockSpec(memory_space=pl.ANY)
    names = sorted(arrays)
    results = pl.pallas_call(
        lambda *refs: None,
        out_shape=[jax.ShapeDtypeStruct(arrays[n].shape, arrays[n].dtype) for n in names],
        in_specs=[hbm] * len(names),
        out_specs=[hbm] * len(names),
        input_output_aliases={i: i for i in range(len(names))},
    )(*[arrays[n] for n in names])
    return dict(zip(names, results))


def along_row(block, moves, ncol):
    return lax.ppermute(block, BOTH, [(a * ncol + c, b * ncol + c) for c in range(ncol) for a, b in moves[c % 2]])


def tree_step(step, block, buffers, row, odd, nrow, ncol):
    line = nrow // 2
    new = {}
    if step == 0:
        new["first"] = along_row(block, ([], [(0, 1)]), ncol)
    elif step == 1:
        held = jnp.where(odd == 1, buffers["first"], block)
        new["half"] = along_row(held, both_lines([(0, line // 2)]), ncol)
    elif step == 2:
        held, reach = buffers["half"], line // 4
        while reach:
            ahead = [(p, p + reach) for p in range(2 * reach, line, 2 * reach)]
            new["on%d" % reach] = along_row(held, both_lines(ahead), ncol)
            new["back%d" % reach] = along_row(held, both_lines([(2 * reach, reach)]), ncol)
            if reach > 1:
                place = row // 2
                held = jnp.where(place % (2 * reach) == reach, new["on%d" % reach], held)
                held = jnp.where(place == reach, new["back%d" % reach], held)
            reach //= 2
    else:
        held, place = block, row // 2
        for name in sorted(buffers):
            for p in arrivals(name, line):
                held = jnp.where((row == 1) if name == "first" else (place == p), buffers[name], held)
        buffers.clear()
        new["line"] = held
        even = [(2 * p, 2 * p + 1) for p in range(line)]
        odds = [(2 * p + 1, 2 * p) for p in range(1, line)]
        new["across"] = along_row(held, (even, odds), ncol)
    return new


def both_lines(moves):
    return [(2 * a, 2 * b) for a, b in moves], [(2 * a + 1, 2 * b + 1) for a, b in moves]


def arrivals(name, line):
    if name == "first":
        return [0]
    if name == "half":
        return [line // 2]
    reach = int(name.strip("onback"))
    if name.startswith("on"):
        return [p + reach for p in range(2 * reach, line, 2 * reach)]
    return [reach]


def along_col(block, bit, nrow, ncol):
    return lax.ppermute(block, BOTH, [(r * ncol + c, r * ncol + (c ^ bit)) for r in range(nrow) for c in range(ncol)])


def core_halves(block):
    half = block.shape[0] // 2
    low = lax.axis_index("col") % 2
    mine = lax.dynamic_slice_in_dim(block, low * half, half, 0)
    other = lax.dynamic_slice_in_dim(block, (1 - low) * half, half, 0)
    return mine, other


def sum_between_chips(mine, nrow, ncol):
    bit = 2
    while bit < ncol:
        mine = mine + along_col(mine, bit, nrow, ncol)
        bit *= 2
    return mine


def scatter_between_chips(keep, nrow, ncol):
    bit = ncol // 2
    while bit > 1:
        half = keep.shape[0] // 2
        keep = keep[:half] + along_col(keep[half:], bit, nrow, ncol)
        bit //= 2
    return keep


def to_rows(mine, step, holders, ncol):
    moves = [(r, r + step) for r in holders]
    return along_row(mine, (moves, moves), ncol)


def received(mine, got, step, holders, row):
    hit = jnp.zeros_like(row == 0)
    for r in holders:
        hit = hit | (row == r + step)
    return jnp.where(hit, got, mine)


def rounds(steps):
    holders, result = [0], []
    for step in steps:
        result.append((step, list(holders)))
        holders += [r + step for r in holders]
    return result


def join(mine, bits, nrow, ncol):
    share, wide = mine.shape[-2:]
    mine = mine.reshape(-1, share, wide)
    for bit in bits:
        other = along_col(mine, bit, nrow, ncol)
        low = (lax.axis_index("col") & bit) == 0
        pair = [jnp.where(low, mine, other), jnp.where(low, other, mine)]
        mine = jnp.stack(pair, 1).reshape(-1, share, wide)
    return mine


def own_part(panels, at, end, first, last):
    own = panels.shape[0]
    col = lax.axis_index("col")
    blocks = []
    for c in range(at // own, -(-end // own)):
        low, high = max(at, c * own), min(end, (c + 1) * own)
        blocks.append(jnp.where(col == c, panels[low - c * own : high - c * own, first:last], 0.0))
    return jnp.concatenate(blocks, 0)


def on_device(nrow, ncol, factor, panels):
    own, width = panels.shape
    row, col = lax.axis_index("row"), lax.axis_index("col")
    odd = col % 2
    share = width // PARTS
    place = jnp.stack([row, col]).astype(jnp.int32)
    halves = [nrow >> k for k in range(1, nrow.bit_length())]
    tree_a, tree_b = rounds([1] + halves[:-1]), rounds(halves)
    live = {"own%d" % i: factor[i * share : (i + 1) * share] for i in range(PARTS)}
    pivots = [{} for _ in range(PARTS)]
    fresh = [[] for _ in range(PARTS)]

    def hops(number):
        for i in range(PARTS):
            if 0 <= number - i <= 3:
                new = tree_step(number - i, live["own%d" % i], pivots[i], row, odd, nrow, ncol)
                pivots[i].update(new)
                fresh[i] = [name for name in new if name != "line"]
            else:
                fresh[i] = []

    def update(i, after):
        across = (row > 0) & (row % 2 != odd)
        choices = [pivots[i]["line"], pivots[i]["across"]]
        return update_product(factor, choices, across, col, ncol, after)

    def own_rest(i, keep):
        return panels[:, i * share : (i + 1) * share] - scatter_between_chips(keep, nrow, ncol)

    def top(at, first):
        block = factor[at : at + share], factor[first : first + share]
        return own_part(panels, at, at + share, first, first + share) - nt_dot(*block)

    chip_bits = [ncol >> (k + 1) for k in range(len(bin(ncol)) - 4)]

    def end(extra, number):
        named = dict(extra)
        for i in range(PARTS):
            if i == number + 1:
                named["own%d" % i] = live["own%d" % i]
            for n in fresh[i]:
                named["%s of %d" % (n, i)] = pivots[i][n]
        named = stage_end(named)
        for i in range(PARTS):
            if i == number + 1:
                live["own%d" % i] = named["own%d" % i]
            for n in fresh[i]:
                pivots[i][n] = named["%s of %d" % (n, i)]
        return {n: named[n] for n in extra}

    hops(0)
    mine, other = core_halves(top(0, 0))
    sum_a = sum_between_chips(mine + along_col(other, 1, nrow, ncol), nrow, ncol)
    mine, other = core_halves(jnp.concatenate([top(0, share), top(share, share)], 1))
    got_b = along_col(other, 1, nrow, ncol)
    kept = end({"a": sum_a, "mine": mine, "got": got_b}, 0)
    hops(1)
    sum_a, sum_b = kept["a"], sum_between_chips(kept["mine"] + kept["got"], nrow, ncol)
    pack_a, share_a = panel_factor(place, ncol, share, sum_a, along_col(sum_a, 1, nrow, ncol))
    kept = end({"b": sum_b, "share": share_a}, 1)
    hops(2)
    sum_b = join(kept["b"], [1], nrow, ncol).reshape(share, 2 * share)
    upper = jnp.dot(pack_a, sum_b[:, :share], precision=HIGH)
    block = sum_b[:, share:] - lax.dot_general(upper, upper, (((0,), (0,)), ((), ())), precision=HIGH)
    quarter = share // ncol
    share_a = jnp.concatenate([kept["share"], lax.dynamic_slice_in_dim(upper, col * quarter, quarter, 0)], 1)
    got_a = to_rows(share_a, *tree_a[0], ncol)
    share_b = panel_factor(place, ncol, share, block)[1]
    kept = end({"a": got_a, "b": share_b}, 2)
    hops(3)
    share_a, share_b = received(share_a, kept["a"], *tree_a[0], row), kept["b"]
    got_b, got_a = to_rows(share_b, *tree_b[0], ncol), to_rows(share_a, *tree_a[1], ncol)
    kept = end({"a": got_a, "b": got_b}, 3)
    hops(4)
    share_a, share_b = received(share_a, kept["a"], *tree_a[1], row), received(share_b, kept["b"], *tree_b[0], row)
    for turn in tree_a[2:-1]:
        share_a = received(share_a, to_rows(share_a, *turn, ncol), *turn, row)
    for turn in tree_b[1:-2]:
        share_b = received(share_b, to_rows(share_b, *turn, ncol), *turn, row)
    got_b, got_a = to_rows(share_b, *tree_b[-2], ncol), to_rows(share_a, *tree_a[-1], ncol)
    keep, send = update(0, [pivots[1]["line"]])
    rest_a = own_rest(0, keep + along_col(send, 1, nrow, ncol))
    kept = end({"a": got_a, "b": got_b, "rest": rest_a}, 4)
    rest_a = kept["rest"]
    share_a = join(received(share_a, kept["a"], *tree_a[-1], row), chip_bits, nrow, ncol)
    share_b = received(share_b, kept["b"], *tree_b[-2], row)
    got_b = to_rows(share_b, *tree_b[-1], ncol)
    keep, send = update(1, [])
    kept = end({"a": share_a, "b": got_b, "keep": keep, "got": along_col(send, 1, nrow, ncol)}, 5)
    rest_b = own_rest(1, kept["keep"] + kept["got"])
    pack_a = join(kept["a"], [1], nrow, ncol).reshape(share, 2 * share)
    pack_b = join(received(share_b, kept["b"], *tree_b[-1], row), chip_bits + [1], nrow, ncol).reshape(share, share)
    out_a = nt_dot(rest_a, pack_a[:, :share], HIGH)
    rest_b = rest_b - jnp.dot(out_a, pack_a[:, share:], precision=HIGH)
    out = [out_a, nt_dot(rest_b, pack_b, HIGH)]
    out = jnp.concatenate(out, 1)
    at_row = lax.broadcasted_iota(jnp.int32, out.shape, 0) + (row * ncol + col) * own
    at_col = lax.broadcasted_iota(jnp.int32, out.shape, 1)
    return jnp.where(at_col <= at_row, out, 0.0)


def solution(mesh):
    return jax.shard_map(
        functools.partial(on_device, mesh.shape["row"], mesh.shape["col"]),
        mesh=mesh,
        in_specs=(P("row", "col"), P(BOTH, None)),
        out_specs=P(BOTH, None),
        check_vma=False,
    )
```

```python
import functools
import jax
import jax.numpy as jnp
from jax import lax
from jax.experimental import pallas as pl
from jax.experimental.pallas import tpu as pltpu
from jax.sharding import PartitionSpec as P

SUB = 8
BLOCK = 128
STEP = 32
PARTS = 2
BOTH = ("row", "col")
HIGH = lax.Precision.HIGHEST


def split(x):
    first = x.astype(jnp.bfloat16)
    rest = x - first.astype(jnp.float32)
    second = rest.astype(jnp.bfloat16)
    return first, second, (rest - second.astype(jnp.float32)).astype(jnp.bfloat16)


def joined_dot(a, b, a_axis):
    a1, a2, a3 = split(a)
    b1, b2, b3 = (a1, a2, a3) if a is b else split(b)
    left = jnp.concatenate([a1, a1, a2, a2, a1, a3], a_axis)
    right = jnp.concatenate([b1, b2, b1, b2, b3, b1], 0)
    return lax.dot_general(left, right, (((a_axis,), (0,)), ((), ())), preferred_element_type=jnp.float32)


def tn_dot(a, b):
    return joined_dot(a, b, 0)


def nn_dot(a, b):
    return joined_dot(a, b, 1)


def row_of(x, k):
    return jnp.broadcast_to(x[k : k + 1, :], x.shape)


def lane_of(x, k):
    return jnp.broadcast_to(x[:, k : k + 1], x.shape)


def inverse_factor(block):
    lane = lax.broadcasted_iota(jnp.int32, (SUB, BLOCK), 1)
    sub = lax.broadcasted_iota(jnp.int32, (SUB, BLOCK), 0)
    groups = [block[SUB * q : SUB * (q + 1), :] for q in range(BLOCK // SUB)]
    per_step = STEP // SUB
    done = []
    for step in range(BLOCK // STEP):
        end = (step + 1) * per_step
        here = []
        for p in range(step * per_step, end):
            first = SUB * p
            inside = (lane >= first) & (lane < first + SUB)
            cols = [lane_of(groups[p], first + k) for k in range(SUB)]
            rows = jnp.where(inside, jnp.where(lane - first == sub, 1.0, 0.0), groups[p])
            scale = jnp.zeros((SUB, BLOCK), jnp.float32)
            col_rows, own_rows = [], []
            for k in range(SUB):
                pivot = row_of(cols[k], k)
                inv = pl.reciprocal(pivot, approx=True)
                scale = jnp.where(sub == k, lax.rsqrt(pivot), scale)
                below = jnp.where(sub > k, cols[k], 0.0)
                raw = [row_of(cols[m], k) for m in range(k + 1, SUB)]
                own = row_of(rows, k) * inv
                for i, m in enumerate(range(k + 1, SUB)):
                    cols[m] = cols[m] - (below * raw[i]) * inv
                rows = rows - below * own
                col_rows.append([r * inv for r in raw])
                own_rows.append(own)
            here.append(rows * scale)
            for q in range(p + 1, end):
                mult = [lane_of(groups[q], first + k) for k in range(SUB)]
                acc = jnp.where(inside, 0.0, groups[q])
                for k in range(SUB):
                    for i, m in enumerate(range(k + 1, SUB)):
                        mult[m] = mult[m] - mult[k] * col_rows[k][i]
                    acc = acc - mult[k] * own_rows[k]
                groups[q] = acc
        span = jnp.concatenate(here, 0)
        base = step * STEP
        span_lane = lax.broadcasted_iota(jnp.int32, (STEP, BLOCK), 1)
        span_row = lax.broadcasted_iota(jnp.int32, (STEP, BLOCK), 0) + base
        span = jnp.where((span_lane <= span_row) | (span_lane >= base + STEP), span, 0.0)
        done.append(jnp.where(span_lane <= span_row, span, 0.0))
        if base + STEP < BLOCK:
            delta = tn_dot(span, span)
            in_step = (lane >= base) & (lane < base + STEP)
            for q in range(end, BLOCK // SUB):
                groups[q] = jnp.where(in_step, 0.0, groups[q]) - delta[SUB * q : SUB * (q + 1), :]
    return jnp.concatenate(done, 0)


def inverse_panel(rest, out_ref):
    size = rest.shape[0]
    uppers, inverses = [], []
    for i in range(size // BLOCK):
        at = i * BLOCK
        inverse = inverse_factor(rest[:BLOCK, :BLOCK])
        line = []
        for j in range(i):
            total = 0.0
            for k in range(j, i):
                block = uppers[k][:, (i - k - 1) * BLOCK : (i - k) * BLOCK]
                total = total + tn_dot(block, inverses[k][j])
            line.append(-nn_dot(inverse, total))
        line.append(inverse)
        inverses.append(line)
        for j, block in enumerate(line):
            out_ref[at : at + BLOCK, j * BLOCK : (j + 1) * BLOCK] = block
        if at + BLOCK < size:
            out_ref[at : at + BLOCK, at + BLOCK :] = jnp.zeros((BLOCK, size - at - BLOCK), jnp.float32)
            uppers.append(nn_dot(inverse, rest[:BLOCK, BLOCK:]))
            rest = rest[BLOCK:, BLOCK:] - tn_dot(uppers[-1], uppers[-1])


def panel_kernel(place_ref, rest_ref, out_ref, share_ref):
    share = share_ref.shape[0]

    @pl.when(place_ref[0] == 0)
    def _():
        inverse_panel(rest_ref[...], out_ref)
        share_ref[...] = out_ref[pl.ds(pl.multiple_of(place_ref[1] * share, share), share), :]


def first_kernel(place_ref, mine_ref, other_ref, out_ref, share_ref, whole):
    half = mine_ref.shape[0]
    low = place_ref[1] % 2

    @pl.when(place_ref[0] == 0)
    def _():
        whole[pl.ds(pl.multiple_of(low * half, half), half), :] = mine_ref[...]
        whole[pl.ds(pl.multiple_of((1 - low) * half, half), half), :] = other_ref[...]

    panel_kernel(place_ref, whole, out_ref, share_ref)


def panel_factor(place, ncol, size, *args):
    vmem = pl.BlockSpec(memory_space=pltpu.VMEM)
    first = args[0].shape[0] < size
    return pl.pallas_call(
        first_kernel if first else panel_kernel,
        out_shape=[
            jax.ShapeDtypeStruct((size, size), jnp.float32),
            jax.ShapeDtypeStruct((size // ncol, size), jnp.float32),
        ],
        in_specs=[pl.BlockSpec(memory_space=pltpu.SMEM)] + [vmem] * len(args),
        out_specs=[vmem, vmem],
        scratch_shapes=[pltpu.VMEM((size, size), jnp.float32)] if first else [],
        compiler_params=pltpu.CompilerParams(vmem_limit_bytes=40 << 20),
        cost_estimate=pl.CostEstimate(flops=2 * 10**10, bytes_accessed=8 * size * size, transcendentals=0),
    )(place, *args)


def nt_dot(a, b, precision=None):
    return lax.dot_general(
        a, b, (((1,), (1,)), ((), ())), precision=precision, preferred_element_type=jnp.float32
    )


def update_kernel(slots, count, order_ref, factor_ref, *refs):
    choices, (keep_ref, send_ref, pivots, sem) = refs[:count], refs[-4:]
    slot = pl.program_id(0)
    for i, choice in enumerate(choices):

        @pl.when((slot == 0) & (order_ref[slots] == i))
        def _():
            copy = pltpu.make_async_copy(choice, pivots, sem)
            copy.start()
            copy.wait()

    product = nt_dot(factor_ref[...], pivots[...])

    @pl.when(slot < slots // 2)
    def _():
        keep_ref[...] = product

    @pl.when(slot >= slots // 2)
    def _():
        send_ref[...] = product


def update_product(factor, choices, which, col, ncol, after):
    rows, depth = factor.shape
    own, count = rows // ncol, choices[0].shape[0]
    half = ncol // 2
    flips = list(range(0, ncol, 2)) + list(range(1, ncol, 2))
    order = jnp.concatenate([col ^ jnp.asarray(flips, jnp.int32), which[None].astype(jnp.int32)])
    out = jax.ShapeDtypeStruct((half * own, count), jnp.float32)
    return pl.pallas_call(
        functools.partial(update_kernel, ncol, len(choices)),
        out_shape=(out, out),
        grid_spec=pltpu.PrefetchScalarGridSpec(
            num_scalar_prefetch=1,
            grid=(ncol,),
            in_specs=[pl.BlockSpec((own, depth), lambda s, order: (order[s], 0))]
            + [pl.BlockSpec(memory_space=pl.ANY)] * (len(choices) + len(after)),
            out_specs=(
                pl.BlockSpec((own, count), lambda s, order: (jnp.minimum(s, half - 1), 0)),
                pl.BlockSpec((own, count), lambda s, order: (jnp.maximum(s - half, 0), 0)),
            ),
            scratch_shapes=[pltpu.VMEM((count, depth), factor.dtype), pltpu.SemaphoreType.DMA],
        ),
        compiler_params=pltpu.CompilerParams(vmem_limit_bytes=40 << 20),
        cost_estimate=pl.CostEstimate(
            flops=2 * rows * depth * count, bytes_accessed=2 * rows * depth + 4 * rows * count, transcendentals=0
        ),
    )(order, factor, *choices, *after)


def stage_end(arrays):
    hbm = pl.BlockSpec(memory_space=pl.ANY)
    names = sorted(arrays)
    results = pl.pallas_call(
        lambda *refs: None,
        out_shape=[jax.ShapeDtypeStruct(arrays[n].shape, arrays[n].dtype) for n in names],
        in_specs=[hbm] * len(names),
        out_specs=[hbm] * len(names),
        input_output_aliases={i: i for i in range(len(names))},
    )(*[arrays[n] for n in names])
    return dict(zip(names, results))


def along_row(block, moves, ncol):
    return lax.ppermute(block, BOTH, [(a * ncol + c, b * ncol + c) for c in range(ncol) for a, b in moves[c % 2]])


def tree_step(step, block, buffers, row, odd, nrow, ncol):
    line = nrow // 2
    new = {}
    if step == 0:
        new["first"] = along_row(block, ([], [(0, 1)]), ncol)
    elif step == 1:
        held = jnp.where(odd == 1, buffers["first"], block)
        new["half"] = along_row(held, both_lines([(0, line // 2)]), ncol)
    elif step == 2:
        held, reach = buffers["half"], line // 4
        while reach:
            ahead = [(p, p + reach) for p in range(2 * reach, line, 2 * reach)]
            new["on%d" % reach] = along_row(held, both_lines(ahead), ncol)
            new["back%d" % reach] = along_row(held, both_lines([(2 * reach, reach)]), ncol)
            if reach > 1:
                place = row // 2
                held = jnp.where(place % (2 * reach) == reach, new["on%d" % reach], held)
                held = jnp.where(place == reach, new["back%d" % reach], held)
            reach //= 2
    else:
        held, place = block, row // 2
        for name in sorted(buffers):
            for p in arrivals(name, line):
                held = jnp.where((row == 1) if name == "first" else (place == p), buffers[name], held)
        buffers.clear()
        new["line"] = held
        even = [(2 * p, 2 * p + 1) for p in range(line)]
        odds = [(2 * p + 1, 2 * p) for p in range(1, line)]
        new["across"] = along_row(held, (even, odds), ncol)
    return new


def both_lines(moves):
    return [(2 * a, 2 * b) for a, b in moves], [(2 * a + 1, 2 * b + 1) for a, b in moves]


def arrivals(name, line):
    if name == "first":
        return [0]
    if name == "half":
        return [line // 2]
    reach = int(name.strip("onback"))
    if name.startswith("on"):
        return [p + reach for p in range(2 * reach, line, 2 * reach)]
    return [reach]


def along_col(block, bit, nrow, ncol):
    return lax.ppermute(block, BOTH, [(r * ncol + c, r * ncol + (c ^ bit)) for r in range(nrow) for c in range(ncol)])


def core_halves(block):
    half = block.shape[0] // 2
    low = lax.axis_index("col") % 2
    mine = lax.dynamic_slice_in_dim(block, low * half, half, 0)
    other = lax.dynamic_slice_in_dim(block, (1 - low) * half, half, 0)
    return mine, other


def sum_between_chips(mine, nrow, ncol):
    bit = 2
    while bit < ncol:
        mine = mine + along_col(mine, bit, nrow, ncol)
        bit *= 2
    return mine


def scatter_between_chips(keep, nrow, ncol):
    bit = ncol // 2
    while bit > 1:
        half = keep.shape[0] // 2
        keep = keep[:half] + along_col(keep[half:], bit, nrow, ncol)
        bit //= 2
    return keep


def to_rows(mine, step, holders, ncol):
    moves = [(r, r + step) for r in holders]
    return along_row(mine, (moves, moves), ncol)


def received(mine, got, step, holders, row):
    hit = jnp.zeros_like(row == 0)
    for r in holders:
        hit = hit | (row == r + step)
    return jnp.where(hit, got, mine)


def rounds(steps):
    holders, result = [0], []
    for step in steps:
        result.append((step, list(holders)))
        holders += [r + step for r in holders]
    return result


def join(mine, bits, nrow, ncol):
    share, wide = mine.shape[-2:]
    mine = mine.reshape(-1, share, wide)
    for bit in bits:
        other = along_col(mine, bit, nrow, ncol)
        low = (lax.axis_index("col") & bit) == 0
        pair = [jnp.where(low, mine, other), jnp.where(low, other, mine)]
        mine = jnp.stack(pair, 1).reshape(-1, share, wide)
    return mine


def own_part(panels, at, end, first, last):
    own = panels.shape[0]
    col = lax.axis_index("col")
    blocks = []
    for c in range(at // own, -(-end // own)):
        low, high = max(at, c * own), min(end, (c + 1) * own)
        blocks.append(jnp.where(col == c, panels[low - c * own : high - c * own, first:last], 0.0))
    return jnp.concatenate(blocks, 0)


def on_device(nrow, ncol, factor, panels):
    own, width = panels.shape
    row, col = lax.axis_index("row"), lax.axis_index("col")
    odd = col % 2
    share = width // PARTS
    place = jnp.stack([row, col]).astype(jnp.int32)
    halves = [nrow >> k for k in range(1, nrow.bit_length())]
    tree_a, tree_b = rounds([1] + halves[:-1]), rounds(halves)
    live = {"own%d" % i: factor[i * share : (i + 1) * share] for i in range(PARTS)}
    pivots = [{} for _ in range(PARTS)]
    fresh = [[] for _ in range(PARTS)]

    def hops(number):
        for i in range(PARTS):
            if 0 <= number - i <= 3:
                new = tree_step(number - i, live["own%d" % i], pivots[i], row, odd, nrow, ncol)
                pivots[i].update(new)
                fresh[i] = [name for name in new if name != "line"]
            else:
                fresh[i] = []

    def update(i, after):
        across = (row > 0) & (row % 2 != odd)
        choices = [pivots[i]["line"], pivots[i]["across"]]
        return update_product(factor, choices, across, col, ncol, after)

    def own_rest(i, keep):
        return panels[:, i * share : (i + 1) * share] - scatter_between_chips(keep, nrow, ncol)

    def top(at, first):
        block = factor[at : at + share], factor[first : first + share]
        return own_part(panels, at, at + share, first, first + share) - nt_dot(*block)

    chip_bits = [ncol >> (k + 1) for k in range(len(bin(ncol)) - 4)]

    def end(extra, number):
        named = dict(extra)
        for i in range(PARTS):
            if i == number + 1:
                named["own%d" % i] = live["own%d" % i]
            for n in fresh[i]:
                named["%s of %d" % (n, i)] = pivots[i][n]
        named = stage_end(named)
        for i in range(PARTS):
            if i == number + 1:
                live["own%d" % i] = named["own%d" % i]
            for n in fresh[i]:
                pivots[i][n] = named["%s of %d" % (n, i)]
        return {n: named[n] for n in extra}

    hops(0)
    mine, other = core_halves(top(0, 0))
    sum_a = sum_between_chips(mine + along_col(other, 1, nrow, ncol), nrow, ncol)
    mine, other = core_halves(jnp.concatenate([top(0, share), top(share, share)], 1))
    got_b = along_col(other, 1, nrow, ncol)
    kept = end({"a": sum_a, "mine": mine, "got": got_b}, 0)
    hops(1)
    sum_a, sum_b = kept["a"], sum_between_chips(kept["mine"] + kept["got"], nrow, ncol)
    pack_a, share_a = panel_factor(place, ncol, share, sum_a, along_col(sum_a, 1, nrow, ncol))
    kept = end({"b": sum_b, "share": share_a}, 1)
    hops(2)
    sum_b = join(kept["b"], [1], nrow, ncol).reshape(share, 2 * share)
    upper = jnp.dot(pack_a, sum_b[:, :share], precision=HIGH)
    block = sum_b[:, share:] - lax.dot_general(upper, upper, (((0,), (0,)), ((), ())), precision=HIGH)
    quarter = share // ncol
    share_a = jnp.concatenate([kept["share"], lax.dynamic_slice_in_dim(upper, col * quarter, quarter, 0)], 1)
    got_a = to_rows(share_a, *tree_a[0], ncol)
    share_b = panel_factor(place, ncol, share, block)[1]
    kept = end({"a": got_a, "b": share_b}, 2)
    hops(3)
    share_a, share_b = received(share_a, kept["a"], *tree_a[0], row), kept["b"]
    got_b, got_a = to_rows(share_b, *tree_b[0], ncol), to_rows(share_a, *tree_a[1], ncol)
    kept = end({"a": got_a, "b": got_b}, 3)
    hops(4)
    share_a, share_b = received(share_a, kept["a"], *tree_a[1], row), received(share_b, kept["b"], *tree_b[0], row)
    for turn in tree_a[2:-1]:
        share_a = received(share_a, to_rows(share_a, *turn, ncol), *turn, row)
    for turn in tree_b[1:-2]:
        share_b = received(share_b, to_rows(share_b, *turn, ncol), *turn, row)
    got_b, got_a = to_rows(share_b, *tree_b[-2], ncol), to_rows(share_a, *tree_a[-1], ncol)
    keep, send = update(0, [pivots[1]["line"]])
    rest_a = own_rest(0, keep + along_col(send, 1, nrow, ncol))
    share_a = join(received(share_a, got_a, *tree_a[-1], row), chip_bits, nrow, ncol)
    kept = end({"a": share_a, "b": got_b, "rest": rest_a}, 4)
    rest_a = kept["rest"]
    share_a = kept["a"]
    share_b = received(share_b, kept["b"], *tree_b[-2], row)
    got_b = to_rows(share_b, *tree_b[-1], ncol)
    keep, send = update(1, [])
    kept = end({"b": got_b, "keep": keep, "got": along_col(send, 1, nrow, ncol)}, 5)
    rest_b = own_rest(1, kept["keep"] + kept["got"])
    pack_a = join(share_a, [1], nrow, ncol).reshape(share, 2 * share)
    pack_b = join(received(share_b, kept["b"], *tree_b[-1], row), chip_bits + [1], nrow, ncol).reshape(share, share)
    out_a = nt_dot(rest_a, pack_a[:, :share], HIGH)
    rest_b = rest_b - jnp.dot(out_a, pack_a[:, share:], precision=HIGH)
    out = [out_a, nt_dot(rest_b, pack_b, HIGH)]
    out = jnp.concatenate(out, 1)
    at_row = lax.broadcasted_iota(jnp.int32, out.shape, 0) + (row * ncol + col) * own
    at_col = lax.broadcasted_iota(jnp.int32, out.shape, 1)
    return jnp.where(at_col <= at_row, out, 0.0)


def solution(mesh):
    return jax.shard_map(
        functools.partial(on_device, mesh.shape["row"], mesh.shape["col"]),
        mesh=mesh,
        in_specs=(P("row", "col"), P(BOTH, None)),
        out_specs=P(BOTH, None),
        check_vma=False,
    )
```

```python
import functools
import jax
import jax.numpy as jnp
from jax import lax
from jax.experimental import pallas as pl
from jax.experimental.pallas import tpu as pltpu
from jax.sharding import PartitionSpec as P

SUB = 8
BLOCK = 128
STEP = 32
PARTS = 2
BOTH = ("row", "col")
HIGH = lax.Precision.HIGHEST


def split(x):
    first = x.astype(jnp.bfloat16)
    rest = x - first.astype(jnp.float32)
    second = rest.astype(jnp.bfloat16)
    return first, second, (rest - second.astype(jnp.float32)).astype(jnp.bfloat16)


def joined_dot(a, b, a_axis):
    a1, a2, a3 = split(a)
    b1, b2, b3 = (a1, a2, a3) if a is b else split(b)
    left = jnp.concatenate([a1, a1, a2, a2, a1, a3], a_axis)
    right = jnp.concatenate([b1, b2, b1, b2, b3, b1], 0)
    return lax.dot_general(left, right, (((a_axis,), (0,)), ((), ())), preferred_element_type=jnp.float32)


def tn_dot(a, b):
    return joined_dot(a, b, 0)


def nn_dot(a, b):
    return joined_dot(a, b, 1)


def row_of(x, k):
    return jnp.broadcast_to(x[k : k + 1, :], x.shape)


def lane_of(x, k):
    return jnp.broadcast_to(x[:, k : k + 1], x.shape)


def inverse_factor(block):
    lane = lax.broadcasted_iota(jnp.int32, (SUB, BLOCK), 1)
    sub = lax.broadcasted_iota(jnp.int32, (SUB, BLOCK), 0)
    groups = [block[SUB * q : SUB * (q + 1), :] for q in range(BLOCK // SUB)]
    per_step = STEP // SUB
    done = []
    for step in range(BLOCK // STEP):
        end = (step + 1) * per_step
        here = []
        for p in range(step * per_step, end):
            first = SUB * p
            inside = (lane >= first) & (lane < first + SUB)
            cols = [lane_of(groups[p], first + k) for k in range(SUB)]
            rows = jnp.where(inside, jnp.where(lane - first == sub, 1.0, 0.0), groups[p])
            scale = jnp.zeros((SUB, BLOCK), jnp.float32)
            col_rows, own_rows = [], []
            for k in range(SUB):
                pivot = row_of(cols[k], k)
                inv = pl.reciprocal(pivot, approx=True)
                scale = jnp.where(sub == k, lax.rsqrt(pivot), scale)
                below = jnp.where(sub > k, cols[k], 0.0)
                raw = [row_of(cols[m], k) for m in range(k + 1, SUB)]
                own = row_of(rows, k) * inv
                for i, m in enumerate(range(k + 1, SUB)):
                    cols[m] = cols[m] - (below * raw[i]) * inv
                rows = rows - below * own
                col_rows.append([r * inv for r in raw])
                own_rows.append(own)
            here.append(rows * scale)
            for q in range(p + 1, end):
                mult = [lane_of(groups[q], first + k) for k in range(SUB)]
                acc = jnp.where(inside, 0.0, groups[q])
                for k in range(SUB):
                    for i, m in enumerate(range(k + 1, SUB)):
                        mult[m] = mult[m] - mult[k] * col_rows[k][i]
                    acc = acc - mult[k] * own_rows[k]
                groups[q] = acc
        span = jnp.concatenate(here, 0)
        base = step * STEP
        span_lane = lax.broadcasted_iota(jnp.int32, (STEP, BLOCK), 1)
        span_row = lax.broadcasted_iota(jnp.int32, (STEP, BLOCK), 0) + base
        span = jnp.where((span_lane <= span_row) | (span_lane >= base + STEP), span, 0.0)
        done.append(jnp.where(span_lane <= span_row, span, 0.0))
        if base + STEP < BLOCK:
            delta = tn_dot(span, span)
            in_step = (lane >= base) & (lane < base + STEP)
            for q in range(end, BLOCK // SUB):
                groups[q] = jnp.where(in_step, 0.0, groups[q]) - delta[SUB * q : SUB * (q + 1), :]
    return jnp.concatenate(done, 0)


def inverse_panel(rest, out_ref):
    size = rest.shape[0]
    uppers, inverses = [], []
    for i in range(size // BLOCK):
        at = i * BLOCK
        inverse = inverse_factor(rest[:BLOCK, :BLOCK])
        line = []
        for j in range(i):
            total = 0.0
            for k in range(j, i):
                block = uppers[k][:, (i - k - 1) * BLOCK : (i - k) * BLOCK]
                total = total + tn_dot(block, inverses[k][j])
            line.append(-nn_dot(inverse, total))
        line.append(inverse)
        inverses.append(line)
        for j, block in enumerate(line):
            out_ref[at : at + BLOCK, j * BLOCK : (j + 1) * BLOCK] = block
        if at + BLOCK < size:
            out_ref[at : at + BLOCK, at + BLOCK :] = jnp.zeros((BLOCK, size - at - BLOCK), jnp.float32)
            uppers.append(nn_dot(inverse, rest[:BLOCK, BLOCK:]))
            rest = rest[BLOCK:, BLOCK:] - tn_dot(uppers[-1], uppers[-1])


def panel_kernel(place_ref, rest_ref, out_ref, share_ref):
    share = share_ref.shape[0]

    @pl.when(place_ref[0] == 0)
    def _():
        inverse_panel(rest_ref[...], out_ref)
        share_ref[...] = out_ref[pl.ds(pl.multiple_of(place_ref[1] * share, share), share), :]


def first_kernel(place_ref, mine_ref, other_ref, out_ref, share_ref, whole):
    half = mine_ref.shape[0]
    low = place_ref[1] % 2

    @pl.when(place_ref[0] == 0)
    def _():
        whole[pl.ds(pl.multiple_of(low * half, half), half), :] = mine_ref[...]
        whole[pl.ds(pl.multiple_of((1 - low) * half, half), half), :] = other_ref[...]

    panel_kernel(place_ref, whole, out_ref, share_ref)


def panel_factor(place, ncol, size, *args):
    vmem = pl.BlockSpec(memory_space=pltpu.VMEM)
    first = args[0].shape[0] < size
    return pl.pallas_call(
        first_kernel if first else panel_kernel,
        out_shape=[
            jax.ShapeDtypeStruct((size, size), jnp.float32),
            jax.ShapeDtypeStruct((size // ncol, size), jnp.float32),
        ],
        in_specs=[pl.BlockSpec(memory_space=pltpu.SMEM)] + [vmem] * len(args),
        out_specs=[vmem, vmem],
        scratch_shapes=[pltpu.VMEM((size, size), jnp.float32)] if first else [],
        compiler_params=pltpu.CompilerParams(vmem_limit_bytes=40 << 20),
        cost_estimate=pl.CostEstimate(flops=2 * 10**10, bytes_accessed=8 * size * size, transcendentals=0),
    )(place, *args)


def nt_dot(a, b, precision=None):
    return lax.dot_general(
        a, b, (((1,), (1,)), ((), ())), precision=precision, preferred_element_type=jnp.float32
    )


def update_kernel(slots, count, order_ref, factor_ref, *refs):
    choices, (keep_ref, send_ref, pivots, sem) = refs[:count], refs[-4:]
    slot = pl.program_id(0)
    for i, choice in enumerate(choices):

        @pl.when((slot == 0) & (order_ref[slots] == i))
        def _():
            copy = pltpu.make_async_copy(choice, pivots, sem)
            copy.start()
            copy.wait()

    product = nt_dot(factor_ref[...], pivots[...])

    @pl.when(slot < slots // 2)
    def _():
        keep_ref[...] = product

    @pl.when(slot >= slots // 2)
    def _():
        send_ref[...] = product


def update_product(factor, choices, which, col, ncol, after):
    rows, depth = factor.shape
    own, count = rows // ncol, choices[0].shape[0]
    half = ncol // 2
    flips = list(range(0, ncol, 2)) + list(range(1, ncol, 2))
    order = jnp.concatenate([col ^ jnp.asarray(flips, jnp.int32), which[None].astype(jnp.int32)])
    out = jax.ShapeDtypeStruct((half * own, count), jnp.float32)
    return pl.pallas_call(
        functools.partial(update_kernel, ncol, len(choices)),
        out_shape=(out, out),
        grid_spec=pltpu.PrefetchScalarGridSpec(
            num_scalar_prefetch=1,
            grid=(ncol,),
            in_specs=[pl.BlockSpec((own, depth), lambda s, order: (order[s], 0))]
            + [pl.BlockSpec(memory_space=pl.ANY)] * (len(choices) + len(after)),
            out_specs=(
                pl.BlockSpec((own, count), lambda s, order: (jnp.minimum(s, half - 1), 0)),
                pl.BlockSpec((own, count), lambda s, order: (jnp.maximum(s - half, 0), 0)),
            ),
            scratch_shapes=[pltpu.VMEM((count, depth), factor.dtype), pltpu.SemaphoreType.DMA],
        ),
        compiler_params=pltpu.CompilerParams(vmem_limit_bytes=40 << 20),
        cost_estimate=pl.CostEstimate(
            flops=2 * rows * depth * count, bytes_accessed=2 * rows * depth + 4 * rows * count, transcendentals=0
        ),
    )(order, factor, *choices, *after)


def stage_end(arrays):
    hbm = pl.BlockSpec(memory_space=pl.ANY)
    names = sorted(arrays)
    results = pl.pallas_call(
        lambda *refs: None,
        out_shape=[jax.ShapeDtypeStruct(arrays[n].shape, arrays[n].dtype) for n in names],
        in_specs=[hbm] * len(names),
        out_specs=[hbm] * len(names),
        input_output_aliases={i: i for i in range(len(names))},
    )(*[arrays[n] for n in names])
    return dict(zip(names, results))


def along_row(block, moves, ncol):
    return lax.ppermute(block, BOTH, [(a * ncol + c, b * ncol + c) for c in range(ncol) for a, b in moves[c % 2]])


def tree_step(step, block, buffers, row, odd, nrow, ncol):
    line = nrow // 2
    new = {}
    if step == 0:
        new["first"] = along_row(block, ([], [(0, 1)]), ncol)
    elif step == 1:
        held = jnp.where(odd == 1, buffers["first"], block)
        new["half"] = along_row(held, both_lines([(0, line // 2)]), ncol)
    elif step == 2:
        held, reach = buffers["half"], line // 4
        while reach:
            ahead = [(p, p + reach) for p in range(2 * reach, line, 2 * reach)]
            new["on%d" % reach] = along_row(held, both_lines(ahead), ncol)
            new["back%d" % reach] = along_row(held, both_lines([(2 * reach, reach)]), ncol)
            if reach > 1:
                place = row // 2
                held = jnp.where(place % (2 * reach) == reach, new["on%d" % reach], held)
                held = jnp.where(place == reach, new["back%d" % reach], held)
            reach //= 2
    else:
        held, place = block, row // 2
        for name in sorted(buffers):
            for p in arrivals(name, line):
                held = jnp.where((row == 1) if name == "first" else (place == p), buffers[name], held)
        buffers.clear()
        new["line"] = held
        even = [(2 * p, 2 * p + 1) for p in range(line)]
        odds = [(2 * p + 1, 2 * p) for p in range(1, line)]
        new["across"] = along_row(held, (even, odds), ncol)
    return new


def both_lines(moves):
    return [(2 * a, 2 * b) for a, b in moves], [(2 * a + 1, 2 * b + 1) for a, b in moves]


def arrivals(name, line):
    if name == "first":
        return [0]
    if name == "half":
        return [line // 2]
    reach = int(name.strip("onback"))
    if name.startswith("on"):
        return [p + reach for p in range(2 * reach, line, 2 * reach)]
    return [reach]


def along_col(block, bit, nrow, ncol):
    return lax.ppermute(block, BOTH, [(r * ncol + c, r * ncol + (c ^ bit)) for r in range(nrow) for c in range(ncol)])


def core_halves(block):
    half = block.shape[0] // 2
    low = lax.axis_index("col") % 2
    mine = lax.dynamic_slice_in_dim(block, low * half, half, 0)
    other = lax.dynamic_slice_in_dim(block, (1 - low) * half, half, 0)
    return mine, other


def sum_between_chips(mine, nrow, ncol):
    bit = 2
    while bit < ncol:
        mine = mine + along_col(mine, bit, nrow, ncol)
        bit *= 2
    return mine


def scatter_between_chips(keep, nrow, ncol):
    bit = ncol // 2
    while bit > 1:
        half = keep.shape[0] // 2
        keep = keep[:half] + along_col(keep[half:], bit, nrow, ncol)
        bit //= 2
    return keep


def to_rows(mine, step, holders, ncol):
    moves = [(r, r + step) for r in holders]
    return along_row(mine, (moves, moves), ncol)


def received(mine, got, step, holders, row):
    hit = jnp.zeros_like(row == 0)
    for r in holders:
        hit = hit | (row == r + step)
    return jnp.where(hit, got, mine)


def rounds(steps):
    holders, result = [0], []
    for step in steps:
        result.append((step, list(holders)))
        holders += [r + step for r in holders]
    return result


def join(mine, bits, nrow, ncol):
    share, wide = mine.shape[-2:]
    mine = mine.reshape(-1, share, wide)
    for bit in bits:
        other = along_col(mine, bit, nrow, ncol)
        low = (lax.axis_index("col") & bit) == 0
        pair = [jnp.where(low, mine, other), jnp.where(low, other, mine)]
        mine = jnp.stack(pair, 1).reshape(-1, share, wide)
    return mine


def own_part(panels, at, end, first, last):
    own = panels.shape[0]
    col = lax.axis_index("col")
    blocks = []
    for c in range(at // own, -(-end // own)):
        low, high = max(at, c * own), min(end, (c + 1) * own)
        blocks.append(jnp.where(col == c, panels[low - c * own : high - c * own, first:last], 0.0))
    return jnp.concatenate(blocks, 0)


def on_device(nrow, ncol, factor, panels):
    own, width = panels.shape
    row, col = lax.axis_index("row"), lax.axis_index("col")
    odd = col % 2
    share = width // PARTS
    place = jnp.stack([row, col]).astype(jnp.int32)
    halves = [nrow >> k for k in range(1, nrow.bit_length())]
    tree_a, tree_b = rounds([1] + halves[:-1]), rounds(halves)
    live = {"own%d" % i: factor[i * share : (i + 1) * share] for i in range(PARTS)}
    pivots = [{} for _ in range(PARTS)]
    fresh = [[] for _ in range(PARTS)]

    def hops(number):
        for i in range(PARTS):
            if 0 <= number - i <= 3:
                new = tree_step(number - i, live["own%d" % i], pivots[i], row, odd, nrow, ncol)
                pivots[i].update(new)
                fresh[i] = [name for name in new if name != "line"]
            else:
                fresh[i] = []

    def update(i, after):
        across = (row > 0) & (row % 2 != odd)
        choices = [pivots[i]["line"], pivots[i]["across"]]
        return update_product(factor, choices, across, col, ncol, after)

    def own_rest(i, keep):
        return panels[:, i * share : (i + 1) * share] - scatter_between_chips(keep, nrow, ncol)

    def top(at, end_row, first):
        block = factor[at:end_row], factor[first : first + share]
        return own_part(panels, at, end_row, first, first + share) - nt_dot(*block)

    chip_bits = [ncol >> (k + 1) for k in range(len(bin(ncol)) - 4)]

    def end(extra, number):
        named = dict(extra)
        for i in range(PARTS):
            if i == number + 1:
                named["own%d" % i] = live["own%d" % i]
            for n in fresh[i]:
                named["%s of %d" % (n, i)] = pivots[i][n]
        named = stage_end(named)
        for i in range(PARTS):
            if i == number + 1:
                live["own%d" % i] = named["own%d" % i]
            for n in fresh[i]:
                pivots[i][n] = named["%s of %d" % (n, i)]
        return {n: named[n] for n in extra}

    hops(0)
    mine, other = core_halves(top(0, share, 0))
    sum_a = sum_between_chips(mine + along_col(other, 1, nrow, ncol), nrow, ncol)
    mine, other = core_halves(top(0, width, share))
    got_b = along_col(other, 1, nrow, ncol)
    kept = end({"a": sum_a, "mine": mine, "got": got_b}, 0)
    hops(1)
    sum_a, sum_b = kept["a"], sum_between_chips(kept["mine"] + kept["got"], nrow, ncol)
    pack_a, share_a = panel_factor(place, ncol, share, sum_a, along_col(sum_a, 1, nrow, ncol))
    kept = end({"b": sum_b, "share": share_a}, 1)
    hops(2)
    mine, other = kept["b"], along_col(kept["b"], 1, nrow, ncol)
    upper = jnp.dot(pack_a, jnp.where(odd == 0, mine, other), precision=HIGH)
    block = jnp.where(odd == 0, other, mine) - lax.dot_general(upper, upper, (((0,), (0,)), ((), ())), precision=HIGH)
    quarter = share // ncol
    share_a = jnp.concatenate([kept["share"], lax.dynamic_slice_in_dim(upper, col * quarter, quarter, 0)], 1)
    got_a = to_rows(share_a, *tree_a[0], ncol)
    share_b = panel_factor(place, ncol, share, block)[1]
    kept = end({"a": got_a, "b": share_b}, 2)
    hops(3)
    share_a, share_b = received(share_a, kept["a"], *tree_a[0], row), kept["b"]
    got_b, got_a = to_rows(share_b, *tree_b[0], ncol), to_rows(share_a, *tree_a[1], ncol)
    kept = end({"a": got_a, "b": got_b}, 3)
    hops(4)
    share_a, share_b = received(share_a, kept["a"], *tree_a[1], row), received(share_b, kept["b"], *tree_b[0], row)
    for turn in tree_a[2:-1]:
        share_a = received(share_a, to_rows(share_a, *turn, ncol), *turn, row)
    for turn in tree_b[1:-2]:
        share_b = received(share_b, to_rows(share_b, *turn, ncol), *turn, row)
    got_a = to_rows(share_a, *tree_a[-1], ncol)
    share_b = received(share_b, to_rows(share_b, *tree_b[-2], ncol), *tree_b[-2], row)
    got_b = to_rows(share_b, *tree_b[-1], ncol)
    keep, send = update(0, [pivots[1]["line"]])
    rest_a = own_rest(0, keep + along_col(send, 1, nrow, ncol))
    share_a = join(received(share_a, got_a, *tree_a[-1], row), chip_bits, nrow, ncol)
    kept = end({"a": share_a, "b": got_b}, 4)
    share_a = kept["a"]
    share_b = join(received(share_b, kept["b"], *tree_b[-1], row), chip_bits, nrow, ncol)
    keep, send = update(1, [])
    kept = end({"b": share_b, "keep": keep, "got": along_col(send, 1, nrow, ncol)}, 5)
    rest_b = own_rest(1, kept["keep"] + kept["got"])
    pack_a = join(share_a, [1], nrow, ncol).reshape(share, 2 * share)
    pack_b = join(kept["b"], [1], nrow, ncol).reshape(share, share)
    out_a = nt_dot(rest_a, pack_a[:, :share], HIGH)
    rest_b = rest_b - jnp.dot(out_a, pack_a[:, share:], precision=HIGH)
    out = [out_a, nt_dot(rest_b, pack_b, HIGH)]
    out = jnp.concatenate(out, 1)
    at_row = lax.broadcasted_iota(jnp.int32, out.shape, 0) + (row * ncol + col) * own
    at_col = lax.broadcasted_iota(jnp.int32, out.shape, 1)
    return jnp.where(at_col <= at_row, out, 0.0)


def solution(mesh):
    return jax.shard_map(
        functools.partial(on_device, mesh.shape["row"], mesh.shape["col"]),
        mesh=mesh,
        in_specs=(P("row", "col"), P(BOTH, None)),
        out_specs=P(BOTH, None),
        check_vma=False,
    )
```

```python
import functools
import jax
import jax.numpy as jnp
from jax import lax
from jax.experimental import pallas as pl
from jax.experimental.pallas import tpu as pltpu
from jax.sharding import PartitionSpec as P

SUB = 8
BLOCK = 128
STEP = 32
PARTS = 2
BOTH = ("row", "col")
HIGH = lax.Precision.HIGHEST


def split(x):
    first = x.astype(jnp.bfloat16)
    rest = x - first.astype(jnp.float32)
    second = rest.astype(jnp.bfloat16)
    return first, second, (rest - second.astype(jnp.float32)).astype(jnp.bfloat16)


def joined_dot(a, b, a_axis):
    a1, a2, a3 = split(a)
    b1, b2, b3 = (a1, a2, a3) if a is b else split(b)
    left = jnp.concatenate([a1, a1, a2, a2, a1, a3], a_axis)
    right = jnp.concatenate([b1, b2, b1, b2, b3, b1], 0)
    return lax.dot_general(left, right, (((a_axis,), (0,)), ((), ())), preferred_element_type=jnp.float32)


def tn_dot(a, b):
    return joined_dot(a, b, 0)


def nn_dot(a, b):
    return joined_dot(a, b, 1)


def row_of(x, k):
    return jnp.broadcast_to(x[k : k + 1, :], x.shape)


def lane_of(x, k):
    return jnp.broadcast_to(x[:, k : k + 1], x.shape)


def inverse_factor(block):
    lane = lax.broadcasted_iota(jnp.int32, (SUB, BLOCK), 1)
    sub = lax.broadcasted_iota(jnp.int32, (SUB, BLOCK), 0)
    groups = [block[SUB * q : SUB * (q + 1), :] for q in range(BLOCK // SUB)]
    per_step = STEP // SUB
    done = []
    for step in range(BLOCK // STEP):
        end = (step + 1) * per_step
        here = []
        for p in range(step * per_step, end):
            first = SUB * p
            inside = (lane >= first) & (lane < first + SUB)
            cols = [lane_of(groups[p], first + k) for k in range(SUB)]
            rows = jnp.where(inside, jnp.where(lane - first == sub, 1.0, 0.0), groups[p])
            scale = jnp.zeros((SUB, BLOCK), jnp.float32)
            col_rows, own_rows = [], []
            for k in range(SUB):
                pivot = row_of(cols[k], k)
                inv = pl.reciprocal(pivot, approx=True)
                scale = jnp.where(sub == k, lax.rsqrt(pivot), scale)
                below = jnp.where(sub > k, cols[k], 0.0)
                raw = [row_of(cols[m], k) for m in range(k + 1, SUB)]
                own = row_of(rows, k) * inv
                for i, m in enumerate(range(k + 1, SUB)):
                    cols[m] = cols[m] - (below * raw[i]) * inv
                rows = rows - below * own
                col_rows.append([r * inv for r in raw])
                own_rows.append(own)
            here.append(rows * scale)
            for q in range(p + 1, end):
                mult = [lane_of(groups[q], first + k) for k in range(SUB)]
                acc = jnp.where(inside, 0.0, groups[q])
                for k in range(SUB):
                    for i, m in enumerate(range(k + 1, SUB)):
                        mult[m] = mult[m] - mult[k] * col_rows[k][i]
                    acc = acc - mult[k] * own_rows[k]
                groups[q] = acc
        span = jnp.concatenate(here, 0)
        base = step * STEP
        span_lane = lax.broadcasted_iota(jnp.int32, (STEP, BLOCK), 1)
        span_row = lax.broadcasted_iota(jnp.int32, (STEP, BLOCK), 0) + base
        span = jnp.where((span_lane <= span_row) | (span_lane >= base + STEP), span, 0.0)
        done.append(jnp.where(span_lane <= span_row, span, 0.0))
        if base + STEP < BLOCK:
            delta = tn_dot(span, span)
            in_step = (lane >= base) & (lane < base + STEP)
            for q in range(end, BLOCK // SUB):
                groups[q] = jnp.where(in_step, 0.0, groups[q]) - delta[SUB * q : SUB * (q + 1), :]
    return jnp.concatenate(done, 0)


def inverse_panel(rest, out_ref):
    size = rest.shape[0]
    uppers, inverses = [], []
    for i in range(size // BLOCK):
        at = i * BLOCK
        inverse = inverse_factor(rest[:BLOCK, :BLOCK])
        line = []
        for j in range(i):
            total = 0.0
            for k in range(j, i):
                block = uppers[k][:, (i - k - 1) * BLOCK : (i - k) * BLOCK]
                total = total + tn_dot(block, inverses[k][j])
            line.append(-nn_dot(inverse, total))
        line.append(inverse)
        inverses.append(line)
        for j, block in enumerate(line):
            out_ref[at : at + BLOCK, j * BLOCK : (j + 1) * BLOCK] = block
        if at + BLOCK < size:
            out_ref[at : at + BLOCK, at + BLOCK :] = jnp.zeros((BLOCK, size - at - BLOCK), jnp.float32)
            uppers.append(nn_dot(inverse, rest[:BLOCK, BLOCK:]))
            rest = rest[BLOCK:, BLOCK:] - tn_dot(uppers[-1], uppers[-1])


def panel_kernel(place_ref, rest_ref, out_ref, share_ref):
    share = share_ref.shape[0]

    @pl.when(place_ref[0] == 0)
    def _():
        inverse_panel(rest_ref[...], out_ref)
        share_ref[...] = out_ref[pl.ds(pl.multiple_of(place_ref[1] * share, share), share), :]


def first_kernel(place_ref, mine_ref, other_ref, out_ref, share_ref, whole):
    half = mine_ref.shape[0]
    low = place_ref[1] % 2

    @pl.when(place_ref[0] == 0)
    def _():
        whole[pl.ds(pl.multiple_of(low * half, half), half), :] = mine_ref[...]
        whole[pl.ds(pl.multiple_of((1 - low) * half, half), half), :] = other_ref[...]

    panel_kernel(place_ref, whole, out_ref, share_ref)


def panel_factor(place, ncol, size, *args):
    vmem = pl.BlockSpec(memory_space=pltpu.VMEM)
    first = args[0].shape[0] < size
    return pl.pallas_call(
        first_kernel if first else panel_kernel,
        out_shape=[
            jax.ShapeDtypeStruct((size, size), jnp.float32),
            jax.ShapeDtypeStruct((size // ncol, size), jnp.float32),
        ],
        in_specs=[pl.BlockSpec(memory_space=pltpu.SMEM)] + [vmem] * len(args),
        out_specs=[vmem, vmem],
        scratch_shapes=[pltpu.VMEM((size, size), jnp.float32)] if first else [],
        compiler_params=pltpu.CompilerParams(vmem_limit_bytes=40 << 20),
        cost_estimate=pl.CostEstimate(flops=2 * 10**10, bytes_accessed=8 * size * size, transcendentals=0),
    )(place, *args)


def nt_dot(a, b, precision=None):
    return lax.dot_general(
        a, b, (((1,), (1,)), ((), ())), precision=precision, preferred_element_type=jnp.float32
    )


def update_kernel(slots, count, order_ref, factor_ref, *refs):
    choices, (keep_ref, send_ref, pivots, sem) = refs[:count], refs[-4:]
    slot = pl.program_id(0)
    for i, choice in enumerate(choices):

        @pl.when((slot == 0) & (order_ref[slots] == i))
        def _():
            copy = pltpu.make_async_copy(choice, pivots, sem)
            copy.start()
            copy.wait()

    product = nt_dot(factor_ref[...], pivots[...])

    @pl.when(slot < slots // 2)
    def _():
        keep_ref[...] = product

    @pl.when(slot >= slots // 2)
    def _():
        send_ref[...] = product


def update_product(factor, choices, which, col, ncol, after):
    rows, depth = factor.shape
    own, count = rows // ncol, choices[0].shape[0]
    half = ncol // 2
    flips = list(range(0, ncol, 2)) + list(range(1, ncol, 2))
    order = jnp.concatenate([col ^ jnp.asarray(flips, jnp.int32), which[None].astype(jnp.int32)])
    out = jax.ShapeDtypeStruct((half * own, count), jnp.float32)
    return pl.pallas_call(
        functools.partial(update_kernel, ncol, len(choices)),
        out_shape=(out, out),
        grid_spec=pltpu.PrefetchScalarGridSpec(
            num_scalar_prefetch=1,
            grid=(ncol,),
            in_specs=[pl.BlockSpec((own, depth), lambda s, order: (order[s], 0))]
            + [pl.BlockSpec(memory_space=pl.ANY)] * (len(choices) + len(after)),
            out_specs=(
                pl.BlockSpec((own, count), lambda s, order: (jnp.minimum(s, half - 1), 0)),
                pl.BlockSpec((own, count), lambda s, order: (jnp.maximum(s - half, 0), 0)),
            ),
            scratch_shapes=[pltpu.VMEM((count, depth), factor.dtype), pltpu.SemaphoreType.DMA],
        ),
        compiler_params=pltpu.CompilerParams(vmem_limit_bytes=60 << 20),
        cost_estimate=pl.CostEstimate(
            flops=2 * rows * depth * count, bytes_accessed=2 * rows * depth + 4 * rows * count, transcendentals=0
        ),
    )(order, factor, *choices, *after)


def stage_end(arrays):
    hbm = pl.BlockSpec(memory_space=pl.ANY)
    names = sorted(arrays)
    results = pl.pallas_call(
        lambda *refs: None,
        out_shape=[jax.ShapeDtypeStruct(arrays[n].shape, arrays[n].dtype) for n in names],
        in_specs=[hbm] * len(names),
        out_specs=[hbm] * len(names),
        input_output_aliases={i: i for i in range(len(names))},
    )(*[arrays[n] for n in names])
    return dict(zip(names, results))


def along_row(block, moves, ncol):
    return lax.ppermute(block, BOTH, [(a * ncol + c, b * ncol + c) for c in range(ncol) for a, b in moves[c % 2]])


def tree_step(step, block, buffers, row, odd, nrow, ncol):
    line = nrow // 2
    new = {}
    if step == 0:
        new["first"] = along_row(block, ([], [(0, 1)]), ncol)
    elif step == 1:
        held = jnp.where(odd == 1, buffers["first"], block)
        new["half"] = along_row(held, both_lines([(0, line // 2)]), ncol)
    elif step == 2:
        held, reach = buffers["half"], line // 4
        while reach:
            ahead = [(p, p + reach) for p in range(2 * reach, line, 2 * reach)]
            new["on%d" % reach] = along_row(held, both_lines(ahead), ncol)
            new["back%d" % reach] = along_row(held, both_lines([(2 * reach, reach)]), ncol)
            if reach > 1:
                place = row // 2
                held = jnp.where(place % (2 * reach) == reach, new["on%d" % reach], held)
                held = jnp.where(place == reach, new["back%d" % reach], held)
            reach //= 2
    else:
        held, place = block, row // 2
        for name in sorted(buffers):
            for p in arrivals(name, line):
                held = jnp.where((row == 1) if name == "first" else (place == p), buffers[name], held)
        buffers.clear()
        new["line"] = held
        even = [(2 * p, 2 * p + 1) for p in range(line)]
        odds = [(2 * p + 1, 2 * p) for p in range(1, line)]
        new["across"] = along_row(held, (even, odds), ncol)
    return new


def both_lines(moves):
    return [(2 * a, 2 * b) for a, b in moves], [(2 * a + 1, 2 * b + 1) for a, b in moves]


def arrivals(name, line):
    if name == "first":
        return [0]
    if name == "half":
        return [line // 2]
    reach = int(name.strip("onback"))
    if name.startswith("on"):
        return [p + reach for p in range(2 * reach, line, 2 * reach)]
    return [reach]


def along_col(block, bit, nrow, ncol):
    return lax.ppermute(block, BOTH, [(r * ncol + c, r * ncol + (c ^ bit)) for r in range(nrow) for c in range(ncol)])


def core_halves(block):
    half = block.shape[0] // 2
    low = lax.axis_index("col") % 2
    mine = lax.dynamic_slice_in_dim(block, low * half, half, 0)
    other = lax.dynamic_slice_in_dim(block, (1 - low) * half, half, 0)
    return mine, other


def sum_between_chips(mine, nrow, ncol):
    bit = 2
    while bit < ncol:
        mine = mine + along_col(mine, bit, nrow, ncol)
        bit *= 2
    return mine


def scatter_between_chips(keep, nrow, ncol):
    bit = ncol // 2
    while bit > 1:
        half = keep.shape[0] // 2
        keep = keep[:half] + along_col(keep[half:], bit, nrow, ncol)
        bit //= 2
    return keep


def to_rows(mine, step, holders, ncol):
    moves = [(r, r + step) for r in holders]
    return along_row(mine, (moves, moves), ncol)


def received(mine, got, step, holders, row):
    hit = jnp.zeros_like(row == 0)
    for r in holders:
        hit = hit | (row == r + step)
    return jnp.where(hit, got, mine)


def rounds(steps):
    holders, result = [0], []
    for step in steps:
        result.append((step, list(holders)))
        holders += [r + step for r in holders]
    return result


def join(mine, bits, nrow, ncol):
    share, wide = mine.shape[-2:]
    mine = mine.reshape(-1, share, wide)
    for bit in bits:
        other = along_col(mine, bit, nrow, ncol)
        low = (lax.axis_index("col") & bit) == 0
        pair = [jnp.where(low, mine, other), jnp.where(low, other, mine)]
        mine = jnp.stack(pair, 1).reshape(-1, share, wide)
    return mine


def own_part(panels, at, end, first, last):
    own = panels.shape[0]
    col = lax.axis_index("col")
    blocks = []
    for c in range(at // own, -(-end // own)):
        low, high = max(at, c * own), min(end, (c + 1) * own)
        blocks.append(jnp.where(col == c, panels[low - c * own : high - c * own, first:last], 0.0))
    return jnp.concatenate(blocks, 0)


def on_device(nrow, ncol, factor, panels):
    own, width = panels.shape
    row, col = lax.axis_index("row"), lax.axis_index("col")
    odd = col % 2
    share = width // PARTS
    place = jnp.stack([row, col]).astype(jnp.int32)
    halves = [nrow >> k for k in range(1, nrow.bit_length())]
    tree_a, tree_b = rounds([1] + halves[:-1]), rounds(halves)
    live = {"own%d" % i: factor[i * share : (i + 1) * share] for i in range(PARTS)}
    pivots = [{} for _ in range(PARTS)]
    fresh = [[] for _ in range(PARTS)]

    def hops(number):
        for i in range(PARTS):
            if 0 <= number - i <= 3:
                new = tree_step(number - i, live["own%d" % i], pivots[i], row, odd, nrow, ncol)
                pivots[i].update(new)
                fresh[i] = [name for name in new if name != "line"]
            else:
                fresh[i] = []

    def update(i, after):
        across = (row > 0) & (row % 2 != odd)
        choices = [pivots[i]["line"], pivots[i]["across"]]
        return update_product(factor, choices, across, col, ncol, after)

    def own_rest(i, keep):
        return panels[:, i * share : (i + 1) * share] - scatter_between_chips(keep, nrow, ncol)

    def top(at, end_row, first):
        block = factor[at:end_row], factor[first : first + share]
        return own_part(panels, at, end_row, first, first + share) - nt_dot(*block)

    chip_bits = [ncol >> (k + 1) for k in range(len(bin(ncol)) - 4)]

    def end(extra, number):
        named = dict(extra)
        for i in range(PARTS):
            if i == number + 1:
                named["own%d" % i] = live["own%d" % i]
            for n in fresh[i]:
                named["%s of %d" % (n, i)] = pivots[i][n]
        named = stage_end(named)
        for i in range(PARTS):
            if i == number + 1:
                live["own%d" % i] = named["own%d" % i]
            for n in fresh[i]:
                pivots[i][n] = named["%s of %d" % (n, i)]
        return {n: named[n] for n in extra}

    hops(0)
    mine, other = core_halves(top(0, share, 0))
    sum_a = sum_between_chips(mine + along_col(other, 1, nrow, ncol), nrow, ncol)
    mine, other = core_halves(top(0, width, share))
    got_b = along_col(other, 1, nrow, ncol)
    kept = end({"a": sum_a, "mine": mine, "got": got_b}, 0)
    hops(1)
    sum_a, sum_b = kept["a"], sum_between_chips(kept["mine"] + kept["got"], nrow, ncol)
    pack_a, share_a = panel_factor(place, ncol, share, sum_a, along_col(sum_a, 1, nrow, ncol))
    kept = end({"b": sum_b, "share": share_a}, 1)
    hops(2)
    mine, other = kept["b"], along_col(kept["b"], 1, nrow, ncol)
    upper = jnp.dot(pack_a, jnp.where(odd == 0, mine, other), precision=HIGH)
    block = jnp.where(odd == 0, other, mine) - lax.dot_general(upper, upper, (((0,), (0,)), ((), ())), precision=HIGH)
    quarter = share // ncol
    share_a = jnp.concatenate([kept["share"], lax.dynamic_slice_in_dim(upper, col * quarter, quarter, 0)], 1)
    got_a = to_rows(share_a, *tree_a[0], ncol)
    share_b = panel_factor(place, ncol, share, block)[1]
    kept = end({"a": got_a, "b": share_b}, 2)
    hops(3)
    share_a, share_b = received(share_a, kept["a"], *tree_a[0], row), kept["b"]
    got_b, got_a = to_rows(share_b, *tree_b[0], ncol), to_rows(share_a, *tree_a[1], ncol)
    kept = end({"a": got_a, "b": got_b}, 3)
    hops(4)
    share_a, share_b = received(share_a, kept["a"], *tree_a[1], row), received(share_b, kept["b"], *tree_b[0], row)
    for turn in tree_a[2:-1]:
        share_a = received(share_a, to_rows(share_a, *turn, ncol), *turn, row)
    for turn in tree_b[1:-2]:
        share_b = received(share_b, to_rows(share_b, *turn, ncol), *turn, row)
    got_a = to_rows(share_a, *tree_a[-1], ncol)
    share_b = received(share_b, to_rows(share_b, *tree_b[-2], ncol), *tree_b[-2], row)
    got_b = to_rows(share_b, *tree_b[-1], ncol)
    keep, send = update(0, [pivots[1]["line"]])
    rest_a = own_rest(0, keep + along_col(send, 1, nrow, ncol))
    share_a = join(received(share_a, got_a, *tree_a[-1], row), chip_bits, nrow, ncol)
    kept = end({"a": share_a, "b": got_b, "rest": rest_a}, 4)
    rest_a, share_a = kept["rest"], kept["a"]
    share_b = join(received(share_b, kept["b"], *tree_b[-1], row), chip_bits, nrow, ncol)
    keep, send = update(1, [])
    kept = end({"b": share_b, "keep": keep, "got": along_col(send, 1, nrow, ncol)}, 5)
    rest_b = own_rest(1, kept["keep"] + kept["got"])
    pack_a = join(share_a, [1], nrow, ncol).reshape(share, 2 * share)
    pack_b = join(kept["b"], [1], nrow, ncol).reshape(share, share)
    out_a = nt_dot(rest_a, pack_a[:, :share], HIGH)
    rest_b = rest_b - jnp.dot(out_a, pack_a[:, share:], precision=HIGH)
    out = [out_a, nt_dot(rest_b, pack_b, HIGH)]
    out = jnp.concatenate(out, 1)
    at_row = lax.broadcasted_iota(jnp.int32, out.shape, 0) + (row * ncol + col) * own
    at_col = lax.broadcasted_iota(jnp.int32, out.shape, 1)
    return jnp.where(at_col <= at_row, out, 0.0)


def solution(mesh):
    return jax.shard_map(
        functools.partial(on_device, mesh.shape["row"], mesh.shape["col"]),
        mesh=mesh,
        in_specs=(P("row", "col"), P(BOTH, None)),
        out_specs=P(BOTH, None),
        check_vma=False,
    )
```

```python
import functools
import jax
import jax.numpy as jnp
from jax import lax
from jax.experimental import pallas as pl
from jax.experimental.pallas import tpu as pltpu
from jax.sharding import PartitionSpec as P

SUB = 8
BLOCK = 128
STEP = 32
PARTS = 2
BOTH = ("row", "col")
HIGH = lax.Precision.HIGHEST


def split(x):
    first = x.astype(jnp.bfloat16)
    rest = x - first.astype(jnp.float32)
    second = rest.astype(jnp.bfloat16)
    return first, second, (rest - second.astype(jnp.float32)).astype(jnp.bfloat16)


def joined_dot(a, b, a_axis):
    a1, a2, a3 = split(a)
    b1, b2, b3 = (a1, a2, a3) if a is b else split(b)
    left = jnp.concatenate([a1, a1, a2, a2, a1, a3], a_axis)
    right = jnp.concatenate([b1, b2, b1, b2, b3, b1], 0)
    return lax.dot_general(left, right, (((a_axis,), (0,)), ((), ())), preferred_element_type=jnp.float32)


def tn_dot(a, b):
    return joined_dot(a, b, 0)


def nn_dot(a, b):
    return joined_dot(a, b, 1)


def row_of(x, k):
    return jnp.broadcast_to(x[k : k + 1, :], x.shape)


def lane_of(x, k):
    return jnp.broadcast_to(x[:, k : k + 1], x.shape)


def inverse_factor(block):
    lane = lax.broadcasted_iota(jnp.int32, (SUB, BLOCK), 1)
    sub = lax.broadcasted_iota(jnp.int32, (SUB, BLOCK), 0)
    groups = [block[SUB * q : SUB * (q + 1), :] for q in range(BLOCK // SUB)]
    per_step = STEP // SUB
    done = []
    for step in range(BLOCK // STEP):
        end = (step + 1) * per_step
        here = []
        for p in range(step * per_step, end):
            first = SUB * p
            inside = (lane >= first) & (lane < first + SUB)
            cols = [lane_of(groups[p], first + k) for k in range(SUB)]
            rows = jnp.where(inside, jnp.where(lane - first == sub, 1.0, 0.0), groups[p])
            scale = jnp.zeros((SUB, BLOCK), jnp.float32)
            col_rows, own_rows = [], []
            for k in range(SUB):
                pivot = row_of(cols[k], k)
                inv = pl.reciprocal(pivot, approx=True)
                scale = jnp.where(sub == k, lax.rsqrt(pivot), scale)
                below = jnp.where(sub > k, cols[k], 0.0)
                raw = [row_of(cols[m], k) for m in range(k + 1, SUB)]
                own = row_of(rows, k) * inv
                for i, m in enumerate(range(k + 1, SUB)):
                    cols[m] = cols[m] - (below * raw[i]) * inv
                rows = rows - below * own
                col_rows.append([r * inv for r in raw])
                own_rows.append(own)
            here.append(rows * scale)
            for q in range(p + 1, end):
                mult = [lane_of(groups[q], first + k) for k in range(SUB)]
                acc = jnp.where(inside, 0.0, groups[q])
                for k in range(SUB):
                    for i, m in enumerate(range(k + 1, SUB)):
                        mult[m] = mult[m] - mult[k] * col_rows[k][i]
                    acc = acc - mult[k] * own_rows[k]
                groups[q] = acc
        span = jnp.concatenate(here, 0)
        base = step * STEP
        span_lane = lax.broadcasted_iota(jnp.int32, (STEP, BLOCK), 1)
        span_row = lax.broadcasted_iota(jnp.int32, (STEP, BLOCK), 0) + base
        span = jnp.where((span_lane <= span_row) | (span_lane >= base + STEP), span, 0.0)
        done.append(jnp.where(span_lane <= span_row, span, 0.0))
        if base + STEP < BLOCK:
            delta = tn_dot(span, span)
            in_step = (lane >= base) & (lane < base + STEP)
            for q in range(end, BLOCK // SUB):
                groups[q] = jnp.where(in_step, 0.0, groups[q]) - delta[SUB * q : SUB * (q + 1), :]
    return jnp.concatenate(done, 0)


def inverse_panel(rest, out_ref):
    size = rest.shape[0]
    uppers, inverses = [], []
    for i in range(size // BLOCK):
        at = i * BLOCK
        inverse = inverse_factor(rest[:BLOCK, :BLOCK])
        line = []
        for j in range(i):
            total = 0.0
            for k in range(j, i):
                block = uppers[k][:, (i - k - 1) * BLOCK : (i - k) * BLOCK]
                total = total + tn_dot(block, inverses[k][j])
            line.append(-nn_dot(inverse, total))
        line.append(inverse)
        inverses.append(line)
        for j, block in enumerate(line):
            out_ref[at : at + BLOCK, j * BLOCK : (j + 1) * BLOCK] = block
        if at + BLOCK < size:
            out_ref[at : at + BLOCK, at + BLOCK :] = jnp.zeros((BLOCK, size - at - BLOCK), jnp.float32)
            uppers.append(nn_dot(inverse, rest[:BLOCK, BLOCK:]))
            rest = rest[BLOCK:, BLOCK:] - tn_dot(uppers[-1], uppers[-1])


def panel_kernel(place_ref, rest_ref, out_ref, share_ref):
    share = share_ref.shape[0]

    @pl.when(place_ref[0] == 0)
    def _():
        inverse_panel(rest_ref[...], out_ref)
        share_ref[...] = out_ref[pl.ds(pl.multiple_of(place_ref[1] * share, share), share), :]


def first_kernel(place_ref, mine_ref, other_ref, out_ref, share_ref, whole):
    half = mine_ref.shape[0]
    low = place_ref[1] % 2

    @pl.when(place_ref[0] == 0)
    def _():
        whole[pl.ds(pl.multiple_of(low * half, half), half), :] = mine_ref[...]
        whole[pl.ds(pl.multiple_of((1 - low) * half, half), half), :] = other_ref[...]

    panel_kernel(place_ref, whole, out_ref, share_ref)


def panel_factor(place, ncol, size, *args):
    vmem = pl.BlockSpec(memory_space=pltpu.VMEM)
    first = args[0].shape[0] < size
    return pl.pallas_call(
        first_kernel if first else panel_kernel,
        out_shape=[
            jax.ShapeDtypeStruct((size, size), jnp.float32),
            jax.ShapeDtypeStruct((size // ncol, size), jnp.float32),
        ],
        in_specs=[pl.BlockSpec(memory_space=pltpu.SMEM)] + [vmem] * len(args),
        out_specs=[vmem, vmem],
        scratch_shapes=[pltpu.VMEM((size, size), jnp.float32)] if first else [],
        compiler_params=pltpu.CompilerParams(vmem_limit_bytes=40 << 20),
        cost_estimate=pl.CostEstimate(flops=2 * 10**10, bytes_accessed=8 * size * size, transcendentals=0),
    )(place, *args)


def nt_dot(a, b, precision=None):
    return lax.dot_general(
        a, b, (((1,), (1,)), ((), ())), precision=precision, preferred_element_type=jnp.float32
    )


def update_kernel(slots, count, order_ref, factor_ref, *refs):
    choices, (keep_ref, send_ref, pivots, sem) = refs[:count], refs[-4:]
    slot = pl.program_id(0)
    for i, choice in enumerate(choices):

        @pl.when((slot == 0) & (order_ref[slots] == i))
        def _():
            copy = pltpu.make_async_copy(choice, pivots, sem)
            copy.start()
            copy.wait()

    product = nt_dot(factor_ref[...], pivots[...])

    @pl.when(slot < slots // 2)
    def _():
        keep_ref[...] = product

    @pl.when(slot >= slots // 2)
    def _():
        send_ref[...] = product


def update_product(factor, choices, which, col, ncol, after):
    rows, depth = factor.shape
    own, count = rows // ncol, choices[0].shape[0]
    half = ncol // 2
    flips = list(range(0, ncol, 2)) + list(range(1, ncol, 2))
    order = jnp.concatenate([col ^ jnp.asarray(flips, jnp.int32), which[None].astype(jnp.int32)])
    out = jax.ShapeDtypeStruct((half * own, count), jnp.float32)
    return pl.pallas_call(
        functools.partial(update_kernel, ncol, len(choices)),
        out_shape=(out, out),
        grid_spec=pltpu.PrefetchScalarGridSpec(
            num_scalar_prefetch=1,
            grid=(ncol,),
            in_specs=[pl.BlockSpec((own, depth), lambda s, order: (order[s], 0))]
            + [pl.BlockSpec(memory_space=pl.ANY)] * (len(choices) + len(after)),
            out_specs=(
                pl.BlockSpec((own, count), lambda s, order: (jnp.minimum(s, half - 1), 0)),
                pl.BlockSpec((own, count), lambda s, order: (jnp.maximum(s - half, 0), 0)),
            ),
            scratch_shapes=[pltpu.VMEM((count, depth), factor.dtype), pltpu.SemaphoreType.DMA],
        ),
        compiler_params=pltpu.CompilerParams(vmem_limit_bytes=40 << 20),
        cost_estimate=pl.CostEstimate(
            flops=2 * rows * depth * count, bytes_accessed=2 * rows * depth + 4 * rows * count, transcendentals=0
        ),
    )(order, factor, *choices, *after)


def stage_end(arrays):
    hbm = pl.BlockSpec(memory_space=pl.ANY)
    names = sorted(arrays)
    results = pl.pallas_call(
        lambda *refs: None,
        out_shape=[jax.ShapeDtypeStruct(arrays[n].shape, arrays[n].dtype) for n in names],
        in_specs=[hbm] * len(names),
        out_specs=[hbm] * len(names),
        input_output_aliases={i: i for i in range(len(names))},
    )(*[arrays[n] for n in names])
    return dict(zip(names, results))


def along_row(block, moves, ncol):
    return lax.ppermute(block, BOTH, [(a * ncol + c, b * ncol + c) for c in range(ncol) for a, b in moves[c % 2]])


def tree_step(step, block, buffers, row, odd, nrow, ncol):
    line = nrow // 2
    new = {}
    if step == 0:
        new["first"] = along_row(block, ([], [(0, 1)]), ncol)
    elif step == 1:
        held = jnp.where(odd == 1, buffers["first"], block)
        new["half"] = along_row(held, both_lines([(0, line // 2)]), ncol)
    elif step == 2:
        held, reach = buffers["half"], line // 4
        while reach:
            ahead = [(p, p + reach) for p in range(2 * reach, line, 2 * reach)]
            new["on%d" % reach] = along_row(held, both_lines(ahead), ncol)
            new["back%d" % reach] = along_row(held, both_lines([(2 * reach, reach)]), ncol)
            if reach > 1:
                place = row // 2
                held = jnp.where(place % (2 * reach) == reach, new["on%d" % reach], held)
                held = jnp.where(place == reach, new["back%d" % reach], held)
            reach //= 2
    else:
        held, place = block, row // 2
        for name in sorted(buffers):
            for p in arrivals(name, line):
                held = jnp.where((row == 1) if name == "first" else (place == p), buffers[name], held)
        buffers.clear()
        new["line"] = held
        even = [(2 * p, 2 * p + 1) for p in range(line)]
        odds = [(2 * p + 1, 2 * p) for p in range(1, line)]
        new["across"] = along_row(held, (even, odds), ncol)
    return new


def both_lines(moves):
    return [(2 * a, 2 * b) for a, b in moves], [(2 * a + 1, 2 * b + 1) for a, b in moves]


def arrivals(name, line):
    if name == "first":
        return [0]
    if name == "half":
        return [line // 2]
    reach = int(name.strip("onback"))
    if name.startswith("on"):
        return [p + reach for p in range(2 * reach, line, 2 * reach)]
    return [reach]


def along_col(block, bit, nrow, ncol):
    return lax.ppermute(block, BOTH, [(r * ncol + c, r * ncol + (c ^ bit)) for r in range(nrow) for c in range(ncol)])


def core_halves(block):
    half = block.shape[0] // 2
    low = lax.axis_index("col") % 2
    mine = lax.dynamic_slice_in_dim(block, low * half, half, 0)
    other = lax.dynamic_slice_in_dim(block, (1 - low) * half, half, 0)
    return mine, other


def sum_between_chips(mine, nrow, ncol):
    bit = 2
    while bit < ncol:
        mine = mine + along_col(mine, bit, nrow, ncol)
        bit *= 2
    return mine


def scatter_between_chips(keep, nrow, ncol):
    bit = ncol // 2
    while bit > 1:
        half = keep.shape[0] // 2
        keep = keep[:half] + along_col(keep[half:], bit, nrow, ncol)
        bit //= 2
    return keep


def to_rows(mine, step, holders, ncol):
    moves = [(r, r + step) for r in holders]
    return along_row(mine, (moves, moves), ncol)


def received(mine, got, step, holders, row):
    hit = jnp.zeros_like(row == 0)
    for r in holders:
        hit = hit | (row == r + step)
    return jnp.where(hit, got, mine)


def rounds(steps):
    holders, result = [0], []
    for step in steps:
        result.append((step, list(holders)))
        holders += [r + step for r in holders]
    return result


def join(mine, bits, nrow, ncol):
    share, wide = mine.shape[-2:]
    mine = mine.reshape(-1, share, wide)
    for bit in bits:
        other = along_col(mine, bit, nrow, ncol)
        low = (lax.axis_index("col") & bit) == 0
        pair = [jnp.where(low, mine, other), jnp.where(low, other, mine)]
        mine = jnp.stack(pair, 1).reshape(-1, share, wide)
    return mine


def own_part(panels, at, end, first, last):
    own = panels.shape[0]
    col = lax.axis_index("col")
    blocks = []
    for c in range(at // own, -(-end // own)):
        low, high = max(at, c * own), min(end, (c + 1) * own)
        blocks.append(jnp.where(col == c, panels[low - c * own : high - c * own, first:last], 0.0))
    return jnp.concatenate(blocks, 0)


def on_device(nrow, ncol, factor, panels):
    own, width = panels.shape
    row, col = lax.axis_index("row"), lax.axis_index("col")
    odd = col % 2
    share = width // PARTS
    place = jnp.stack([row, col]).astype(jnp.int32)
    halves = [nrow >> k for k in range(1, nrow.bit_length())]
    tree_a, tree_b = rounds([1] + halves[:-1]), rounds(halves)
    live = {"own%d" % i: factor[i * share : (i + 1) * share] for i in range(PARTS)}
    pivots = [{} for _ in range(PARTS)]
    fresh = [[] for _ in range(PARTS)]

    def hops(number):
        for i in range(PARTS):
            if 0 <= number - i <= 3:
                new = tree_step(number - i, live["own%d" % i], pivots[i], row, odd, nrow, ncol)
                pivots[i].update(new)
                fresh[i] = [name for name in new if name != "line"]
            else:
                fresh[i] = []

    def update(i, after):
        across = (row > 0) & (row % 2 != odd)
        choices = [pivots[i]["line"], pivots[i]["across"]]
        return update_product(factor, choices, across, col, ncol, after)

    def own_rest(i, keep):
        return panels[:, i * share : (i + 1) * share] - scatter_between_chips(keep, nrow, ncol)

    def top(at, end_row, first):
        block = factor[at:end_row], factor[first : first + share]
        return own_part(panels, at, end_row, first, first + share) - nt_dot(*block)

    chip_bits = [ncol >> (k + 1) for k in range(len(bin(ncol)) - 4)]

    def end(extra, number):
        named = dict(extra)
        for i in range(PARTS):
            if i == number + 1:
                named["own%d" % i] = live["own%d" % i]
            for n in fresh[i]:
                named["%s of %d" % (n, i)] = pivots[i][n]
        named = stage_end(named)
        for i in range(PARTS):
            if i == number + 1:
                live["own%d" % i] = named["own%d" % i]
            for n in fresh[i]:
                pivots[i][n] = named["%s of %d" % (n, i)]
        return {n: named[n] for n in extra}

    hops(0)
    mine, other = core_halves(top(0, share, 0))
    sum_a = sum_between_chips(mine + along_col(other, 1, nrow, ncol), nrow, ncol)
    mine, other = core_halves(top(0, width, share))
    got_b = along_col(other, 1, nrow, ncol)
    kept = end({"a": sum_a, "mine": mine, "got": got_b}, 0)
    hops(1)
    sum_a, sum_b = kept["a"], sum_between_chips(kept["mine"] + kept["got"], nrow, ncol)
    pack_a, share_a = panel_factor(place, ncol, share, sum_a, along_col(sum_a, 1, nrow, ncol))
    kept = end({"b": sum_b, "share": share_a}, 1)
    hops(2)
    mine, other = kept["b"], along_col(kept["b"], 1, nrow, ncol)
    upper = jnp.dot(pack_a, jnp.where(odd == 0, mine, other), precision=HIGH)
    block = jnp.where(odd == 0, other, mine) - lax.dot_general(upper, upper, (((0,), (0,)), ((), ())), precision=HIGH)
    quarter = share // ncol
    share_a = jnp.concatenate([kept["share"], lax.dynamic_slice_in_dim(upper, col * quarter, quarter, 0)], 1)
    got_a = to_rows(share_a, *tree_a[0], ncol)
    share_b = panel_factor(place, ncol, share, block)[1]
    kept = end({"a": got_a, "b": share_b}, 2)
    hops(3)
    share_a, share_b = received(share_a, kept["a"], *tree_a[0], row), kept["b"]
    got_b, got_a = to_rows(share_b, *tree_b[0], ncol), to_rows(share_a, *tree_a[1], ncol)
    kept = end({"a": got_a, "b": got_b}, 3)
    hops(4)
    share_a, share_b = received(share_a, kept["a"], *tree_a[1], row), received(share_b, kept["b"], *tree_b[0], row)
    for turn in tree_a[2:-1]:
        share_a = received(share_a, to_rows(share_a, *turn, ncol), *turn, row)
    for turn in tree_b[1:-2]:
        share_b = received(share_b, to_rows(share_b, *turn, ncol), *turn, row)
    got_a = to_rows(share_a, *tree_a[-1], ncol)
    share_b = received(share_b, to_rows(share_b, *tree_b[-2], ncol), *tree_b[-2], row)
    got_b = to_rows(share_b, *tree_b[-1], ncol)
    keep, send = update(0, [pivots[1]["line"]])
    keep = keep + along_col(send, 1, nrow, ncol)
    share_a = join(received(share_a, got_a, *tree_a[-1], row), chip_bits, nrow, ncol)
    kept = end({"a": share_a, "b": got_b, "keep": keep}, 4)
    share_a, rest_a = kept["a"], own_rest(0, kept["keep"])
    share_b = join(received(share_b, kept["b"], *tree_b[-1], row), chip_bits, nrow, ncol)
    keep, send = update(1, [])
    kept = end({"b": share_b, "keep": keep, "got": along_col(send, 1, nrow, ncol)}, 5)
    rest_b = own_rest(1, kept["keep"] + kept["got"])
    pack_a = join(share_a, [1], nrow, ncol).reshape(share, 2 * share)
    pack_b = join(kept["b"], [1], nrow, ncol).reshape(share, share)
    out_a = nt_dot(rest_a, pack_a[:, :share], HIGH)
    rest_b = rest_b - jnp.dot(out_a, pack_a[:, share:], precision=HIGH)
    out = [out_a, nt_dot(rest_b, pack_b, HIGH)]
    out = jnp.concatenate(out, 1)
    at_row = lax.broadcasted_iota(jnp.int32, out.shape, 0) + (row * ncol + col) * own
    at_col = lax.broadcasted_iota(jnp.int32, out.shape, 1)
    return jnp.where(at_col <= at_row, out, 0.0)


def solution(mesh):
    return jax.shard_map(
        functools.partial(on_device, mesh.shape["row"], mesh.shape["col"]),
        mesh=mesh,
        in_specs=(P("row", "col"), P(BOTH, None)),
        out_specs=P(BOTH, None),
        check_vma=False,
    )
```
